32 devices in a mesh: dp: 8 (over z, y), ep: 4 (over x, core).
Axes of the slice: x: 2, y: 2, z: 4, core: 2. Of those that a mesh axis runs over, the one named last changes fastest.
Arguments:
- hidden_in: bfloat16 [4096, 2048], P(('dp', 'ep')), may hold values from -6 to 6
- segment_ids: int32 [4096], P(('dp', 'ep')), may hold values from 0 to 15, as said below
- expert_ids: int32 [4096, 4], P('dp'), may hold values from 0 to 7, all different within a row
- priority: int32 [8, 2048], P('dp'), may hold values from 0 to 2047, each once within a row
- capacity: int32 [8], replicated, may hold values from 256 to 320, as said below
- norm_attn: bfloat16 [2048], P(('dp', 'ep')), may hold values from 0.5 to 1.5
- w_query: bfloat16 [2048, 2048], P(('dp', 'ep')), may hold values from -0.125 to 0.125
- w_key: bfloat16 [2048, 2048], P(('dp', 'ep')), may hold values from -0.125 to 0.125
- w_value: bfloat16 [2048, 2048], P(('dp', 'ep')), may hold values from -0.125 to 0.125
- bias_query: bfloat16 [2048], P(('dp', 'ep')), may hold values from -1.5 to 1.5
- bias_key: bfloat16 [2048], P(('dp', 'ep')), may hold values from -1.5 to 1.5
- bias_value: bfloat16 [2048], P(('dp', 'ep')), may hold values from -1.5 to 1.5
- w_out: bfloat16 [2048, 2048], P(('dp', 'ep')), may hold values from -1 to 1
- norm_ffn: bfloat16 [2048], P(('dp', 'ep')), may hold values from 0.5 to 1.5
- w_router: bfloat16 [2048, 8], P(('dp', 'ep')), may hold values from -0.0625 to 0.0625
- w_shared_gate: bfloat16 [2048], P(('dp', 'ep')), may hold values from -0.125 to 0.125
- shared_gate_proj: bfloat16 [2048, 5632], P('dp', 'ep'), may hold values from -0.125 to 0.125
- shared_up_proj: bfloat16 [2048, 5632], P('dp', 'ep'), may hold values from -0.125 to 0.125
- shared_down_proj: bfloat16 [2048, 5632], P('dp', 'ep'), may hold values from -0.21875 to 0.21875
- expert_gate_proj: bfloat16 [2048, 8, 1408], P('dp', 'ep'), may hold values from -0.125 to 0.125
- expert_up_proj: bfloat16 [2048, 8, 1408], P('dp', 'ep'), may hold values from -0.125 to 0.125
- expert_down_proj: bfloat16 [2048, 8, 1408], P('dp', 'ep'), may hold values from -0.875 to 0.875
- out_grad: bfloat16 [4096, 2048], P(('dp', 'ep')), may hold values from -6 to 6
Outputs:
- output: bfloat16 [4096, 2048], P(('dp', 'ep'))
- input_grad: float32 [4096, 2048], P(('dp', 'ep'))
- grad_norm_attn: float32 [2048], P(('dp', 'ep'))
- grad_w_query: float32 [2048, 2048], P(('dp', 'ep'))
- grad_w_key: float32 [2048, 2048], P(('dp', 'ep'))
- grad_w_value: float32 [2048, 2048], P(('dp', 'ep'))
- grad_bias_query: float32 [2048], P(('dp', 'ep'))
- grad_bias_key: float32 [2048], P(('dp', 'ep'))
- grad_bias_value: float32 [2048], P(('dp', 'ep'))
- grad_w_out: float32 [2048, 2048], P(('dp', 'ep'))
- grad_norm_ffn: float32 [2048], P(('dp', 'ep'))
- grad_w_router: float32 [2048, 8], P(('dp', 'ep'))
- grad_w_shared_gate: float32 [2048], P(('dp', 'ep'))
- grad_shared_gate_proj: float32 [2048, 5632], P('dp', 'ep')
- grad_shared_up_proj: float32 [2048, 5632], P('dp', 'ep')
- grad_shared_down_proj: float32 [2048, 5632], P('dp', 'ep')
- grad_expert_gate_proj: float32 [2048, 8, 1408], P('dp', 'ep')
- grad_expert_up_proj: float32 [2048, 8, 1408], P('dp', 'ep')
- grad_expert_down_proj: float32 [2048, 8, 1408], P('dp', 'ep')
The draws below stay inside these ranges and needn't reach their ends.
Inputs may be any that keep to these rules, and one draw needn't show every extreme that they name: `segment_ids`: sequence numbers never fall; each block of 512 tokens begins a new sequence of more than 128 tokens, and its remaining tokens, if any, form one more sequence; some block is one sequence of exactly 512 tokens. `expert_ids`: each token names 4 different experts. `priority`: each group's row is a permutation over its pairs. `capacity`: some expert has exactly 320 slots in every draw.
All inputs are finite; a program needn't handle non-finite values.
Results may differ from the reference program's by a relative error of at most 0.024.
Values may be sent and summed in bfloat16 or wider, within the bound.
No kernel may reach another device: no remote copies, remote signals or barrier semaphores. Data moves between devices by JAX's collectives and lax.ppermute only.
A program may use at most 512 MiB of HBM per device.

```python
import jax
import jax.numpy as jnp
from jax import lax

D = 2048
HEADS = 16
HD = 128
FE = 1408
FS = 5632
TOPK = 4
TOK_DEV = 128
EXPERTS = 8
TOKENS = 4096
GROUPS = 8
GROUP_ROWS = 512
MAXLEN = 512
PAIRS = 2048
EXP_MEAN = 256
CAPMAX = 320


def draw_capacity(key, part):
    key = jax.random.fold_in(key, 7)
    first_key, second_key = jax.random.split(key)
    values = jax.random.randint(first_key, (EXPERTS,), EXP_MEAN, CAPMAX + 1, dtype=jnp.int32)
    chosen = jax.random.randint(second_key, (), 0, EXPERTS, dtype=jnp.int32)
    return values.at[chosen].set(CAPMAX)


def draw_segment_ids(key, part):
    key = jax.random.fold_in(key, 11)
    first_key, second_key, third_key = jax.random.split(key, 3)
    shard_count = GROUP_ROWS // TOK_DEV
    offset = jax.random.randint(third_key, (), 0, shard_count - 1, dtype=jnp.int32)
    group_index = jnp.arange(GROUPS, dtype=jnp.int32)
    boundary_shard = 1 + (group_index + offset) % (shard_count - 1)
    extra = jax.random.randint(first_key, (GROUPS,), 1, TOK_DEV + 1, dtype=jnp.int32)
    firsts = jnp.minimum(boundary_shard * TOK_DEV + extra, GROUP_ROWS)
    whole_group = jax.random.randint(second_key, (), 0, GROUPS - 1, dtype=jnp.int32)
    firsts = firsts.at[whole_group].set(GROUP_ROWS)
    rows = jnp.arange(GROUP_ROWS, dtype=jnp.int32)
    later = (rows[None, :] >= firsts[:, None]).astype(jnp.int32)
    numbers = 2 * group_index[:, None] + later
    return numbers.reshape(-1)


def levels(key, extent, cuts, smallest, largest):
    level, own = 1.0, jax.random.fold_in(key, 6)
    for dim, parts in cuts:
        draws = jnp.exp(jax.random.uniform(jax.random.fold_in(own, dim), (parts,), jnp.float32, smallest / len(cuts), largest / len(cuts)))
        level = level * jnp.repeat(draws, extent[dim] // parts).reshape([-1 if axis == dim else 1 for axis in range(len(extent))])
    return level


def different_ones(rng, rows, count, top, lift):
    sequence = jax.random.permutation(jax.random.fold_in(rng, 1), count)
    boost = sequence
    for power in range(3):
        boost = boost * boost // count
    boost = boost * lift // count
    chance = jax.random.randint(jax.random.fold_in(rng, 2), (rows, count), 0, 4096) + boost
    holders = jax.random.permutation(jax.random.fold_in(rng, 3), rows)[jnp.arange(count) % rows]
    chance = jnp.where(jnp.arange(rows)[:, None] == holders[None, :], 1 << 14, chance)
    score = chance * count + jnp.arange(count)
    return lax.top_k(score.astype(jnp.int32), top)[1].astype(jnp.int32)


def centred(key, dims, deviation, bound, cuts=(), held_as=jnp.bfloat16):
    values = jax.random.normal(key, dims, jnp.float32) * deviation
    if len(cuts) > 0:
        values = levels(key, dims, cuts, -0.22, 0.18) * values
    return jnp.clip(values, min=-bound, max=bound).astype(held_as)


def setup_inputs(seed: int = 0) -> dict:
    key_of = jax.random.split(jax.random.key(seed), 24)
    return {
        "hidden_in": centred(key_of[0], (TOKENS, D), 1.0, 6.0, ((0, 32),)),
        "segment_ids": draw_segment_ids(jax.random.fold_in(key_of[23], 71), 0),
        "expert_ids": different_ones(key_of[2], TOKENS, EXPERTS, TOPK, 4096),
        "priority": jax.vmap(lambda own: jax.random.permutation(own, PAIRS))(jax.random.split(key_of[3], GROUPS)).reshape((GROUPS, PAIRS)).astype(jnp.int32),
        "capacity": draw_capacity(jax.random.fold_in(key_of[23], 71), 0),
        "norm_attn": jnp.clip(1.0 + 0.1 * jax.random.normal(key_of[5], (D,), jnp.float32), 0.5, 1.5).astype(jnp.bfloat16),
        "w_query": centred(key_of[6], (D, D), D ** -0.5, 0.125, ((0, 32),)),
        "w_key": centred(key_of[7], (D, D), D ** -0.5, 0.125, ((0, 32),)),
        "w_value": centred(key_of[8], (D, D), D ** -0.5, 0.125, ((0, 32),)),
        "bias_query": centred(key_of[9], (D,), 0.3, 1.5, ((0, 32),)),
        "bias_key": centred(key_of[10], (D,), 0.3, 1.5, ((0, 32),)),
        "bias_value": centred(key_of[11], (D,), 0.3, 1.5, ((0, 32),)),
        "w_out": centred(key_of[12], (D, D), (D // 64) ** -0.5, 1.0, ((0, 32),)),
        "norm_ffn": jnp.clip(1.0 + 0.1 * jax.random.normal(key_of[13], (D,), jnp.float32), 0.5, 1.5).astype(jnp.bfloat16),
        "w_router": centred(key_of[14], (D, EXPERTS), (4 * D) ** -0.5, 0.0625, ((0, 32),)),
        "w_shared_gate": centred(key_of[15], (D,), D ** -0.5, 0.125, ((0, 32),)),
        "shared_gate_proj": centred(key_of[16], (D, FS), D ** -0.5, 0.125, ((0, 8), (1, 4))),
        "shared_up_proj": centred(key_of[17], (D, FS), D ** -0.5, 0.125, ((0, 8), (1, 4))),
        "shared_down_proj": centred(key_of[18], (D, FS), (FS // 8) ** -0.5, 0.21875, ((0, 8), (1, 4))),
        "expert_gate_proj": centred(key_of[19], (D, EXPERTS, FE), D ** -0.5, 0.125, ((0, 8), (1, 4))),
        "expert_up_proj": centred(key_of[20], (D, EXPERTS, FE), D ** -0.5, 0.125, ((0, 8), (1, 4))),
        "expert_down_proj": centred(key_of[21], (D, EXPERTS, FE), (FE // 32) ** -0.5, 0.875, ((0, 8), (1, 4))),
        "out_grad": centred(key_of[22], (TOKENS, D), 1.0, 6.0, ((0, 32),)),
    }


epsilon = 1e-06
rotary_base = 1000000.0
masked_score = -1e+30
highest_precision = lax.Precision.HIGHEST

@jax.custom_vjp
def low(v):
    return lax.optimization_barrier(v.astype(jnp.bfloat16)).astype(jnp.float32)

@jax.custom_vjp
def low_back(v):
    return v

def low_keep(v):
    return (low(v), None)

def low_pass(kept, grad):
    return (grad,)

def back_keep(v):
    return (v, None)

def back_low(kept, grad):
    return (low(grad),)
low.defvjp(low_keep, low_pass)
low_back.defvjp(back_keep, back_low)

def matmul(left_side, right_side):
    return jnp.dot(left_side, right_side, precision=highest_precision)

def rms_norm(values, gain_vector):
    return values * lax.rsqrt(lax.optimization_barrier(jnp.mean(values * values, -1, keepdims=True)) + epsilon) * gain_vector

def rotate(values, positions):
    row_count = values.shape[0]
    split_heads = values.reshape(row_count, -1, HD)
    half_size = HD // 2
    inverse = 1.0 / rotary_base ** (jnp.arange(0, HD, 2, dtype=jnp.float32) / HD)
    angles = positions.astype(jnp.float32)[:, None] * inverse[None, :]
    cosine = jnp.cos(angles)[:, None, :]
    sine = jnp.sin(angles)[:, None, :]
    first_half = split_heads[..., :half_size]
    second_half = split_heads[..., half_size:]
    turned = jnp.concatenate([first_half * cosine - second_half * sine, second_half * cosine + first_half * sine], -1)
    return turned.reshape(row_count, -1)

def slot_table(pair_experts, pair_order, capacity, experts):
    pair_count = pair_experts.shape[0]
    pair_index = jnp.arange(pair_count, dtype=jnp.int32)
    by_priority = jnp.zeros((pair_count,), jnp.int32).at[pair_order].set(pair_index)
    labels = jnp.arange(experts, dtype=jnp.int32)[None, :]
    sorted_hits = (pair_experts[by_priority][:, None] == labels).astype(jnp.int32)
    earlier = jnp.cumsum(sorted_hits, 0) - sorted_hits
    sorted_slots = lax.optimization_barrier(jnp.sum(earlier * sorted_hits, 1))
    slot_of_pair = jnp.zeros((pair_count,), jnp.int32).at[by_priority].set(sorted_slots)
    hits = (pair_experts[:, None] == labels).astype(jnp.int32)
    pair_limit = lax.optimization_barrier(jnp.sum(hits * capacity[None, :], 1))
    target = jnp.where(slot_of_pair < pair_limit, pair_experts * CAPMAX + slot_of_pair, experts * CAPMAX)
    empty_row = jnp.full((experts * CAPMAX,), pair_count // TOPK, jnp.int32)
    return empty_row.at[target].set(pair_index // TOPK, mode='drop')

def reference(hidden_in, segment_ids, expert_ids, priority, capacity, norm_attn, w_query, w_key, w_value, bias_query, bias_key, bias_value, w_out, norm_ffn, w_router, w_shared_gate, shared_gate_proj, shared_up_proj, shared_down_proj, expert_gate_proj, expert_up_proj, expert_down_proj, out_grad):
    index_all = jnp.arange(TOKENS, dtype=jnp.int32)
    starts = jnp.concatenate([jnp.ones((1,), dtype=bool), segment_ids[1:] != segment_ids[:-1]])
    positions = index_all - lax.cummax(jnp.where(starts, index_all, 0))
    slot_tokens = jax.vmap(lambda group_ids, group_order: slot_table(group_ids, group_order, capacity, EXPERTS))(expert_ids.reshape(GROUPS, PAIRS), priority)
    slot_expert = jnp.arange(EXPERTS * CAPMAX, dtype=jnp.int32) // CAPMAX
    block_rows = min(512, TOKENS)
    block_count = TOKENS // block_rows
    head_scale = HD ** (-0.5)

    def forward_pass(input_arrays, attention_gain, query_weight, key_weight, value_weight, query_bias, key_bias, value_bias, output_weight, feedforward_gain, router_weight, shared_gate_vector, shared_gate_weight, shared_up_weight, shared_down_weight, expert_gate_weight, expert_up_weight, expert_down_weight):
        attn_in = low(rms_norm(input_arrays, attention_gain))
        query_pre = low_back(matmul(attn_in, query_weight) + query_bias)
        key_pre = low_back(matmul(attn_in, key_weight) + key_bias)
        value_pre = low_back(matmul(attn_in, value_weight) + value_bias)
        query_rot = low(rotate(query_pre, positions))
        key_rot = low(rotate(key_pre, positions))
        value_low = low(value_pre)
        key_pad = jnp.concatenate([jnp.zeros((MAXLEN, D), jnp.float32), key_rot])
        value_pad = jnp.concatenate([jnp.zeros((MAXLEN, D), jnp.float32), value_low])

        def attend(block):
            start = (block * block_rows).astype(jnp.int32)
            query_block = lax.dynamic_slice_in_dim(query_rot, start, block_rows, 0).reshape(block_rows, HEADS, HD)
            key_block = lax.dynamic_slice_in_dim(key_pad, start, block_rows + MAXLEN, 0).reshape(-1, HEADS, HD)
            value_block = lax.dynamic_slice_in_dim(value_pad, start, block_rows + MAXLEN, 0).reshape(-1, HEADS, HD)
            place_block = lax.dynamic_slice_in_dim(positions, start, block_rows, 0)
            scores = jnp.einsum('qhd,khd->hqk', query_block, key_block, precision=highest_precision) * head_scale
            scores = low_back(scores)
            spread = MAXLEN + jnp.arange(block_rows, dtype=jnp.int32)[:, None] - jnp.arange(block_rows + MAXLEN, dtype=jnp.int32)[None, :]
            valid = (spread >= 0) & (spread <= place_block[:, None])
            scores = jnp.where(valid[None], scores, masked_score)
            weights = low(jax.nn.softmax(scores, -1))
            mixed = jnp.einsum('hqk,khd->qhd', weights, value_block, precision=highest_precision)
            return mixed.reshape(block_rows, D)
        attn = lax.map(jax.checkpoint(attend), jnp.arange(block_count, dtype=jnp.int32)).reshape(TOKENS, D)
        attn_low = low(low_back(attn))
        mid = input_arrays + low_back(matmul(attn_low, output_weight))
        ffn_in = low(rms_norm(mid, feedforward_gain))

        def expert_block(pieces):
            group_in, slot_token = pieces
            router = jax.nn.softmax(matmul(group_in, router_weight), -1)
            share = jax.nn.sigmoid(matmul(group_in, shared_gate_vector))
            shared_gate = low_back(matmul(group_in, shared_gate_weight))
            shared_up = low_back(matmul(group_in, shared_up_weight))
            shared_hidden = low(jax.nn.silu(shared_gate) * shared_up)
            shared_out = low_back(matmul(shared_hidden, shared_down_weight.T))
            padded_in = jnp.concatenate([group_in, jnp.zeros((1, D), jnp.float32)])
            slot_input = padded_in[slot_token].reshape(EXPERTS, CAPMAX, D)
            expert_gate = low_back(jnp.einsum('prt,tpo->pro', slot_input, expert_gate_weight, precision=highest_precision))
            expert_up_matrix = low_back(jnp.einsum('prt,tpo->pro', slot_input, expert_up_weight, precision=highest_precision))
            expert_hidden = low(jax.nn.silu(expert_gate) * expert_up_matrix)
            expert_out = low_back(jnp.einsum('rmz,prz->rmp', expert_hidden, expert_down_weight, precision=highest_precision))
            padded_router = jnp.concatenate([router, jnp.zeros((1, EXPERTS), jnp.float32)])
            slot_gate = padded_router[slot_token, slot_expert]
            combined = jnp.concatenate([share[:, None] * shared_out, jnp.zeros((1, D), jnp.float32)])
            combined = combined.at[slot_token].add(slot_gate[:, None] * expert_out.reshape(-1, D))
            return combined[:GROUP_ROWS]
        ffn_out = lax.map(jax.checkpoint(expert_block), (ffn_in.reshape(GROUPS, GROUP_ROWS, D), slot_tokens)).reshape(TOKENS, D)
        return mid + ffn_out
    result, pullback = jax.vjp(forward_pass, hidden_in.astype(jnp.float32), norm_attn.astype(jnp.float32), w_query.astype(jnp.float32), w_key.astype(jnp.float32), w_value.astype(jnp.float32), bias_query.astype(jnp.float32), bias_key.astype(jnp.float32), bias_value.astype(jnp.float32), w_out.astype(jnp.float32), norm_ffn.astype(jnp.float32), w_router.astype(jnp.float32), w_shared_gate.astype(jnp.float32), shared_gate_proj.astype(jnp.float32), shared_up_proj.astype(jnp.float32), shared_down_proj.astype(jnp.float32), expert_gate_proj.astype(jnp.float32), expert_up_proj.astype(jnp.float32), expert_down_proj.astype(jnp.float32))
    grads = pullback(out_grad.astype(jnp.float32))
    return (result.astype(jnp.bfloat16), grads[0], grads[1], grads[2], grads[3], grads[4], grads[5], grads[6], grads[7], grads[8], grads[9], grads[10], grads[11], grads[12], grads[13], grads[14], grads[15], grads[16], grads[17])
```

```python
import jax
import jax.numpy as jnp
from jax import lax
from jax.sharding import PartitionSpec as P

HD = 128
TOPK = 4
EXP_DEV = 2
RING_SIZE = 8
CORNER_ROWS = 48
AXES = ("dp", "ep")

RING = (0, 2, 4, 6, 7, 5, 3, 1)
PLACE = tuple(RING.index(j) for j in range(RING_SIZE))

epsilon = 1e-06
rotary_base = 1000000.0
masked_score = -1e30
contract_rows = (((0,), (0,)), ((), ()))
contract_cols = (((1,), (1,)), ((), ()))
single_float = jnp.float32
bf16 = jnp.bfloat16


def dot(left, right, dims=(((1,), (0,)), ((), ()))):
    return lax.dot_general(left, right, dims, preferred_element_type=single_float)


def move(block, where):
    sets = lax.axis_size("dp") // RING_SIZE
    ranks = lax.axis_size("ep")
    pairs = []
    for j in range(RING_SIZE):
        for e in range(ranks):
            to = where(j, e)
            if to is None:
                continue
            for s in range(sets):
                pairs.append(((j * sets + s) * ranks + e, (to[0] * sets + s) * ranks + to[1]))
    return lax.ppermute(block, AXES, pairs)


def around(j, hops):
    return RING[(PLACE[j] + hops) % RING_SIZE]


def to_core(block):
    return move(block, lambda j, e: (j, e ^ 1))


def to_side(block):
    return move(block, lambda j, e: (j, e ^ 2))


def out_hop(block, only_one=False):
    return move(
        block,
        lambda j, e: None if only_one and e % 2 == 0 else (around(j, 1 if e % 2 else -1), e),
    )


def back_hop(block, only_one=False):
    return move(
        block,
        lambda j, e: None if only_one and e % 2 == 0 else (around(j, -1 if e % 2 else 1), e),
    )


def ring_up(block):
    return move(block, lambda j, e: (around(j, 1), e))


def ring_down(block):
    return move(block, lambda j, e: (around(j, -1), e))


def in_set(sets):
    return [[j * sets + s for s in range(sets)] for j in range(RING_SIZE)]


def set_gather(block, axis):
    sets = lax.axis_size("dp") // RING_SIZE
    if sets == 1:
        return block
    return lax.all_gather(block, "dp", axis_index_groups=in_set(sets), axis=axis, tiled=True)


def set_scatter(block, axis):
    sets = lax.axis_size("dp") // RING_SIZE
    if sets == 1:
        return block
    return lax.psum_scatter(
        block, "dp", scatter_dimension=axis, axis_index_groups=in_set(sets), tiled=True
    )


def group_gather(block, ep_index):
    near = to_core(block)
    far = to_side(block)
    parts = [block, near, far, to_core(far)]
    whole = jnp.zeros((4,) + block.shape, block.dtype)
    for m, part in enumerate(parts):
        whole = lax.dynamic_update_index_in_dim(whole, part, ep_index ^ m, 0)
    return whole


def group_scatter(parts, ep_index):
    part = [lax.dynamic_index_in_dim(parts, ep_index ^ m, 0, False) for m in range(4)]
    got = to_core(jnp.stack([part[1], part[3]]).astype(bf16)).astype(single_float)
    near = part[0].astype(single_float) + got[0]
    far = part[2].astype(single_float) + got[1]
    return near + to_side(far.astype(bf16)).astype(single_float)


def ring_gather(block, place):
    position = jnp.asarray(PLACE)[place]
    order = jnp.asarray(RING)
    half = block.shape[0] // 2
    up, down = [block], [block]
    for _ in range(3):
        up.append(ring_up(up[-1]))
        down.append(ring_down(down[-1]))
    last = jnp.concatenate([ring_up(up[3][:half]), ring_down(down[3][half:])])
    whole = jnp.zeros((RING_SIZE,) + block.shape, block.dtype)
    whole = lax.dynamic_update_index_in_dim(whole, block, place, 0)
    for k in range(1, 4):
        whole = lax.dynamic_update_index_in_dim(
            whole, up[k], order[(position - k) % RING_SIZE], 0
        )
        whole = lax.dynamic_update_index_in_dim(
            whole, down[k], order[(position + k) % RING_SIZE], 0
        )
    return lax.dynamic_update_index_in_dim(whole, last, order[(position + 4) % RING_SIZE], 0)


def ring_scatter(parts, place):
    position = jnp.asarray(PLACE)[place]
    order = jnp.asarray(RING)
    half = parts.shape[1] // 2

    def part(hops):
        return lax.dynamic_index_in_dim(
            parts, order[(position + hops) % RING_SIZE], 0, False
        ).astype(single_float)

    opposite = part(4).astype(bf16)
    up = ring_up(opposite[:half]).astype(single_float)
    down = ring_down(opposite[half:]).astype(single_float)
    up = jnp.pad(up, ((0, parts.shape[1] - half), (0, 0)))
    down = jnp.pad(down, ((half, 0), (0, 0)))
    for k in (3, 2, 1):
        up = ring_up((part(k) + up).astype(bf16)).astype(single_float)
        down = ring_down((part(-k) + down).astype(bf16)).astype(single_float)
    return part(0) + up + down


def ring_exchange(blocks, place):
    whole = jnp.zeros_like(blocks)
    own = lax.dynamic_index_in_dim(blocks, place, 0, False)
    whole = lax.dynamic_update_index_in_dim(whole, own, place, 0)
    for k in range(1, RING_SIZE):
        block = lax.dynamic_index_in_dim(blocks, place ^ k, 0, False)
        got = move(block, lambda j, e: (j ^ k, e))
        whole = lax.dynamic_update_index_in_dim(whole, got, place ^ k, 0)
    return whole


def token_gather(block, core):
    head, tail = block[:CORNER_ROWS], block[CORNER_ROWS:]
    tails = [jnp.concatenate([tail, to_core(tail)])]
    far = to_side(head)
    heads = [jnp.concatenate([head, to_core(head), far, to_core(far)])]
    for k in range(4):
        tails.append(out_hop(tails[-1], k == 3))
        heads.append(out_hop(heads[-1], k == 3))
    tails = [jnp.where(core == 0, tails[0], tails[4])] + tails[1:4]
    heads = [jnp.where(core == 0, heads[0], heads[4])] + heads[1:4]
    sides = [to_side(part) for part in tails]
    return jnp.concatenate(heads + tails + sides)


def token_scatter(parts, core):
    rows = parts.shape[0] // 16
    head_rows, tail_rows = 4 * CORNER_ROWS, 2 * (rows - CORNER_ROWS)
    base = 4 * head_rows
    heads = [parts[k * head_rows : (k + 1) * head_rows] for k in range(4)]
    tails = [parts[base + k * tail_rows : base + (k + 1) * tail_rows] for k in range(4)]
    base = base + 4 * tail_rows
    sides = [parts[base + k * tail_rows : base + (k + 1) * tail_rows] for k in range(4)]
    wide = lambda value: value.astype(single_float)
    low = lambda value: value.astype(bf16)
    tails = [wide(tails[k]) + wide(to_side(low(sides[k]))) for k in range(4)]

    def run(pieces):
        total = wide(back_hop(low(pieces[0]), True)) + wide(pieces[3])
        total = wide(back_hop(low(total))) + wide(pieces[2])
        total = wide(back_hop(low(total))) + wide(pieces[1])
        total = wide(back_hop(low(total)))
        return total + jnp.where(core == 0, wide(pieces[0]), 0.0)

    tail = run(tails)
    half = tail_rows // 2
    tail = tail[:half] + wide(to_core(low(tail[half:])))
    head = run(heads).reshape(4, CORNER_ROWS, -1)
    got = wide(to_core(low(head[1::2])))
    near, far = head[0] + got[0], head[2] + got[1]
    head = near + wide(to_side(low(far)))
    return jnp.concatenate([head, tail])


def rms_scale(values):
    return lax.rsqrt(jnp.mean(values * values, -1, keepdims=True) + epsilon)


def rotary_table(positions):
    inverse = 1.0 / rotary_base ** (jnp.arange(0, HD, 2, dtype=single_float) / HD)
    angles = positions.astype(single_float)[:, None] * inverse[None, :]
    cosine, sine = jnp.cos(angles), jnp.sin(angles)
    return (
        jnp.concatenate([cosine, cosine], -1)[:, None, :],
        jnp.concatenate([-sine, sine], -1)[:, None, :],
    )


def rotate(values, table, direction):
    heads = values.reshape(values.shape[0], -1, HD)
    swapped = jnp.concatenate([heads[..., HD // 2 :], heads[..., : HD // 2]], -1)
    return heads * table[0] + swapped * (direction * table[1])


def kept_pairs(expert_ids, priority, capacity, ep_index, tokens):
    experts = capacity.shape[0]
    order = priority.reshape(-1, TOPK)
    own_experts = lax.dynamic_slice_in_dim(expert_ids, ep_index * tokens, tokens, 0)
    own_order = lax.dynamic_slice_in_dim(order, ep_index * tokens, tokens, 0)
    all_experts = expert_ids.reshape(1, -1)
    all_order = priority.reshape(1, -1)
    labels = jnp.arange(experts, dtype=jnp.int32)[None, :]
    kept = jnp.zeros((tokens, experts), bool)
    for k in range(TOPK):
        expert = own_experts[:, k : k + 1]
        ahead = (all_experts == expert) & (all_order < own_order[:, k : k + 1])
        slot = jnp.sum(ahead.astype(jnp.int32), 1, keepdims=True)
        kept = kept | ((labels == expert) & (slot < capacity[None, :]))
    return kept


def own_heads(features, core, side):
    lead = features.shape[:-1]
    split = features.reshape(lead + (2, -1, 2, HD))
    axis = len(lead)
    split = lax.dynamic_index_in_dim(split, core, axis, False)
    split = lax.dynamic_index_in_dim(split, side, axis + 1, False)
    return split.reshape(lead + (-1,))


def heads_to_rows(heads, dp_count, n, core, side, ep_index):
    rows = heads.shape[0]
    if 2 * n == HD:
        low, high = heads[..., :n], heads[..., n:]
        keep = jnp.where(core == 0, low, high).reshape(rows, -1)
        got = to_core(jnp.where(core == 0, high, low).reshape(rows, -1))
        return jnp.where(
            core == 0, jnp.concatenate([keep, got], 1), jnp.concatenate([got, keep], 1)
        )
    every = lax.all_gather(heads, "ep", axis=0)
    every = every.reshape((2, 2) + heads.shape).transpose(2, 1, 3, 0, 4)
    every = every.reshape(rows, dp_count, 4, n)
    return lax.dynamic_index_in_dim(every, ep_index, 2, False).reshape(rows, -1)


def rows_to_heads(features, dp_count, n, core, side, ep_index):
    rows = features.shape[0]
    if 2 * n == HD:
        half = features.shape[1] // 2
        low, high = features[:, :half], features[:, half:]
        keep = jnp.where(core == 0, low, high).reshape(rows, -1, n)
        got = to_core(jnp.where(core == 0, high, low)).reshape(rows, -1, n)
        return jnp.where(
            core == 0, jnp.concatenate([keep, got], -1), jnp.concatenate([got, keep], -1)
        )
    every = lax.all_gather(features, "ep", axis=0).reshape(4, rows, dp_count, n)
    every = every.transpose(1, 2, 0, 3).reshape(rows, -1)
    return own_heads(every, core, side).reshape(rows, -1, HD)


def body(
    hidden_in,
    segment_ids,
    expert_ids,
    priority,
    capacity,
    norm_attn,
    w_query,
    w_key,
    w_value,
    bias_query,
    bias_key,
    bias_value,
    w_out,
    norm_ffn,
    w_router,
    w_shared_gate,
    shared_gate_proj,
    shared_up_proj,
    shared_down_proj,
    expert_gate_proj,
    expert_up_proj,
    expert_down_proj,
    out_grad,
):
    tokens, model_width = hidden_in.shape
    group_rows = 4 * tokens
    head_scale = HD ** (-0.5)
    dp_count = lax.axis_size("dp")
    sets = dp_count // RING_SIZE
    place = lax.axis_index("dp") // sets
    ep_index = lax.axis_index("ep")
    core, side = ep_index % 2, ep_index // 2
    n = norm_attn.shape[0]
    experts = capacity.shape[0]

    small = jnp.concatenate(
        [
            jnp.stack([norm_attn, bias_query, bias_key, bias_value, norm_ffn, w_shared_gate]),
            w_router.T,
            jnp.zeros((2, n), bf16),
        ]
    )
    small = lax.all_gather(small, AXES, axis=0).transpose(1, 0, 2).reshape(16, model_width)
    attention_gain = small[0].astype(single_float)
    feedforward_gain = small[4].astype(single_float)
    gate_rows = small[5:14]
    head_bias = own_heads(small[1:4], core, side).astype(single_float)

    group_x = group_gather(hidden_in, ep_index).reshape(group_rows, model_width)
    segments = group_gather(segment_ids.reshape(1, tokens), ep_index).reshape(group_rows)
    group_index = jnp.arange(group_rows, dtype=jnp.int32)
    first = segments == segments[0]
    first_count = jnp.sum(first.astype(jnp.int32))
    positions = jnp.where(first, group_index, group_index - first_count)
    valid = (segments[:, None] == segments[None, :]) & (
        group_index[None, :] <= group_index[:, None]
    )
    table = rotary_table(positions)

    def head_columns(weight):
        split = weight.reshape(n, 2, -1, 2, HD).transpose(3, 1, 0, 2, 4)
        return split.reshape(4, n, -1)

    qkv = jnp.concatenate([head_columns(w) for w in (w_query, w_key, w_value)], -1)
    head_width = qkv.shape[-1] // 3
    qkv = lax.all_to_all(qkv, "ep", 0, 0).reshape(4 * n, -1)
    qkv_weight = ring_gather(set_gather(qkv, 0), place).reshape(model_width, -1)
    out_weight = ring_gather(set_gather(w_out, 0), place).reshape(-1, model_width)

    def unit_slices(shared, routed):
        every = jnp.concatenate([shared[:, None, :], routed], 1)
        every = every.reshape(every.shape[0], 1 + EXP_DEV, RING_SIZE, -1)
        return every.transpose(2, 1, 3, 0)

    slices = jnp.stack(
        [
            unit_slices(shared_gate_proj, expert_gate_proj),
            unit_slices(shared_up_proj, expert_up_proj),
            unit_slices(shared_down_proj, expert_down_proj),
        ],
        1,
    )
    units = slices.shape[3]
    slices = set_gather(slices, 4)
    row_block = slices.shape[4]
    chip_units = 2 * (1 + EXP_DEV) * units
    slices = ring_exchange(slices, place)
    slices = slices.transpose(1, 2, 3, 0, 4).reshape(3, -1, model_width)
    slices = jnp.concatenate([slices, to_core(slices)], 1)
    gate_weight, up_weight, down_weight = slices[0], slices[1], slices[2]

    kept_own = kept_pairs(expert_ids, priority, capacity, ep_index, tokens)
    kept_own = jnp.pad(kept_own.astype(bf16), ((0, 0), (0, HD - experts)))
    wide_grad = token_gather(jnp.concatenate([out_grad, kept_own], 1), core)
    ring_grad = wide_grad[:, :model_width]
    kept = wide_grad[:, model_width : model_width + experts].astype(single_float)

    x_float = group_x.astype(single_float)
    attn_in = (x_float * rms_scale(x_float) * attention_gain).astype(bf16)
    pre = dot(attn_in, qkv_weight)
    query = rotate(pre[:, :head_width] + head_bias[0], table, 1.0).astype(bf16)
    key = rotate(pre[:, head_width : 2 * head_width] + head_bias[1], table, 1.0).astype(bf16)
    value = (pre[:, 2 * head_width :] + head_bias[2]).astype(bf16).reshape(group_rows, -1, HD)

    def score_table():
        raw = jnp.einsum("thd,khd->htk", query, key, preferred_element_type=single_float)
        return jnp.where(valid[None], raw * head_scale, masked_score)

    scores = score_table()
    top_score = jnp.max(scores, -1, keepdims=True)
    exps = jnp.exp(scores - top_score)
    totals = jnp.sum(exps, -1, keepdims=True)
    log_total = top_score + jnp.log(totals)
    probs_low = (exps / totals).astype(bf16)
    attn = jnp.einsum("htk,khd->thd", probs_low, value, preferred_element_type=single_float)
    attn_rows = heads_to_rows(attn.astype(bf16), dp_count, n, core, side, ep_index)
    mid = hidden_in.astype(single_float) + group_scatter(
        dot(attn_rows, out_weight).reshape(4, tokens, model_width), ep_index
    )
    scale_two = rms_scale(mid)
    normed_two = mid * scale_two
    ffn_in = (normed_two * feedforward_gain).astype(bf16)

    ring_in = token_gather(ffn_in, core)
    logits = dot(ring_in, gate_rows, contract_cols)
    share = jax.nn.sigmoid(logits[:, :1])
    router = jax.nn.softmax(logits[:, 1 : 1 + experts], -1)
    labels = jnp.arange(experts, dtype=jnp.int32)[None, :]
    held = [EXP_DEV * (ep_index ^ flip) + i for flip in (0, 1) for i in range(EXP_DEV)]
    hits = [(labels == expert).astype(single_float) * kept for expert in held]
    routed = [jnp.sum(router * hit, -1, keepdims=True) for hit in hits]
    unit_scale = [share] + routed[:EXP_DEV] + [share] + routed[EXP_DEV:]
    unit_set = (jnp.arange(chip_units, dtype=jnp.int32) // units)[None, :]

    def by_unit(columns):
        spread = jnp.broadcast_to(columns[-1], (columns[-1].shape[0], chip_units))
        for k in range(len(columns) - 2, -1, -1):
            spread = jnp.where(unit_set == k, columns[k], spread)
        return spread

    gate = dot(ring_in, gate_weight, contract_cols)
    up = dot(ring_in, up_weight, contract_cols)
    logistic = jax.nn.sigmoid(gate)
    act = gate * logistic
    slope = logistic * (1.0 + gate * (1.0 - logistic))
    hidden = act * up
    weight_of_unit = by_unit(unit_scale)
    hidden_low = hidden.astype(bf16).astype(single_float)
    scaled_hidden = (weight_of_unit * hidden_low).astype(bf16)
    ffn_out = token_scatter(dot(scaled_hidden, down_weight).astype(bf16), core)
    output = (mid + ffn_out).astype(bf16)

    d_hidden = dot(ring_grad, down_weight, contract_cols)
    product = d_hidden * hidden_low
    d_scale = [
        jnp.sum(jnp.where(unit_set == k, product, 0.0), -1, keepdims=True)
        for k in range(len(unit_scale))
    ]
    d_routed = d_scale[1 : 1 + EXP_DEV] + d_scale[2 + EXP_DEV :]
    d_share_logit = (d_scale[0] + d_scale[1 + EXP_DEV]) * share * (1.0 - share)
    d_router = sum(d * hit for d, hit in zip(d_routed, hits))
    d_logits = router * (d_router - jnp.sum(router * d_router, -1, keepdims=True))
    d_rows = jnp.concatenate([d_share_logit, d_logits], 1)
    d_rows_high = d_rows.astype(bf16)
    d_rows_low = (d_rows - d_rows_high.astype(single_float)).astype(bf16)
    d_rows_both = jnp.concatenate([d_rows_high, d_rows_low], 1)
    d_scaled = d_hidden * weight_of_unit
    d_gate = (d_scaled * up * slope).astype(bf16)
    d_up = (d_scaled * act).astype(bf16)
    d_ring = dot(d_gate, gate_weight) + dot(d_up, up_weight)
    d_ring = d_ring + dot(d_rows_both, jnp.concatenate([gate_rows, gate_rows]))
    d_ffn_in = token_scatter(d_ring.astype(bf16), core)
    grad_rows = dot(d_rows_both, ring_in, contract_rows)
    grad_rows = grad_rows[: 1 + experts] + grad_rows[1 + experts :]

    unit_grads = jnp.stack(
        [
            dot(d_gate, ring_in, contract_rows).astype(bf16),
            dot(d_up, ring_in, contract_rows).astype(bf16),
            dot(scaled_hidden, ring_grad, contract_rows).astype(bf16),
        ]
    )
    half_units = chip_units // 2
    unit_grads = unit_grads[:, :half_units].astype(single_float) + to_core(
        unit_grads[:, half_units:]
    ).astype(single_float)
    unit_grads = unit_grads.astype(bf16).reshape(3, half_units, RING_SIZE, row_block)
    unit_grads = ring_exchange(unit_grads.transpose(2, 0, 1, 3), place)
    unit_grads = set_scatter(unit_grads, 3)
    unit_grads = unit_grads.reshape(RING_SIZE, 3, 1 + EXP_DEV, units, -1)
    unit_grads = unit_grads.transpose(1, 4, 2, 0, 3).astype(single_float)
    unit_grads = unit_grads.reshape(3, unit_grads.shape[1], 1 + EXP_DEV, -1)

    d_normed_two = d_ffn_in * feedforward_gain
    d_mid = out_grad.astype(single_float) + scale_two * (
        d_normed_two - normed_two * jnp.mean(d_normed_two * normed_two, -1, keepdims=True)
    )
    grad_gain_ffn = jnp.sum(d_ffn_in * normed_two, 0)
    d_branch = group_gather(d_mid.astype(bf16), ep_index).reshape(group_rows, model_width)
    d_attn = rows_to_heads(
        dot(d_branch, out_weight, contract_cols).astype(bf16), dp_count, n, core, side, ep_index
    )
    grad_out_rows = dot(attn_rows, d_branch, contract_rows).astype(bf16)
    grad_out_rows = ring_scatter(grad_out_rows.reshape(RING_SIZE, -1, model_width), place)
    grad_out_w = set_scatter(grad_out_rows, 0)
    probs = jnp.exp(score_table() - log_total)
    d_probs = jnp.einsum("thd,khd->htk", d_attn, value, preferred_element_type=single_float)
    d_value = jnp.einsum("htk,thd->khd", probs_low, d_attn, preferred_element_type=single_float)
    d_scores = (probs * (d_probs - jnp.sum(probs * d_probs, -1, keepdims=True))).astype(bf16)
    d_query = head_scale * jnp.einsum(
        "htk,khd->thd", d_scores, key, preferred_element_type=single_float
    )
    d_key = head_scale * jnp.einsum(
        "htk,thd->khd", d_scores, query, preferred_element_type=single_float
    )
    d_pre = [rotate(d_query, table, -1.0), rotate(d_key, table, -1.0), d_value]
    d_pre = jnp.concatenate([d.reshape(group_rows, -1) for d in d_pre], 1).astype(bf16)
    grad_bias = jnp.sum(d_pre.astype(single_float), 0).reshape(3, 1, -1, 1, HD)
    grad_qkv = dot(attn_in, d_pre, contract_rows).astype(bf16)
    grad_qkv = ring_scatter(grad_qkv.reshape(RING_SIZE, -1, 3 * head_width), place)
    grad_qkv = set_scatter(grad_qkv, 0).astype(bf16)
    grad_qkv = lax.all_to_all(grad_qkv.reshape(4, n, 3 * head_width), "ep", 0, 0)
    grad_qkv = grad_qkv.reshape(2, 2, n, 3, -1, HD).transpose(3, 2, 1, 4, 0, 5)
    grad_qkv = grad_qkv.reshape(3, n, model_width).astype(single_float)
    d_attn_in = group_scatter(
        dot(d_pre, qkv_weight, contract_cols).reshape(4, tokens, model_width), ep_index
    )
    own_x = hidden_in.astype(single_float)
    scale_one = rms_scale(own_x)
    normed_one = own_x * scale_one
    grad_gain_attn = jnp.sum(d_attn_in * normed_one, 0)
    d_normed_one = d_attn_in * attention_gain
    input_grad = d_mid + scale_one * (
        d_normed_one - normed_one * jnp.mean(d_normed_one * normed_one, -1, keepdims=True)
    )

    grad_bias_full = jnp.zeros((3, 2, model_width // (4 * HD), 2, HD), single_float)
    grad_bias_full = lax.dynamic_update_slice(grad_bias_full, grad_bias, (0, core, 0, side, 0))
    small_grads = jnp.concatenate(
        [
            grad_gain_attn[None],
            grad_bias_full.reshape(3, model_width),
            grad_gain_ffn[None],
            grad_rows,
            jnp.zeros((2, model_width), single_float),
        ]
    )
    small_grads = small_grads.reshape(16, -1, n).transpose(1, 0, 2)
    small_grads = lax.psum_scatter(small_grads, AXES, scatter_dimension=0)
    return (
        output,
        input_grad,
        small_grads[0],
        grad_qkv[0],
        grad_qkv[1],
        grad_qkv[2],
        small_grads[1],
        small_grads[2],
        small_grads[3],
        grad_out_w,
        small_grads[4],
        small_grads[6:14].T,
        small_grads[5],
        unit_grads[0, :, 0],
        unit_grads[1, :, 0],
        unit_grads[2, :, 0],
        unit_grads[0, :, 1:],
        unit_grads[1, :, 1:],
        unit_grads[2, :, 1:],
    )


def solution(mesh):
    rows, vector, split = P(AXES, None), P(AXES), P("dp", "ep")
    routed = P("dp", "ep", None)
    return jax.shard_map(
        body,
        mesh=mesh,
        in_specs=(
            (rows, vector, P("dp", None), P("dp", None), P(), vector)
            + (rows,) * 3
            + (vector,) * 3
            + (rows, vector, rows, vector)
            + (split,) * 3
            + (routed,) * 3
            + (rows,)
        ),
        out_specs=(
            (rows, rows, vector)
            + (rows,) * 3
            + (vector,) * 3
            + (rows, vector, rows, vector)
            + (split,) * 3
            + (routed,) * 3
        ),
        check_vma=False,
    )
```

```python
import jax
import jax.numpy as jnp
from jax import lax
from jax.experimental import pallas as pl
from jax.experimental.pallas import tpu as pltpu
from jax.sharding import PartitionSpec as P

HD = 128
TOPK = 4
EXP_DEV = 2
RING_SIZE = 8
CORNER_ROWS = 48
ROW_SPLIT = 16
VMEM_BYTES = 60 * 1024 * 1024
AXES = ("dp", "ep")

RING = (0, 2, 4, 6, 7, 5, 3, 1)
PLACE = tuple(RING.index(j) for j in range(RING_SIZE))

epsilon = 1e-06
rotary_base = 1000000.0
masked_score = -1e30
contract_rows = (((0,), (0,)), ((), ()))
contract_cols = (((1,), (1,)), ((), ()))
single_float = jnp.float32
bf16 = jnp.bfloat16


def dot(left, right, dims=(((1,), (0,)), ((), ()))):
    return lax.dot_general(left, right, dims, preferred_element_type=single_float)


def move(block, where):
    sets = lax.axis_size("dp") // RING_SIZE
    ranks = lax.axis_size("ep")
    pairs = []
    for j in range(RING_SIZE):
        for e in range(ranks):
            to = where(j, e)
            if to is None:
                continue
            for s in range(sets):
                pairs.append(((j * sets + s) * ranks + e, (to[0] * sets + s) * ranks + to[1]))
    return lax.ppermute(block, AXES, pairs)


def around(j, hops):
    return RING[(PLACE[j] + hops) % RING_SIZE]


def to_core(block):
    return move(block, lambda j, e: (j, e ^ 1))


def to_side(block):
    return move(block, lambda j, e: (j, e ^ 2))


def out_hop(block, only_one=False):
    return move(
        block,
        lambda j, e: None if only_one and e % 2 == 0 else (around(j, 1 if e % 2 else -1), e),
    )


def back_hop(block, only_one=False):
    return move(
        block,
        lambda j, e: None if only_one and e % 2 == 0 else (around(j, -1 if e % 2 else 1), e),
    )


def ring_up(block):
    return move(block, lambda j, e: (around(j, 1), e))


def ring_down(block):
    return move(block, lambda j, e: (around(j, -1), e))


def in_set(sets):
    return [[j * sets + s for s in range(sets)] for j in range(RING_SIZE)]


def set_gather(block, axis):
    sets = lax.axis_size("dp") // RING_SIZE
    if sets == 1:
        return block
    return lax.all_gather(block, "dp", axis_index_groups=in_set(sets), axis=axis, tiled=True)


def set_scatter(block, axis):
    sets = lax.axis_size("dp") // RING_SIZE
    if sets == 1:
        return block
    return lax.psum_scatter(
        block, "dp", scatter_dimension=axis, axis_index_groups=in_set(sets), tiled=True
    )


def group_gather(block, ep_index):
    near = to_core(block)
    far = to_side(block)
    parts = [block, near, far, to_core(far)]
    whole = jnp.zeros((4,) + block.shape, block.dtype)
    for m, part in enumerate(parts):
        whole = lax.dynamic_update_index_in_dim(whole, part, ep_index ^ m, 0)
    return whole


def group_scatter(parts, ep_index, link=bf16):
    part = [lax.dynamic_index_in_dim(parts, ep_index ^ m, 0, False) for m in range(4)]
    got = to_core(jnp.stack([part[1], part[3]]).astype(link)).astype(single_float)
    near = part[0].astype(single_float) + got[0]
    far = part[2].astype(single_float) + got[1]
    return near + to_side(far.astype(link)).astype(single_float)


def ring_pieces(block, place):
    position = jnp.asarray(PLACE)[place]
    order = jnp.asarray(RING)
    half = block.shape[0] // 32 * 16
    up, down = [block], [block]
    for _ in range(3):
        up.append(ring_up(up[-1]))
        down.append(ring_down(down[-1]))
    pieces = [(place, block)]
    for k in range(1, 4):
        pieces.append((order[(position - k) % RING_SIZE], up[k]))
        pieces.append((order[(position + k) % RING_SIZE], down[k]))
    last = jnp.concatenate([ring_up(up[3][:half]), ring_down(down[3][half:])])
    return pieces + [(order[(position + 4) % RING_SIZE], last)]


def in_place_order(pieces):
    whole = jnp.zeros((RING_SIZE,) + pieces[0][1].shape, pieces[0][1].dtype)
    for where, piece in pieces:
        whole = lax.dynamic_update_index_in_dim(whole, piece, where, 0)
    return whole


def ring_scatter(parts, place, link=bf16):
    position = jnp.asarray(PLACE)[place]
    order = jnp.asarray(RING)
    half = parts.shape[1] // 2

    def part(hops):
        return lax.dynamic_index_in_dim(
            parts, order[(position + hops) % RING_SIZE], 0, False
        ).astype(single_float)

    opposite = part(4).astype(link)
    up = ring_up(opposite[:half]).astype(single_float)
    down = ring_down(opposite[half:]).astype(single_float)
    up = jnp.pad(up, ((0, parts.shape[1] - half), (0, 0)))
    down = jnp.pad(down, ((half, 0), (0, 0)))
    for k in (3, 2, 1):
        up = ring_up((part(k) + up).astype(link)).astype(single_float)
        down = ring_down((part(-k) + down).astype(link)).astype(single_float)
    return part(0) + up + down


def ring_exchange(blocks):
    sets = lax.axis_size("dp") // RING_SIZE
    groups = [[j * sets + s for j in range(RING_SIZE)] for s in range(sets)]
    return lax.all_to_all(blocks, "dp", 0, 0, axis_index_groups=groups if sets > 1 else None)


def token_gather(block, core):
    head, tail = block[:CORNER_ROWS], block[CORNER_ROWS:]
    tails = [jnp.concatenate([tail, to_core(tail)])]
    far = to_side(head)
    heads = [jnp.concatenate([head, to_core(head), far, to_core(far)])]
    side = move(tails[0], lambda j, e: (j, e ^ 2) if e % 2 == 0 else None)
    sides = [None]
    for k in range(4):
        tails.append(out_hop(tails[-1], k == 3))
        heads.append(out_hop(heads[-1], k == 3))
        if k < 3:
            sides.append(to_side(tails[-1]))
    side = side + move(tails[4], lambda j, e: (j, e ^ 2) if e % 2 else None)
    sides[0] = side
    tails[0] = jnp.where(core == 0, tails[0], tails[4])
    heads[0] = jnp.where(core == 0, heads[0], heads[4])
    return [(heads[k], tails[k], sides[k]) for k in range(4)], heads[4]


def token_scatter(slots, core):
    wide = lambda value: value.astype(single_float)
    low = lambda value: value.astype(bf16)
    heads = [slot[0] for slot in slots]
    tails = [wide(slot[1]) + wide(to_side(slot[2])) for slot in slots]

    def run(pieces):
        total = wide(back_hop(low(pieces[0]), True)) + wide(pieces[3])
        total = wide(back_hop(low(total))) + wide(pieces[2])
        total = wide(back_hop(low(total))) + wide(pieces[1])
        total = wide(back_hop(low(total)))
        return total + jnp.where(core == 0, wide(pieces[0]), 0.0)

    tail = run(tails)
    half = tail.shape[0] // 2
    tail = tail[:half] + wide(to_core(low(tail[half:])))
    head = run(heads).reshape(4, CORNER_ROWS, -1)
    got = wide(to_core(low(head[1::2])))
    near, far = head[0] + got[0], head[2] + got[1]
    head = near + wide(to_side(low(far)))
    return jnp.concatenate([head, tail])


def rms_scale(values):
    return lax.rsqrt(jnp.mean(values * values, -1, keepdims=True) + epsilon)


def rotary_table(positions):
    inverse = 1.0 / rotary_base ** (jnp.arange(0, HD, 2, dtype=single_float) / HD)
    angles = positions.astype(single_float)[:, None] * inverse[None, :]
    cosine, sine = jnp.cos(angles), jnp.sin(angles)
    return (
        jnp.concatenate([cosine, cosine], -1)[:, None, :],
        jnp.concatenate([-sine, sine], -1)[:, None, :],
    )


def rotate(values, table, direction):
    heads = values.reshape(values.shape[0], -1, HD)
    swapped = jnp.concatenate([heads[..., HD // 2 :], heads[..., : HD // 2]], -1)
    return heads * table[0] + swapped * (direction * table[1])


def kept_pairs(expert_ids, priority, capacity, ep_index, tokens):
    experts = capacity.shape[0]
    order = priority.reshape(-1, TOPK)
    own_experts = lax.dynamic_slice_in_dim(expert_ids, ep_index * tokens, tokens, 0)
    own_order = lax.dynamic_slice_in_dim(order, ep_index * tokens, tokens, 0)
    all_experts = expert_ids.reshape(1, -1)
    all_order = priority.reshape(1, -1)
    labels = jnp.arange(experts, dtype=jnp.int32)[None, :]
    kept = jnp.zeros((tokens, experts), bool)
    for k in range(TOPK):
        expert = own_experts[:, k : k + 1]
        ahead = (all_experts == expert) & (all_order < own_order[:, k : k + 1])
        slot = jnp.sum(ahead.astype(jnp.int32), 1, keepdims=True)
        kept = kept | ((labels == expert) & (slot < capacity[None, :]))
    return kept


def own_heads(features, core, side):
    lead = features.shape[:-1]
    split = features.reshape(lead + (2, -1, 2, HD))
    axis = len(lead)
    split = lax.dynamic_index_in_dim(split, core, axis, False)
    split = lax.dynamic_index_in_dim(split, side, axis + 1, False)
    return split.reshape(lead + (-1,))


def heads_to_rows(heads, dp_count, n, core, side, ep_index):
    rows = heads.shape[0]
    if 2 * n == HD:
        low, high = heads[..., :n], heads[..., n:]
        keep = jnp.where(core == 0, low, high).reshape(rows, -1)
        got = to_core(jnp.where(core == 0, high, low).reshape(rows, -1))
        return jnp.where(
            core == 0, jnp.concatenate([keep, got], 1), jnp.concatenate([got, keep], 1)
        )
    every = lax.all_gather(heads, "ep", axis=0)
    every = every.reshape((2, 2) + heads.shape).transpose(2, 1, 3, 0, 4)
    every = every.reshape(rows, dp_count, 4, n)
    return lax.dynamic_index_in_dim(every, ep_index, 2, False).reshape(rows, -1)


def rows_to_heads(features, dp_count, n, core, side, ep_index):
    rows = features.shape[0]
    if 2 * n == HD:
        half = features.shape[1] // 2
        low, high = features[:, :half], features[:, half:]
        keep = jnp.where(core == 0, low, high).reshape(rows, -1, n)
        got = to_core(jnp.where(core == 0, high, low)).reshape(rows, -1, n)
        return jnp.where(
            core == 0, jnp.concatenate([keep, got], -1), jnp.concatenate([got, keep], -1)
        )
    every = lax.all_gather(features, "ep", axis=0).reshape(4, rows, dp_count, n)
    every = every.transpose(1, 2, 0, 3).reshape(rows, -1)
    return own_heads(every, core, side).reshape(rows, -1, HD)


def cost(flops, bytes_accessed):
    return pl.CostEstimate(flops=int(flops), bytes_accessed=int(bytes_accessed), transcendentals=0)


def params(grid_rank):
    return pltpu.CompilerParams(
        dimension_semantics=("arbitrary",) * grid_rank, vmem_limit_bytes=VMEM_BYTES
    )


def lay_out_units(own, other):
    count, half, rows = own.shape
    step = half // 3

    def kernel(own_ref, other_ref, whole):
        for owner, part in enumerate((own_ref, other_ref)):
            for j in range(count):
                whole[owner, :, j * rows : (j + 1) * rows] = part[j]

    block = pl.BlockSpec((count, step, rows), lambda i: (0, i, 0))
    weights = pl.pallas_call(
        kernel,
        grid=(3,),
        in_specs=[block, block],
        out_specs=pl.BlockSpec((2, step, count * rows), lambda i: (0, i, 0)),
        out_shape=jax.ShapeDtypeStruct((2, half, count * rows), bf16),
        compiler_params=params(1),
        cost_estimate=cost(0, 8 * half * count * rows),
        name="lay_out_units",
    )(own, other)
    return weights.reshape(2 * half, count * rows)


def unit_set(shape, units):
    return lax.broadcasted_iota(jnp.int32, shape, 1) // units


def by_unit(columns, sets):
    spread = columns[-1]
    for k in range(len(columns) - 2, -1, -1):
        spread = jnp.where(sets == k, columns[k], spread)
    return spread


def routing(logits, kept, experts):
    lane = lax.broadcasted_iota(jnp.int32, logits.shape, 1)
    expert_lane = (lane >= 1) & (lane <= experts)
    share = jnp.sum(jnp.where(lane == 0, jax.nn.sigmoid(logits), 0.0), 1, keepdims=True)
    top = jnp.max(jnp.where(expert_lane, logits, masked_score), 1, keepdims=True)
    weight = jnp.exp(jnp.where(expert_lane, logits - top, masked_score))
    router = weight / jnp.sum(weight, 1, keepdims=True)
    return lane, share, router, kept.astype(single_float)


def unit_columns(lane, share, held, values):
    columns = [jnp.sum(jnp.where(lane == 1 + e, values, 0.0), 1, keepdims=True) for e in held]
    return [share] + columns[:EXP_DEV] + [share] + columns[EXP_DEV:]


def slot_specs(slot, width, lanes=None):
    if lanes is None:
        return [pl.BlockSpec((part.shape[0], width), lambda *_: (0, 0)) for part in slot]
    return [pl.BlockSpec((part.shape[0], HD), lambda *_: (0, width // HD)) for part in slot]


def slot_shapes(slot, width):
    return [jax.ShapeDtypeStruct((part.shape[0], width), bf16) for part in slot]


def split_rows(refs, value):
    start = 0
    for ref in refs:
        ref[...] = value[start : start + ref.shape[0]]
        start += ref.shape[0]


def weight_copies(sources, held, sems):
    return [
        pltpu.make_async_copy(source, held.at[m], sems.at[m]) for m, source in enumerate(sources)
    ]


def slot_call(kernel, held, slot, index, inputs, in_specs, kept, shapes, specs, total, width, name):
    step = sum(part.shape[0] for part in slot)
    shared = kept[0] if isinstance(kept[0], jax.Array) else None
    arrays = list(kept) if shared is not None else []
    kept_shapes = [jax.ShapeDtypeStruct(k.shape, k.dtype) for k in kept]
    kept_specs = [pl.BlockSpec((step, k.shape[1]), lambda *_: (index, 0)) for k in kept]
    first = 1 + len(inputs)
    return pl.pallas_call(
        kernel,
        grid_spec=pltpu.PrefetchScalarGridSpec(
            num_scalar_prefetch=1,
            grid=(1,),
            in_specs=in_specs + [pl.BlockSpec(memory_space=pl.ANY)] * len(arrays),
            out_specs=kept_specs + specs,
            scratch_shapes=[pltpu.VMEM((3, total, width), bf16), pltpu.SemaphoreType.DMA((3,))],
        ),
        out_shape=kept_shapes + shapes,
        input_output_aliases={first + i: i for i in range(len(arrays))},
        compiler_params=params(1),
        cost_estimate=cost(6 * step * width * total, 2 * (3 * total * width + 6 * step * width)),
        name=name,
    )(held, *inputs, *arrays)


def ffn_forward(held, slot, index, weights, rows, experts, kept):
    total, width = weights[0].shape
    units = total // (2 * (1 + EXP_DEV))
    step = sum(part.shape[0] for part in slot)
    known = len(kept) if isinstance(kept[0], jax.Array) else 0

    def kernel(held_ref, *refs):
        parts, lanes, (gate_w, up_w, down_w, rows_ref) = refs[:3], refs[3:6], refs[6:10]
        x_all, scaled, out, (low, act, rest, logit, w_ref, sems) = (
            refs[10 + known],
            refs[11 + known],
            refs[12 + known : 15 + known],
            refs[15 + known :],
        )
        copies = weight_copies((gate_w, up_w, down_w), w_ref, sems)
        for copy in copies:
            copy.start()
        x = jnp.concatenate([part[...] for part in parts], 0)
        x_all[...] = x
        logits = dot(x, rows_ref[...], contract_cols)
        logit[...] = logits
        kept_lanes = jnp.concatenate([part[...] for part in lanes], 0)
        lane, share, router, kept_now = routing(logits, kept_lanes, experts)
        held_now = [held_ref[i] for i in range(2 * EXP_DEV)]
        columns = unit_columns(lane, share, held_now, router * kept_now)
        copies[0].wait()
        gate = dot(x, w_ref[0], contract_cols)
        copies[1].wait()
        up = dot(x, w_ref[1], contract_cols)
        logistic = jax.nn.sigmoid(gate)
        active = gate * logistic
        act[...] = active.astype(bf16)
        rest[...] = (up * (logistic * (1.0 + gate * (1.0 - logistic)))).astype(bf16)
        hidden = (active * up).astype(bf16)
        low[...] = hidden
        factor = by_unit(columns, unit_set((step, total), units))
        hidden = (factor * hidden.astype(single_float)).astype(bf16)
        scaled[...] = hidden
        copies[2].wait()
        split_rows(out, dot(hidden, w_ref[2]).astype(bf16))

    whole = lambda *_: (0, 0)
    hbm = pl.BlockSpec(memory_space=pl.ANY)
    unit_block = pl.BlockSpec((step, total), whole)
    return slot_call(
        kernel,
        held,
        slot,
        index,
        [*slot, *slot, *weights, rows],
        slot_specs(slot, width) + slot_specs(slot, width, HD) + [hbm] * 3 + [pl.BlockSpec(rows.shape, whole)],
        kept,
        slot_shapes(slot, width)
        + [jax.ShapeDtypeStruct((step, total), bf16)] * 3
        + [jax.ShapeDtypeStruct((step, HD), single_float)],
        slot_specs(slot, width) + [unit_block] * 3 + [pl.BlockSpec((step, HD), whole)],
        total,
        width,
        "ffn_forward",
    )


def ffn_backward(held, slot, index, grads, weights, rows, saved, experts, kept):
    total, width = weights[0].shape
    units = total // (2 * (1 + EXP_DEV))
    step = sum(part.shape[0] for part in slot)
    known = len(kept) if isinstance(kept[0], jax.Array) else 0

    def kernel(held_ref, *refs):
        parts, lanes, (gate_w, up_w, down_w, rows_ref) = refs[:3], refs[3:6], refs[6:10]
        low, act, rest, logit = refs[10:14]
        g_all, gate_all, up_all, row_all = refs[14 + known : 18 + known]
        out, (w_ref, sems) = refs[18 + known : 21 + known], refs[21 + known :]
        copies = weight_copies((down_w, gate_w, up_w), w_ref, sems)
        for copy in copies:
            copy.start()
        grad = jnp.concatenate([part[...] for part in parts], 0)
        g_all[...] = grad
        kept_lanes = jnp.concatenate([part[...] for part in lanes], 0)
        lane, share, router, kept_now = routing(logit[...], kept_lanes, experts)
        held_now = [held_ref[i] for i in range(2 * EXP_DEV)]
        columns = unit_columns(lane, share, held_now, router * kept_now)
        sets = unit_set((step, total), units)
        copies[0].wait()
        d_hidden = dot(grad, w_ref[0], contract_cols)
        product = d_hidden * low[...].astype(single_float)
        sums = [
            jnp.sum(jnp.where(sets == k, product, 0.0), 1, keepdims=True)
            for k in range(len(columns))
        ]
        d_scaled = d_hidden * by_unit(columns, sets)
        d_gate = (d_scaled * rest[...].astype(single_float)).astype(bf16)
        d_up = (d_scaled * act[...].astype(single_float)).astype(bf16)
        gate_all[...] = d_gate
        up_all[...] = d_up
        d_router = jnp.zeros_like(router)
        for expert, total_of in zip(held_now, sums[1 : 1 + EXP_DEV] + sums[2 + EXP_DEV :]):
            d_router = d_router + jnp.where(lane == 1 + expert, total_of, 0.0)
        d_router = d_router * kept_now
        d_logits = router * (d_router - jnp.sum(router * d_router, 1, keepdims=True))
        d_share = (sums[0] + sums[1 + EXP_DEV]) * share * (1.0 - share)
        d_rows = jnp.where(lane == 0, d_share, d_logits)
        high = d_rows.astype(bf16).astype(single_float)
        remains = pltpu.roll(d_rows - high, ROW_SPLIT, 1)
        both = jnp.where(lane < ROW_SPLIT, high, remains).astype(bf16)
        row_all[...] = both
        copies[1].wait()
        d_ring = dot(d_gate, w_ref[1]) + dot(both, rows_ref[...])
        copies[2].wait()
        d_ring = d_ring + dot(d_up, w_ref[2])
        split_rows(out, d_ring.astype(bf16))

    whole = lambda *_: (0, 0)
    hbm = pl.BlockSpec(memory_space=pl.ANY)
    unit_block = pl.BlockSpec((step, total), whole)
    return slot_call(
        kernel,
        held,
        grads,
        index,
        [*grads, *slot, *weights, rows, *saved],
        slot_specs(grads, width)
        + slot_specs(slot, width, HD)
        + [hbm] * 3
        + [pl.BlockSpec(rows.shape, whole)]
        + [unit_block] * 3
        + [pl.BlockSpec((step, HD), whole)],
        kept,
        slot_shapes(grads, width),
        slot_specs(grads, width),
        total,
        width,
        "ffn_backward",
    )


def pack_unit_grads(mine, other):
    half, width = other.shape
    rows = width // RING_SIZE
    step = half // 3

    def kernel(own, got, out):
        for j in range(RING_SIZE):
            column = slice(j * rows, (j + 1) * rows)
            total = own[:, column].astype(single_float) + got[:, column].astype(single_float)
            out[j] = total.astype(bf16)

    block = pl.BlockSpec((step, width), lambda i: (i, 0))
    return pl.pallas_call(
        kernel,
        grid=(3,),
        in_specs=[block, block],
        out_specs=pl.BlockSpec((RING_SIZE, step, rows), lambda i: (0, i, 0)),
        out_shape=jax.ShapeDtypeStruct((RING_SIZE, half, rows), bf16),
        compiler_params=params(1),
        cost_estimate=cost(half * width, 6 * half * width),
        name="pack_unit_grads",
    )(mine, other)


def unpack_unit_grads(blocks):
    _, half, rows = blocks.shape
    units = half // (1 + EXP_DEV)
    width = units * RING_SIZE

    def kernel(part, shared, routed, joined):
        for s in range(1 + EXP_DEV):
            for j in range(RING_SIZE):
                joined[j * units : (j + 1) * units, :] = part[j, s * units : (s + 1) * units, :]
            turned = joined[...].astype(single_float).T
            if s == 0:
                shared[...] = turned
            else:
                routed[s - 1] = turned

    return pl.pallas_call(
        kernel,
        grid=(1,),
        in_specs=[pl.BlockSpec(blocks.shape, lambda i: (0, 0, 0))],
        out_specs=[
            pl.BlockSpec((rows, width), lambda i: (0, 0)),
            pl.BlockSpec((EXP_DEV, rows, width), lambda i: (0, 0, 0)),
        ],
        scratch_shapes=[pltpu.VMEM((width, rows), bf16)],
        out_shape=[
            jax.ShapeDtypeStruct((rows, width), single_float),
            jax.ShapeDtypeStruct((EXP_DEV, rows, width), single_float),
        ],
        compiler_params=params(1),
        cost_estimate=cost(0, 18 * rows * width),
        name="unpack_unit_grads",
    )(blocks)


def after(value, *events):
    return lax.optimization_barrier((value, events))[0]


def body(
    hidden_in,
    segment_ids,
    expert_ids,
    priority,
    capacity,
    norm_attn,
    w_query,
    w_key,
    w_value,
    bias_query,
    bias_key,
    bias_value,
    w_out,
    norm_ffn,
    w_router,
    w_shared_gate,
    shared_gate_proj,
    shared_up_proj,
    shared_down_proj,
    expert_gate_proj,
    expert_up_proj,
    expert_down_proj,
    out_grad,
):
    tokens, model_width = hidden_in.shape
    group_rows = 4 * tokens
    head_scale = HD ** (-0.5)
    dp_count = lax.axis_size("dp")
    sets = dp_count // RING_SIZE
    place = lax.axis_index("dp") // sets
    ep_index = lax.axis_index("ep")
    core, side = ep_index % 2, ep_index // 2
    n = norm_attn.shape[0]
    experts = capacity.shape[0]

    group_x = group_gather(hidden_in, ep_index).reshape(group_rows, model_width)
    segments = group_gather(segment_ids.reshape(1, tokens), ep_index).reshape(group_rows)
    group_index = jnp.arange(group_rows, dtype=jnp.int32)
    first = segments == segments[0]
    first_count = jnp.sum(first.astype(jnp.int32))
    positions = jnp.where(first, group_index, group_index - first_count)
    valid = (segments[:, None] == segments[None, :]) & (
        group_index[None, :] <= group_index[:, None]
    )
    table = rotary_table(positions)

    def head_columns(weight):
        split = weight.reshape(n, 2, -1, 2, HD).transpose(3, 1, 0, 2, 4)
        return split.reshape(4, n, -1)

    small = jnp.concatenate(
        [
            jnp.stack([norm_attn, bias_query, bias_key, bias_value, norm_ffn, w_shared_gate]),
            w_router.T,
            jnp.zeros((2, n), bf16),
        ]
    )
    qkv = jnp.concatenate([head_columns(w) for w in (w_query, w_key, w_value)], -1)
    head_width = qkv.shape[-1] // 3
    small = jnp.pad(small, ((0, 0), (0, 3 * head_width - n)))
    qkv = jnp.concatenate([qkv, jnp.broadcast_to(small, (4,) + small.shape)], 1)
    qkv = lax.all_to_all(qkv, "ep", 0, 0)
    small = set_gather(qkv[:, n:, :n].transpose(1, 0, 2).reshape(16, 4 * n), 1)
    row_block = small.shape[1]
    small = jnp.pad(small, ((0, 0), (0, 3 * head_width - row_block)))
    qkv = set_gather(qkv[:, :n].reshape(4 * n, -1), 0)
    qkv = ring_pieces(jnp.concatenate([qkv, small]), place)
    qkv_weight = in_place_order([(j, piece[:row_block]) for j, piece in qkv])
    qkv_weight = qkv_weight.reshape(model_width, -1)
    small = in_place_order([(j, piece[row_block:, :row_block]) for j, piece in qkv])
    small = small.transpose(1, 0, 2).reshape(16, model_width)
    attention_gain = small[0].astype(single_float)
    feedforward_gain = small[4].astype(single_float)
    gate_rows = small[5:14]
    gate_rows = jnp.pad(gate_rows, ((0, ROW_SPLIT - gate_rows.shape[0]), (0, 0)))
    gate_rows = jnp.pad(
        jnp.concatenate([gate_rows, gate_rows]), ((0, HD - 2 * ROW_SPLIT), (0, 0))
    )
    head_bias = own_heads(small[1:4], core, side).astype(single_float)
    out_weight = after(set_gather(w_out, 0), qkv[-1][1])
    out_pieces = ring_pieces(out_weight, place)
    out_weight = in_place_order(out_pieces).reshape(-1, model_width)

    def unit_slices(shared, routed):
        every = jnp.concatenate([shared[:, None, :], routed], 1)
        every = every.reshape(every.shape[0], 1 + EXP_DEV, RING_SIZE, -1)
        every = set_gather(every.transpose(2, 1, 3, 0), 3)
        return every.reshape(RING_SIZE, -1, row_block)

    units = expert_gate_proj.shape[2] // RING_SIZE
    half_units = (1 + EXP_DEV) * units
    matrices = (
        (shared_gate_proj, expert_gate_proj),
        (shared_up_proj, expert_up_proj),
        (shared_down_proj, expert_down_proj),
    )
    weights = []
    for (shared, routed), event in zip(matrices, (qkv[1][1], qkv[3][1], qkv[5][1])):
        blocks = unit_slices(*after((shared, routed), event))
        weights.append(ring_exchange(after(blocks, qkv[-1][1])))
    weights = [lay_out_units(blocks, to_core(blocks)) for blocks in weights]

    kept_own = kept_pairs(expert_ids, priority, capacity, ep_index, tokens)
    kept_own = jnp.pad(kept_own.astype(bf16), ((0, 0), (1, HD - 1 - experts)))

    x_float = group_x.astype(single_float)
    attn_in = (x_float * rms_scale(x_float) * attention_gain).astype(bf16)
    pre = dot(attn_in, qkv_weight)
    query = rotate(pre[:, :head_width] + head_bias[0], table, 1.0).astype(bf16)
    key = rotate(pre[:, head_width : 2 * head_width] + head_bias[1], table, 1.0).astype(bf16)
    value = (pre[:, 2 * head_width :] + head_bias[2]).astype(bf16).reshape(group_rows, -1, HD)

    def score_table():
        raw = jnp.einsum("thd,khd->htk", query, key, preferred_element_type=single_float)
        return jnp.where(valid[None], raw * head_scale, masked_score)

    scores = score_table()
    top_score = jnp.max(scores, -1, keepdims=True)
    exps = jnp.exp(scores - top_score)
    totals = jnp.sum(exps, -1, keepdims=True)
    log_total = top_score + jnp.log(totals)
    probs_low = (exps / totals).astype(bf16)
    attn = jnp.einsum("htk,khd->thd", probs_low, value, preferred_element_type=single_float)
    attn_rows = heads_to_rows(attn.astype(bf16), dp_count, n, core, side, ep_index)
    mid = hidden_in.astype(single_float) + group_scatter(
        dot(attn_rows, out_weight).reshape(4, tokens, model_width), ep_index
    )
    scale_two = rms_scale(mid)
    normed_two = mid * scale_two
    ffn_in = (normed_two * feedforward_gain).astype(bf16)

    ring_slots, last = token_gather(jnp.concatenate([ffn_in, kept_own], 1), core)
    grad_slots, _ = token_gather(after(out_grad, last), core)
    held = jnp.stack([EXP_DEV * (ep_index ^ flip) + i for flip in (0, 1) for i in range(EXP_DEV)])
    held = held.astype(jnp.int32)
    total = 2 * half_units
    all_rows = 4 * group_rows
    shape = lambda lanes: jax.ShapeDtypeStruct((all_rows, lanes), bf16)
    kept = [shape(model_width), shape(total)]
    results = [None] * 4
    for k in (1, 2, 3, 0):
        found = ffn_forward(held, ring_slots[k], k, weights, gate_rows, experts, kept)
        kept, results[k] = found[:2], (found[2:5], found[5:])
    ring_in, scaled_hidden = kept

    kept = [shape(model_width), shape(total), shape(total), shape(HD)]
    d_slots = [None] * 4
    for k in (0, 3, 2, 1):
        found = ffn_backward(
            held, ring_slots[k], k, grad_slots[k], weights, gate_rows, results[k][1], experts, kept
        )
        kept, d_slots[k] = found[:4], found[4:]
    ring_grad, d_gate, d_up, d_rows = kept
    d_ffn_in = token_scatter(d_slots, core)
    ffn_out = token_scatter([after(out, d_ffn_in) for out, _ in results], core)
    output = (mid + ffn_out).astype(bf16)
    grad_rows = dot(d_rows, ring_in, contract_rows)
    grad_rows = grad_rows[: 1 + experts] + grad_rows[ROW_SPLIT : ROW_SPLIT + 1 + experts]

    unit_grads = []
    for left, right in ((d_gate, ring_in), (d_up, ring_in), (scaled_hidden, ring_grad)):
        grad = dot(left, right, contract_rows).astype(bf16)
        grad = pack_unit_grads(grad, to_core(grad[half_units:]))
        grad = ring_exchange(grad)
        if sets == 1:
            shared, routed = unpack_unit_grads(grad)
            unit_grads.append((shared, routed.transpose(1, 0, 2)))
        else:
            grad = set_scatter(grad, 2).reshape(RING_SIZE, 1 + EXP_DEV, units, -1)
            grad = grad.transpose(3, 1, 0, 2).astype(single_float)
            grad = grad.reshape(grad.shape[0], 1 + EXP_DEV, -1)
            unit_grads.append((grad[:, 0], grad[:, 1:]))

    d_normed_two = d_ffn_in * feedforward_gain
    d_mid = out_grad.astype(single_float) + scale_two * (
        d_normed_two - normed_two * jnp.mean(d_normed_two * normed_two, -1, keepdims=True)
    )
    grad_gain_ffn = jnp.sum(d_ffn_in * normed_two, 0)
    d_branch = group_gather(d_mid.astype(bf16), ep_index).reshape(group_rows, model_width)
    d_attn = rows_to_heads(
        dot(d_branch, out_weight, contract_cols).astype(bf16), dp_count, n, core, side, ep_index
    )
    grad_out_rows = dot(attn_rows, d_branch, contract_rows).astype(bf16)
    grad_out_rows = ring_scatter(grad_out_rows.reshape(RING_SIZE, -1, model_width), place)
    grad_out_w = set_scatter(grad_out_rows, 0)
    probs = jnp.exp(score_table() - log_total)
    d_probs = jnp.einsum("thd,khd->htk", d_attn, value, preferred_element_type=single_float)
    d_value = jnp.einsum("htk,thd->khd", probs_low, d_attn, preferred_element_type=single_float)
    d_scores = (probs * (d_probs - jnp.sum(probs * d_probs, -1, keepdims=True))).astype(bf16)
    d_query = head_scale * jnp.einsum(
        "htk,khd->thd", d_scores, key, preferred_element_type=single_float
    )
    d_key = head_scale * jnp.einsum(
        "htk,thd->khd", d_scores, query, preferred_element_type=single_float
    )
    d_pre = [rotate(d_query, table, -1.0), rotate(d_key, table, -1.0), d_value]
    d_pre = jnp.concatenate([d.reshape(group_rows, -1) for d in d_pre], 1).astype(bf16)
    grad_bias = jnp.sum(d_pre.astype(single_float), 0).reshape(3, 1, -1, 1, HD)
    grad_qkv = dot(attn_in, d_pre, contract_rows).astype(bf16)
    grad_qkv = ring_scatter(grad_qkv.reshape(RING_SIZE, -1, 3 * head_width), place)
    grad_qkv = set_scatter(grad_qkv, 0).astype(bf16)
    grad_qkv = lax.all_to_all(grad_qkv.reshape(4, n, 3 * head_width), "ep", 0, 0)
    grad_qkv = grad_qkv.reshape(2, 2, n, 3, -1, HD).transpose(3, 2, 1, 4, 0, 5)
    grad_qkv = grad_qkv.reshape(3, n, model_width).astype(single_float)
    d_attn_in = group_scatter(
        dot(d_pre, qkv_weight, contract_cols).reshape(4, tokens, model_width), ep_index
    )
    own_x = hidden_in.astype(single_float)
    scale_one = rms_scale(own_x)
    normed_one = own_x * scale_one
    grad_gain_attn = jnp.sum(d_attn_in * normed_one, 0)
    d_normed_one = d_attn_in * attention_gain
    input_grad = d_mid + scale_one * (
        d_normed_one - normed_one * jnp.mean(d_normed_one * normed_one, -1, keepdims=True)
    )

    grad_bias_full = jnp.zeros((3, 2, model_width // (4 * HD), 2, HD), single_float)
    grad_bias_full = lax.dynamic_update_slice(grad_bias_full, grad_bias, (0, core, 0, side, 0))
    small_grads = jnp.concatenate(
        [
            grad_gain_attn[None],
            grad_bias_full.reshape(3, model_width),
            grad_gain_ffn[None],
            grad_rows,
            jnp.zeros((2, model_width), single_float),
        ]
    )
    small_grads = small_grads.reshape(16, RING_SIZE, sets, 4, n).transpose(3, 1, 0, 2, 4)
    small_grads = group_scatter(
        small_grads.reshape(4, RING_SIZE, 16, sets * n), ep_index, single_float
    )
    small_grads = set_scatter(ring_scatter(small_grads, place, single_float), 1)
    return (
        output,
        input_grad,
        small_grads[0],
        grad_qkv[0],
        grad_qkv[1],
        grad_qkv[2],
        small_grads[1],
        small_grads[2],
        small_grads[3],
        grad_out_w,
        small_grads[4],
        small_grads[6:14].T,
        small_grads[5],
        unit_grads[0][0],
        unit_grads[1][0],
        unit_grads[2][0],
        unit_grads[0][1],
        unit_grads[1][1],
        unit_grads[2][1],
    )


def solution(mesh):
    rows, vector, split = P(AXES, None), P(AXES), P("dp", "ep")
    routed = P("dp", "ep", None)
    return jax.shard_map(
        body,
        mesh=mesh,
        in_specs=(
            (rows, vector, P("dp", None), P("dp", None), P(), vector)
            + (rows,) * 3
            + (vector,) * 3
            + (rows, vector, rows, vector)
            + (split,) * 3
            + (routed,) * 3
            + (rows,)
        ),
        out_specs=(
            (rows, rows, vector)
            + (rows,) * 3
            + (vector,) * 3
            + (rows, vector, rows, vector)
            + (split,) * 3
            + (routed,) * 3
        ),
        check_vma=False,
    )
```

```python
import jax
import jax.numpy as jnp
from jax import lax
from jax.experimental import pallas as pl
from jax.experimental.pallas import tpu as pltpu
from jax.sharding import PartitionSpec as P

HD = 128
TOPK = 4
EXP_DEV = 2
RING_SIZE = 8
UNIT_SETS = 1 + EXP_DEV
CORNER_ROWS = 64
UNIT_PAD = 64
TILE_ROWS = 64
ROW_SPLIT = 16
VMEM_BYTES = 60 * 1024 * 1024
SLOT_VMEM_BYTES = 36 * 1024 * 1024
AXES = ("dp", "ep")

RING = (0, 2, 4, 6, 7, 5, 3, 1)
PLACE = tuple(RING.index(j) for j in range(RING_SIZE))

epsilon = 1e-06
rotary_base = 1000000.0
masked_score = -1e30
contract_rows = (((0,), (0,)), ((), ()))
contract_cols = (((1,), (1,)), ((), ()))
single_float = jnp.float32
bf16 = jnp.bfloat16


def dot(left, right, dims=(((1,), (0,)), ((), ()))):
    return lax.dot_general(left, right, dims, preferred_element_type=single_float)


def after(value, *events):
    return lax.optimization_barrier((value, events))[0] if events else value


def move(block, where):
    sets = lax.axis_size("dp") // RING_SIZE
    ranks = lax.axis_size("ep")
    pairs = []
    for j in range(RING_SIZE):
        for e in range(ranks):
            to = where(j, e)
            if to is None:
                continue
            for s in range(sets):
                pairs.append(((j * sets + s) * ranks + e, (to[0] * sets + s) * ranks + to[1]))
    return lax.ppermute(block, AXES, pairs)


def around(j, hops):
    return RING[(PLACE[j] + hops) % RING_SIZE]


def to_core(block):
    return move(block, lambda j, e: (j, e ^ 1))


def to_side(block):
    return move(block, lambda j, e: (j, e ^ 2))


def out_hop(block):
    return move(block, lambda j, e: (around(j, 1 if e % 2 else -1), e))


def back_hop(block):
    return move(block, lambda j, e: (around(j, -1 if e % 2 else 1), e))


def ring_up(block):
    return move(block, lambda j, e: (around(j, 1), e))


def ring_down(block):
    return move(block, lambda j, e: (around(j, -1), e))


def in_set(sets):
    return [[j * sets + s for s in range(sets)] for j in range(RING_SIZE)]


def set_gather(block, axis):
    sets = lax.axis_size("dp") // RING_SIZE
    if sets == 1:
        return block
    return lax.all_gather(block, "dp", axis_index_groups=in_set(sets), axis=axis, tiled=True)


def set_scatter(block, axis):
    sets = lax.axis_size("dp") // RING_SIZE
    if sets == 1:
        return block
    return lax.psum_scatter(
        block, "dp", scatter_dimension=axis, axis_index_groups=in_set(sets), tiled=True
    )


def group_gather(block, ep_index, before_last=()):
    near = to_core(block)
    far = after(to_side(block), *before_last)
    parts = [block, near, far, to_core(far)]
    whole = jnp.zeros((4,) + block.shape, block.dtype)
    for m, part in enumerate(parts):
        whole = lax.dynamic_update_index_in_dim(whole, part, ep_index ^ m, 0)
    return whole


def group_scatter(parts, ep_index, link=bf16, before_last=()):
    part = [lax.dynamic_index_in_dim(parts, ep_index ^ m, 0, False) for m in range(4)]
    got = to_core(jnp.stack([part[1], part[3]]).astype(link)).astype(single_float)
    near = part[0].astype(single_float) + got[0]
    far = part[2].astype(single_float) + got[1]
    far = after(far.astype(link), *before_last)
    return near + to_side(far).astype(single_float)


def group_exchange(blocks, ep_index):
    whole = jnp.zeros_like(blocks)
    for m in range(4):
        block = lax.dynamic_index_in_dim(blocks, ep_index ^ m, 0, False)
        if m:
            block = move(block, lambda j, e, m=m: (j, e ^ m))
        whole = lax.dynamic_update_index_in_dim(whole, block, ep_index ^ m, 0)
    return whole


def ring_position(place):
    return jnp.where(place % 2 == 1, RING_SIZE - 1 - place // 2, place // 2)


def place_at(position):
    position = position % RING_SIZE
    return jnp.where(position < 4, 2 * position, 2 * (RING_SIZE - 1 - position) + 1)


def ring_pieces(blocks, place, arrived):
    position = ring_position(place)
    up = down = blocks
    events = arrived(0, [(place, blocks)])
    for k in range(1, 4):
        up, down = after((up, down), *events)
        up, down = [ring_up(block) for block in up], [ring_down(block) for block in down]
        events = arrived(k, [(place_at(position - k), up), (place_at(position + k), down)])
    up, down = after((up, down), *events)
    last = []
    for first, second in zip(up, down):
        half = first.shape[0] // 32 * 16
        last.append(jnp.concatenate([ring_up(first[:half]), ring_down(second[half:])]))
    arrived(4, [(place_at(position + 4), last)])


def ring_scatter(every, place, events=()):
    position = ring_position(place)
    events = dict(enumerate(events))

    def part(hops):
        where = place_at(position + hops)
        return [wide(lax.dynamic_index_in_dim(parts, where, 0, False)) for parts in every]

    def hop(up, down, k):
        up, down = after(([low(x) for x in up], [low(x) for x in down]), *events.get(k, ()))
        return [wide(ring_up(x)) for x in up], [wide(ring_down(x)) for x in down]

    opposite = part(4)
    cuts = [x.shape[0] // 32 * 16 for x in opposite]
    up, down = hop(
        [x[:cut] for x, cut in zip(opposite, cuts)], [x[cut:] for x, cut in zip(opposite, cuts)], 0
    )
    up = [jnp.pad(x, ((0, y.shape[0] - x.shape[0]), (0, 0))) for x, y in zip(up, opposite)]
    down = [jnp.pad(x, ((y.shape[0] - x.shape[0], 0), (0, 0))) for x, y in zip(down, opposite)]
    for k in (3, 2, 1):
        up = [x + y for x, y in zip(part(k), up)]
        down = [x + y for x, y in zip(part(-k), down)]
        up, down = hop(up, down, 4 - k)
    return [x + y + z for x, y, z in zip(part(0), up, down)]


def ring_exchange(blocks):
    sets = lax.axis_size("dp") // RING_SIZE
    groups = [[j * sets + s for j in range(RING_SIZE)] for s in range(sets)]
    return lax.all_to_all(blocks, "dp", 0, 0, axis_index_groups=groups if sets > 1 else None)


def half_block(block):
    n, tail = CORNER_ROWS, (block.shape[0] - 4 * CORNER_ROWS) // 2
    return jnp.concatenate([block[:n], block[2 * n : 3 * n], block[4 * n : 4 * n + tail]])


def other_half(block):
    n, tail = CORNER_ROWS, (block.shape[0] - 4 * CORNER_ROWS) // 2
    return jnp.concatenate([block[n : 2 * n], block[3 * n : 4 * n], block[4 * n + tail :]])


def spread_half(half):
    n = CORNER_ROWS
    tail = half[2 * n :]
    heads, ends = jnp.zeros_like(half[:n]), jnp.zeros_like(tail)
    return jnp.concatenate([half[:n], heads, half[n : 2 * n], heads, tail, ends])


def gather_start(block):
    head, tail = block[:CORNER_ROWS], block[CORNER_ROWS:]
    far = to_side(head)
    ring = jnp.concatenate([head, to_core(head), far, to_core(far), tail, to_core(tail)])
    return ring, (jnp.concatenate([head, far, tail]), to_side(tail))


def with_side(block, heads):
    return block, to_side(block[heads:])


def scatter_parts(parts):
    count = len(parts) // 2
    out = []
    for block, side in zip(parts[:count], parts[count:]):
        block, side = block.astype(single_float), to_side(side).astype(single_float)
        cut = block.shape[0] - side.shape[0]
        out.append(jnp.concatenate([block[:cut], block[cut:] + side]))
    return out


def scatter_end(total, own):
    n = CORNER_ROWS
    got = to_core(other_half(total).astype(bf16)).astype(single_float)
    total = half_block(total) + own + got
    far = to_side(total[n : 2 * n].astype(bf16)).astype(single_float)
    return jnp.concatenate([total[:n] + far, total[2 * n :]])


def low(value):
    return value.astype(bf16)


def wide(value):
    return value.astype(single_float)


def rms_scale(values):
    return lax.rsqrt(jnp.mean(values * values, -1, keepdims=True) + epsilon)


def rotary_table(positions):
    inverse = 1.0 / rotary_base ** (jnp.arange(0, HD, 2, dtype=single_float) / HD)
    angles = positions.astype(single_float)[:, None] * inverse[None, :]
    cosine, sine = jnp.cos(angles), jnp.sin(angles)
    return (
        jnp.concatenate([cosine, cosine], -1)[:, None, :],
        jnp.concatenate([-sine, sine], -1)[:, None, :],
    )


def rotate(values, table, direction):
    heads = values.reshape(values.shape[0], -1, HD)
    swapped = jnp.concatenate([heads[..., HD // 2 :], heads[..., : HD // 2]], -1)
    return heads * table[0] + swapped * (direction * table[1])


def kept_pairs(expert_ids, priority, capacity, ep_index, tokens):
    experts = capacity.shape[0]
    order = priority.reshape(-1, TOPK)
    own_experts = lax.dynamic_slice_in_dim(expert_ids, ep_index * tokens, tokens, 0)
    own_order = lax.dynamic_slice_in_dim(order, ep_index * tokens, tokens, 0)
    all_experts = expert_ids.reshape(1, -1)
    all_order = priority.reshape(1, -1)
    labels = jnp.arange(experts, dtype=jnp.int32)[None, :]
    kept = jnp.zeros((tokens, experts), bool)
    for k in range(TOPK):
        expert = own_experts[:, k : k + 1]
        ahead = (all_experts == expert) & (all_order < own_order[:, k : k + 1])
        slot = jnp.sum(ahead.astype(jnp.int32), 1, keepdims=True)
        kept = kept | ((labels == expert) & (slot < capacity[None, :]))
    return kept


def own_heads(features, core, side):
    lead = features.shape[:-1]
    split = features.reshape(lead + (2, -1, 2, HD))
    axis = len(lead)
    split = lax.dynamic_index_in_dim(split, core, axis, False)
    split = lax.dynamic_index_in_dim(split, side, axis + 1, False)
    return split.reshape(lead + (-1,))


def heads_to_rows(heads, dp_count, n, core, side, ep_index):
    rows = heads.shape[0]
    if 2 * n == HD:
        low, high = heads[..., :n], heads[..., n:]
        keep = jnp.where(core == 0, low, high).reshape(rows, -1)
        got = to_core(jnp.where(core == 0, high, low).reshape(rows, -1))
        return jnp.where(
            core == 0, jnp.concatenate([keep, got], 1), jnp.concatenate([got, keep], 1)
        )
    every = lax.all_gather(heads, "ep", axis=0)
    every = every.reshape((2, 2) + heads.shape).transpose(2, 1, 3, 0, 4)
    every = every.reshape(rows, dp_count, 4, n)
    return lax.dynamic_index_in_dim(every, ep_index, 2, False).reshape(rows, -1)


def rows_to_heads(features, dp_count, n, core, side, ep_index):
    rows = features.shape[0]
    if 2 * n == HD:
        half = features.shape[1] // 2
        low, high = features[:, :half], features[:, half:]
        keep = jnp.where(core == 0, low, high).reshape(rows, -1, n)
        got = to_core(jnp.where(core == 0, high, low)).reshape(rows, -1, n)
        return jnp.where(
            core == 0, jnp.concatenate([keep, got], -1), jnp.concatenate([got, keep], -1)
        )
    every = lax.all_gather(features, "ep", axis=0).reshape(4, rows, dp_count, n)
    every = every.transpose(1, 2, 0, 3).reshape(rows, -1)
    return own_heads(every, core, side).reshape(rows, -1, HD)


def cost(flops, bytes_accessed):
    return pl.CostEstimate(flops=int(flops), bytes_accessed=int(bytes_accessed), transcendentals=0)


def params(grid_rank, vmem=VMEM_BYTES):
    return pltpu.CompilerParams(
        dimension_semantics=("arbitrary",) * grid_rank, vmem_limit_bytes=vmem
    )


def padded(units):
    return -(-units // UNIT_PAD) * UNIT_PAD


def lay_out_units(blocks, offsets, step):
    count, _, rows = blocks[0].shape
    wide_step = padded(step)

    def kernel(*refs):
        whole = refs[-1]
        for owner, part in enumerate(refs[:-1]):
            for j in range(count):
                whole[owner, :step, j * rows : (j + 1) * rows] = part[j]
            if wide_step > step:
                whole[owner, step:, :] = jnp.zeros((wide_step - step, count * rows), bf16)

    half = UNIT_SETS * wide_step
    weights = pl.pallas_call(
        kernel,
        grid=(UNIT_SETS,),
        in_specs=[
            pl.BlockSpec((count, step, rows), lambda i, first=first: (0, first + i, 0))
            for first in offsets
        ],
        out_specs=pl.BlockSpec((len(blocks), wide_step, count * rows), lambda i: (0, i, 0)),
        out_shape=jax.ShapeDtypeStruct((len(blocks), half, count * rows), bf16),
        compiler_params=params(1),
        cost_estimate=cost(0, 4 * len(blocks) * half * count * rows),
        name="lay_out_units",
    )(*blocks)
    return weights.reshape(len(blocks) * half, count * rows)


def routing(logits, kept, experts):
    lane = lax.broadcasted_iota(jnp.int32, logits.shape, 1)
    expert_lane = (lane >= 1) & (lane <= experts)
    top = jnp.max(jnp.where(expert_lane, logits, masked_score), 1, keepdims=True)
    weight = jnp.exp(jnp.where(expert_lane, logits - top, masked_score))
    router = weight / jnp.sum(weight, 1, keepdims=True)
    return lane, jax.nn.sigmoid(logits), router, kept.astype(single_float)


def high_low(value):
    high = value.astype(bf16)
    return high, (value - high.astype(single_float)).astype(bf16)


def unit_factor(lane, share, router, kept, spread_ref, total):
    high, rest = high_low(jnp.where(lane == 0, share, router * kept))
    spread = spread_ref[:, :total]
    return dot(high, spread) + dot(rest, spread)


def by_tiles(rows, total, work):
    def chunk(i, carry):
        here = pl.ds(pl.multiple_of(i * TILE_ROWS, TILE_ROWS), TILE_ROWS)
        for first in range(0, total, HD):
            work(here, first)
        return carry

    lax.fori_loop(0, rows // TILE_ROWS, chunk, 0)


def slot_specs(slot, width, lanes=None):
    if lanes is None:
        return [pl.BlockSpec((part.shape[0], width), lambda *_: (0, 0)) for part in slot]
    return [pl.BlockSpec((part.shape[0], HD), lambda *_: (0, width // HD)) for part in slot]


def slot_shapes(slot, width):
    return [jax.ShapeDtypeStruct((part.shape[0], width), bf16) for part in slot]


def split_rows(refs, value):
    start = 0
    for ref in refs:
        ref[...] = value[start : start + ref.shape[0]]
        start += ref.shape[0]


def slot_call(kernel, slot, index, inputs, in_specs, kept, shapes, specs, scratch, flops, name):
    step = sum(part.shape[0] for part in slot)
    arrays = list(kept) if isinstance(kept[0], jax.Array) else []
    kept_shapes = [jax.ShapeDtypeStruct(k.shape, k.dtype) for k in kept]
    kept_specs = [pl.BlockSpec((step, k.shape[1]), lambda *_: (index, 0)) for k in kept]
    return pl.pallas_call(
        kernel,
        grid=(1,),
        in_specs=in_specs + [pl.BlockSpec(memory_space=pl.ANY)] * len(arrays),
        out_specs=kept_specs + specs,
        out_shape=kept_shapes + shapes,
        scratch_shapes=scratch,
        input_output_aliases={len(inputs) + i: i for i in range(len(arrays))},
        compiler_params=params(1, SLOT_VMEM_BYTES),
        cost_estimate=cost(flops, flops // 100),
        name=name,
    )(*inputs, *arrays)


def ffn_forward(slot, index, gate_up, down, rows, spread, experts, kept):
    total, width = down.shape
    step = sum(part.shape[0] for part in slot)
    known = len(kept) if isinstance(kept[0], jax.Array) else 0

    def kernel(*refs):
        count = len(slot)
        parts, lanes, refs = refs[:count], refs[count : 2 * count], refs[2 * count :]
        (gate_up_w, down_w, rows_ref, spread_ref), refs = refs[:4], refs[4 + known :]
        (x_all, scaled), out = refs[:2], refs[2 : 2 + count]
        low_ref, act, rest, logit, both, factor = refs[2 + count :]
        x = jnp.concatenate([part[...] for part in parts], 0)
        x_all[...] = x
        logits = dot(x, rows_ref[...], contract_cols)
        logit[...] = logits
        kept_lanes = jnp.concatenate([part[...] for part in lanes], 0)
        lane, share, router, kept_now = routing(logits, kept_lanes, experts)
        factor[...] = unit_factor(lane, share, router, kept_now, spread_ref, total)
        both[...] = dot(x, gate_up_w[...], contract_cols)

        def work(here, first):
            tile = here, pl.ds(first, HD)
            gate, up = both[tile], both[here, pl.ds(total + first, HD)]
            logistic = jax.nn.sigmoid(gate)
            active = gate * logistic
            act[tile] = active.astype(bf16)
            rest[tile] = (up * (logistic + active * (1.0 - logistic))).astype(bf16)
            hidden = (active * up).astype(bf16)
            low_ref[tile] = hidden
            scaled[tile] = (factor[tile] * hidden.astype(single_float)).astype(bf16)

        by_tiles(step, total, work)
        split_rows(out, dot(scaled[...], down_w[...]).astype(bf16))

    whole = lambda *_: (0, 0)
    resident = pl.BlockSpec(memory_space=pltpu.VMEM)
    unit_block = pl.BlockSpec((step, total), whole)
    return slot_call(
        kernel,
        slot,
        index,
        [*slot, *slot, gate_up, down, rows, spread],
        slot_specs(slot, width) + slot_specs(slot, width, HD) + [resident] * 4,
        kept,
        slot_shapes(slot, width)
        + [jax.ShapeDtypeStruct((step, total), bf16)] * 3
        + [jax.ShapeDtypeStruct((step, HD), single_float)],
        slot_specs(slot, width) + [unit_block] * 3 + [pl.BlockSpec((step, HD), whole)],
        [pltpu.VMEM((step, 2 * total), single_float), pltpu.VMEM((step, total), single_float)],
        6 * step * width * total,
        "ffn_forward",
    )


def ffn_backward(slot, index, grads, gate_up, down, rows, spread, saved, experts, kept):
    total, width = down.shape
    step = sum(part.shape[0] for part in slot)
    known = len(kept) if isinstance(kept[0], jax.Array) else 0

    def kernel(*refs):
        count = len(slot)
        parts, lanes, refs = refs[:count], refs[count : 2 * count], refs[2 * count :]
        (gate_up_w, down_w, rows_ref, spread_ref), refs = refs[:4], refs[4:]
        (low_ref, act, rest, logit), refs = refs[:4], refs[4 + known :]
        (d_both, row_all), out = refs[:2], refs[2 : 2 + count]
        d_hidden, factor, products = refs[2 + count :]
        grad = jnp.concatenate([part[...] for part in parts], 0)
        kept_lanes = jnp.concatenate([part[...] for part in lanes], 0)
        lane, share, router, kept_now = routing(logit[...], kept_lanes, experts)
        factor[...] = unit_factor(lane, share, router, kept_now, spread_ref, total)
        d_hidden[...] = dot(grad, down_w[...], contract_cols)

        def work(here, first):
            tile, other = (here, pl.ds(first, HD)), (here, pl.ds(total + first, HD))
            d_unit = d_hidden[tile]
            high, remains = high_low(d_unit * low_ref[tile].astype(single_float))
            products[tile] = high
            products[other] = remains
            d_unit = d_unit * factor[tile]
            d_both[tile] = (d_unit * rest[tile].astype(single_float)).astype(bf16)
            d_both[other] = (d_unit * act[tile].astype(single_float)).astype(bf16)

        by_tiles(step, total, work)
        sums = dot(products[...], spread_ref[...], contract_cols)
        d_router = sums * kept_now
        d_logits = router * (d_router - jnp.sum(router * d_router, 1, keepdims=True))
        d_rows = jnp.where(lane == 0, sums * share * (1.0 - share), d_logits)
        high = d_rows.astype(bf16).astype(single_float)
        remains = pltpu.roll(d_rows - high, ROW_SPLIT, 1)
        rows_both = jnp.where(lane < ROW_SPLIT, high, remains).astype(bf16)
        row_all[...] = rows_both
        d_ring = dot(d_both[...], gate_up_w[...]) + dot(rows_both, rows_ref[...])
        split_rows(out, d_ring.astype(bf16))

    whole = lambda *_: (0, 0)
    resident = pl.BlockSpec(memory_space=pltpu.VMEM)
    unit_block = pl.BlockSpec((step, total), whole)
    return slot_call(
        kernel,
        grads,
        index,
        [*grads, *slot, gate_up, down, rows, spread, *saved],
        slot_specs(grads, width)
        + slot_specs(slot, width, HD)
        + [resident] * 4
        + [unit_block] * 3
        + [pl.BlockSpec((step, HD), whole)],
        kept,
        slot_shapes(grads, width),
        slot_specs(grads, width),
        [
            pltpu.VMEM((step, total), single_float),
            pltpu.VMEM((step, total), single_float),
            pltpu.VMEM((step, 2 * total), bf16),
        ],
        6 * step * width * total,
        "ffn_backward",
    )


def pack_unit_grads(pairs, units):
    width = pairs[0][0].shape[1]
    rows, wide_step = width // RING_SIZE, padded(units)
    steps = len(pairs) * UNIT_SETS

    def kernel(*refs):
        out = refs[-1]
        for p in range(len(pairs)):
            own, got = refs[2 * p : 2 * p + 2]

            @pl.when(pl.program_id(0) // UNIT_SETS == p)
            def _():
                for j in range(RING_SIZE):
                    part = (slice(0, units), slice(j * rows, (j + 1) * rows))
                    total = own[part].astype(single_float) + got[part].astype(single_float)
                    out[j] = total.astype(bf16)

    def block(p):
        return pl.BlockSpec(
            (wide_step, width), lambda i: (jnp.clip(i - p * UNIT_SETS, 0, UNIT_SETS - 1), 0)
        )

    return pl.pallas_call(
        kernel,
        grid=(steps,),
        in_specs=[block(p) for p in range(len(pairs)) for _ in range(2)],
        out_specs=pl.BlockSpec((RING_SIZE, units, rows), lambda i: (0, i, 0)),
        out_shape=jax.ShapeDtypeStruct((RING_SIZE, steps * units, rows), bf16),
        compiler_params=params(1),
        cost_estimate=cost(0, 6 * steps * units * width),
        name="pack_unit_grads",
    )(*[array for pair in pairs for array in pair])


def unpack_unit_grads(blocks, matrix, units):
    rows = blocks.shape[2]
    half = UNIT_SETS * units
    width = units * RING_SIZE

    def kernel(part, shared, routed, joined):
        for s in range(1 + EXP_DEV):
            for j in range(RING_SIZE):
                joined[j * units : (j + 1) * units, :] = part[j, s * units : (s + 1) * units, :]
            turned = joined[...].astype(single_float).T
            if s == 0:
                shared[...] = turned
            else:
                routed[s - 1] = turned

    return pl.pallas_call(
        kernel,
        grid=(1,),
        in_specs=[pl.BlockSpec((RING_SIZE, half, rows), lambda i: (0, matrix, 0))],
        out_specs=[
            pl.BlockSpec((rows, width), lambda i: (0, 0)),
            pl.BlockSpec((EXP_DEV, rows, width), lambda i: (0, 0, 0)),
        ],
        scratch_shapes=[pltpu.VMEM((width, rows), bf16)],
        out_shape=[
            jax.ShapeDtypeStruct((rows, width), single_float),
            jax.ShapeDtypeStruct((EXP_DEV, rows, width), single_float),
        ],
        compiler_params=params(1),
        cost_estimate=cost(0, 18 * rows * width),
        name="unpack_unit_grads",
    )(blocks)


def body(
    hidden_in,
    segment_ids,
    expert_ids,
    priority,
    capacity,
    norm_attn,
    w_query,
    w_key,
    w_value,
    bias_query,
    bias_key,
    bias_value,
    w_out,
    norm_ffn,
    w_router,
    w_shared_gate,
    shared_gate_proj,
    shared_up_proj,
    shared_down_proj,
    expert_gate_proj,
    expert_up_proj,
    expert_down_proj,
    out_grad,
):
    tokens, model_width = hidden_in.shape
    group_rows = 4 * tokens
    head_scale = HD ** (-0.5)
    dp_count = lax.axis_size("dp")
    sets = dp_count // RING_SIZE
    place = lax.axis_index("dp") // sets
    ep_index = lax.axis_index("ep")
    core, side = ep_index % 2, ep_index // 2
    n = norm_attn.shape[0]
    experts = capacity.shape[0]

    group_x = group_gather(hidden_in, ep_index).reshape(group_rows, model_width)
    segments = group_gather(segment_ids.reshape(1, tokens), ep_index).reshape(group_rows)
    group_index = jnp.arange(group_rows, dtype=jnp.int32)
    first = segments == segments[0]
    first_count = jnp.sum(first.astype(jnp.int32))
    positions = jnp.where(first, group_index, group_index - first_count)
    valid = (segments[:, None] == segments[None, :]) & (
        group_index[None, :] <= group_index[:, None]
    )
    table = rotary_table(positions)

    row_block = model_width // RING_SIZE
    units = expert_gate_proj.shape[2] // RING_SIZE
    half_units = (1 + EXP_DEV) * padded(units)

    def unit_slices(shared, routed):
        every = jnp.concatenate([shared[:, None, :], routed], 1)
        every = every.reshape(every.shape[0], 1 + EXP_DEV, RING_SIZE, -1)
        every = set_gather(every.transpose(2, 1, 3, 0), 3)
        return every.reshape(RING_SIZE, -1, row_block)

    gate_units = ring_exchange(unit_slices(shared_gate_proj, expert_gate_proj))

    def head_columns(weight):
        split = weight.reshape(n, 2, -1, 2, HD).transpose(3, 1, 0, 2, 4)
        return split.reshape(4, n, -1)

    small = jnp.concatenate(
        [
            jnp.stack([norm_attn, bias_query, bias_key, bias_value, norm_ffn, w_shared_gate]),
            w_router.T,
            jnp.zeros((2, n), bf16),
        ]
    )
    qkv = jnp.concatenate([head_columns(w) for w in (w_query, w_key, w_value)], -1)
    head_width = qkv.shape[-1] // 3
    quarter = row_block // 4
    small = jnp.pad(small, ((0, 0), (0, 3 * head_width - n)))
    qkv = jnp.concatenate([qkv, jnp.broadcast_to(small, (4,) + small.shape)], 1)
    qkv = group_exchange(qkv, ep_index)
    small = set_gather(qkv[:, n:, :n].transpose(1, 0, 2).reshape(16, 4 * n), 1)
    small = jnp.pad(small, ((0, 0), (0, 3 * head_width - row_block)))
    qkv = set_gather(qkv[:, :n].reshape(4 * n, -1), 0)
    gathered = [
        jnp.zeros((RING_SIZE, row_block, 3 * head_width), bf16),
        jnp.zeros((RING_SIZE, quarter, model_width), bf16),
        jnp.zeros((RING_SIZE, 16, row_block), bf16),
    ]
    later_units = []

    def arrived(k, pieces):
        for where, (dense, rows) in pieces:
            found = dense[:row_block], rows, dense[row_block:, :row_block]
            for i in range(3):
                gathered[i] = lax.dynamic_update_index_in_dim(gathered[i], found[i], where, 0)
        if k in (0, 4):
            return ()
        if k < 3:
            halves = ((shared_up_proj, expert_up_proj), (shared_down_proj, expert_down_proj))[k - 1]
            later_units.append(unit_slices(*after(halves, pieces[0][1][0])))
        return (gate_units,) if k == 1 else (later_units[k - 2],)

    ring_pieces([jnp.concatenate([qkv, small]), set_gather(w_out, 0)], place, arrived)
    qkv_weight = gathered[0].reshape(model_width, -1)
    out_weight = gathered[1].reshape(-1, model_width)
    small = gathered[2].transpose(1, 0, 2).reshape(16, model_width)
    attention_gain = small[0].astype(single_float)
    feedforward_gain = small[4].astype(single_float)
    gate_rows = small[5:14]
    gate_rows = jnp.pad(gate_rows, ((0, ROW_SPLIT - gate_rows.shape[0]), (0, 0)))
    gate_rows = jnp.pad(
        jnp.concatenate([gate_rows, gate_rows]), ((0, HD - 2 * ROW_SPLIT), (0, 0))
    )
    head_bias = own_heads(small[1:4], core, side).astype(single_float)
    late_units = ring_exchange(after(jnp.concatenate(later_units, 1), gathered[0]))

    kept_own = kept_pairs(expert_ids, priority, capacity, ep_index, tokens)
    kept_own = jnp.pad(kept_own.astype(bf16), ((0, 0), (1, HD - 1 - experts)))

    x_float = group_x.astype(single_float)
    attn_in = (x_float * rms_scale(x_float) * attention_gain).astype(bf16)
    pre = dot(attn_in, qkv_weight)
    query = rotate(pre[:, :head_width] + head_bias[0], table, 1.0).astype(bf16)
    key = rotate(pre[:, head_width : 2 * head_width] + head_bias[1], table, 1.0).astype(bf16)
    value = (pre[:, 2 * head_width :] + head_bias[2]).astype(bf16).reshape(group_rows, -1, HD)

    def score_table():
        raw = jnp.einsum("thd,khd->htk", query, key, preferred_element_type=single_float)
        return jnp.where(valid[None], raw * head_scale, masked_score)

    scores = score_table()
    top_score = jnp.max(scores, -1, keepdims=True)
    exps = jnp.exp(scores - top_score)
    totals = jnp.sum(exps, -1, keepdims=True)
    log_total = top_score + jnp.log(totals)
    probs_low = (exps / totals).astype(bf16)
    attn = jnp.einsum("htk,khd->thd", probs_low, value, preferred_element_type=single_float)
    attn_rows = heads_to_rows(attn.astype(bf16), dp_count, n, core, side, ep_index)
    mid = hidden_in.astype(single_float) + group_scatter(
        dot(attn_rows, out_weight).reshape(4, tokens, model_width),
        ep_index,
        before_last=(late_units,),
    )
    scale_two = rms_scale(mid)
    normed_two = mid * scale_two
    ffn_in = (normed_two * feedforward_gain).astype(bf16)

    def gathered_slots(block, first_events, step_events):
        block, own = gather_start(block)
        sides = []
        for k in (1, 2, 3):
            block = out_hop(after(block, *first_events, *step_events(k), *sides[:-1]))
            first_events = ()
            slot = with_side(block, 4 * CORNER_ROWS)
            sides = sides[-1:] + [slot[1]]
            yield k, slot, block
        block = out_hop(after(half_block(block), *step_events(0), *sides[:-1]))
        far = with_side(block, 2 * CORNER_ROWS)
        yield 0, (own[0], far[0], own[1], far[1]), block

    ready = []
    moved = [gate_units]
    ring_slots = [None] * 4

    def lay_out(k):
        if k == 1:
            moved.append(to_core(after(gate_units, ffn_in)))
        if k == 2:
            ready.append(moved[-1])
            moved.append(to_core(after(late_units, ready[-1])))
        if k == 3:
            own, other = moved[1:]
            ready.append(
                lay_out_units(
                    [gate_units, own, late_units, other], [0, 0, 0, 0], units
                )
            )
        if k == 0:
            ready.append(
                lay_out_units([late_units, moved[2]], [UNIT_SETS, UNIT_SETS], units)
            )
        return ready[-1:]

    tokens_in = jnp.concatenate([ffn_in, kept_own], 1)
    for k, slot, block in gathered_slots(tokens_in, (), lay_out):
        ring_slots[k] = slot
    gate_up, down = ready[-2:]

    held = [EXP_DEV * (ep_index ^ flip) + i for flip in (0, 1) for i in range(EXP_DEV)]
    lanes = [0] + [1 + e for e in held[:EXP_DEV]] + [0] + [1 + e for e in held[EXP_DEV:]]
    lanes = jnp.repeat(jnp.stack([jnp.asarray(lane, jnp.int32) for lane in lanes]), padded(units))
    spread = (jnp.arange(HD, dtype=jnp.int32)[:, None] == lanes[None, :]).astype(bf16)
    spread = jnp.concatenate([spread, spread], 1)
    total = 2 * half_units
    all_rows = 4 * group_rows
    shape = lambda lanes: jax.ShapeDtypeStruct((all_rows, lanes), bf16)

    kept = [shape(model_width), shape(total)]
    results, grad_slots = [None] * 4, [None] * 4
    done = []

    def forward(k):
        found = ffn_forward(
            after(ring_slots[k], *done[-1:]), k, gate_up, down, gate_rows, spread, experts, kept
        )
        count = len(ring_slots[k])
        results[k] = found[2 : 2 + count], found[2 + count :]
        return found[:2]

    for k, slot, last in gathered_slots(out_grad, (block,), lambda k: kept[1:] if done else ()):
        kept = forward(k)
        grad_slots[k] = slot
        done.append(last)
    ring_in, scaled_hidden = kept
    ring_grad = jnp.concatenate([part for slot in grad_slots for part in slot])

    def backward(k, kept, *events):
        found = ffn_backward(
            ring_slots[k],
            k,
            after(grad_slots[k], *events),
            gate_up,
            down,
            gate_rows,
            spread,
            results[k][1],
            experts,
            kept,
        )
        return found[:2], scatter_parts(found[2:])

    def back_pair(first, second, *events):
        both = after(jnp.concatenate([low(first), low(second)]), *events)
        both = wide(back_hop(both))
        return both[: first.shape[0]], both[first.shape[0] :]

    kept = [shape(2 * total), shape(HD)]
    out_own, out_far = scatter_parts(results[0][0])
    out = wide(back_hop(low(out_far)))
    (out_slot,) = scatter_parts(after(results[3][0], out_far))
    kept, (d_own, d_far) = backward(0, kept, ring_grad)
    d_ring, out = back_pair(d_far, spread_half(out) + out_slot)
    (out_slot,) = scatter_parts(after(results[2][0], d_far))
    kept, (d_slot,) = backward(3, kept, d_far)
    down_grad = dot(*after((scaled_hidden, ring_grad), d_far), contract_rows).astype(bf16)
    d_ring, out = back_pair(spread_half(d_ring) + d_slot, out + out_slot, kept, down_grad)
    (out_slot,) = scatter_parts(after(results[1][0], d_slot))
    kept, (d_slot,) = backward(2, kept, d_slot)
    d_ring, out = back_pair(d_ring + d_slot, out + out_slot, kept)
    kept, (d_slot,) = backward(1, kept, d_slot)
    d_both, d_rows = kept

    def pair(grad):
        return grad, to_core(grad[half_units:])

    down_grad = pack_unit_grads([pair(after(down_grad, d_slot))], units)
    d_ring = wide(back_hop(low(d_ring + d_slot)))
    down_grad = ring_exchange(down_grad)
    gate_grad = dot(d_both[:, :total], ring_in, contract_rows).astype(bf16)
    d_ring, out = after((d_ring, out), gate_grad)
    d_ffn_in = scatter_end(d_ring, d_own)
    output = (mid + scatter_end(out, out_own)).astype(bf16)
    grad_rows = dot(d_rows, ring_in, contract_rows)
    grad_rows = grad_rows[: 1 + experts] + grad_rows[ROW_SPLIT : ROW_SPLIT + 1 + experts]

    d_normed_two = d_ffn_in * feedforward_gain
    d_mid = out_grad.astype(single_float) + scale_two * (
        d_normed_two - normed_two * jnp.mean(d_normed_two * normed_two, -1, keepdims=True)
    )
    grad_gain_ffn = jnp.sum(d_ffn_in * normed_two, 0)
    up_grad = dot(*after((d_both[:, total:], ring_in), d_ffn_in), contract_rows).astype(bf16)
    d_branch = group_gather(d_mid.astype(bf16), ep_index, (up_grad, down_grad))
    d_branch = d_branch.reshape(group_rows, model_width)
    d_attn = dot(d_branch, out_weight, contract_cols).astype(bf16)
    late_grads = [pair(after(grad, down_grad)) for grad in (gate_grad, up_grad)]
    late_grads = ring_exchange(pack_unit_grads(late_grads, units))
    d_attn = rows_to_heads(d_attn, dp_count, n, core, side, ep_index)
    grad_out_rows = dot(attn_rows, d_branch, contract_rows).astype(bf16)
    probs = jnp.exp(score_table() - log_total)
    d_probs = jnp.einsum("thd,khd->htk", d_attn, value, preferred_element_type=single_float)
    d_value = jnp.einsum("htk,thd->khd", probs_low, d_attn, preferred_element_type=single_float)
    d_scores = (probs * (d_probs - jnp.sum(probs * d_probs, -1, keepdims=True))).astype(bf16)
    d_query = head_scale * jnp.einsum(
        "htk,khd->thd", d_scores, key, preferred_element_type=single_float
    )
    d_key = head_scale * jnp.einsum(
        "htk,thd->khd", d_scores, query, preferred_element_type=single_float
    )
    d_pre = [rotate(d_query, table, -1.0), rotate(d_key, table, -1.0), d_value]
    d_pre = jnp.concatenate([d.reshape(group_rows, -1) for d in d_pre], 1).astype(bf16)
    d_attn_in = group_scatter(
        dot(d_pre, qkv_weight, contract_cols).reshape(4, tokens, model_width),
        ep_index,
    )
    grad_bias = jnp.sum(d_pre.astype(single_float), 0).reshape(3, 1, -1, 1, HD)
    grad_qkv = dot(attn_in, d_pre, contract_rows).astype(bf16)
    grad_qkv = grad_qkv.reshape(RING_SIZE, row_block, 3 * head_width)
    own_x = hidden_in.astype(single_float)
    scale_one = rms_scale(own_x)
    normed_one = own_x * scale_one
    grad_gain_attn = jnp.sum(d_attn_in * normed_one, 0)
    d_normed_one = d_attn_in * attention_gain
    input_grad = d_mid + scale_one * (
        d_normed_one - normed_one * jnp.mean(d_normed_one * normed_one, -1, keepdims=True)
    )

    grad_bias_full = jnp.zeros((3, 2, model_width // (4 * HD), 2, HD), single_float)
    grad_bias_full = lax.dynamic_update_slice(grad_bias_full, grad_bias, (0, core, 0, side, 0))
    small_grads = jnp.concatenate(
        [
            grad_gain_attn[None],
            grad_bias_full.reshape(3, model_width),
            grad_gain_ffn[None],
            grad_rows,
            jnp.zeros((2, model_width), single_float),
        ]
    )
    small_grads = small_grads.reshape(16, RING_SIZE, sets, 4, n).transpose(3, 1, 0, 2, 4)
    small_grads = group_scatter(
        small_grads.reshape(4, RING_SIZE, 16, sets * n), ep_index, single_float
    )
    small_grads = jnp.pad(small_grads, ((0, 0), (0, 0), (0, model_width - sets * n)))
    grad_rows = jnp.concatenate(
        [grad_out_rows.reshape(RING_SIZE, -1, model_width), small_grads.astype(bf16)], 1
    )

    def finished(grad, m):
        if sets == 1:
            shared, routed = unpack_unit_grads(grad, m, units)
            return shared, routed.transpose(1, 0, 2)
        grad = grad[:, m * UNIT_SETS * units : (m + 1) * UNIT_SETS * units]
        grad = set_scatter(grad, 2).reshape(RING_SIZE, UNIT_SETS, units, -1)
        grad = grad.transpose(3, 1, 0, 2).astype(single_float)
        grad = grad.reshape(grad.shape[0], UNIT_SETS, -1)
        return grad[:, 0], grad[:, 1:]

    down_out = finished(after(down_grad, grad_rows), 0)
    gate_out = finished(after(late_grads, grad_rows), 0)
    up_out = finished(after(late_grads, grad_rows), 1)
    grad_qkv, grad_rows = ring_scatter(
        [grad_qkv, grad_rows],
        place,
        [(late_grads,), (down_out,), (gate_out,), (up_out,)],
    )
    grad_out_w = set_scatter(grad_rows[:quarter], 0)
    small_grads = set_scatter(grad_rows[quarter:, : sets * n], 1)
    grad_qkv = set_scatter(grad_qkv, 0).astype(bf16)
    grad_qkv = group_exchange(grad_qkv.reshape(4, n, 3 * head_width), ep_index)
    grad_qkv = grad_qkv.reshape(2, 2, n, 3, -1, HD).transpose(3, 2, 1, 4, 0, 5)
    grad_qkv = grad_qkv.reshape(3, n, model_width).astype(single_float)
    unit_outs = [gate_out, up_out, down_out]
    return (
        output,
        input_grad,
        small_grads[0],
        grad_qkv[0],
        grad_qkv[1],
        grad_qkv[2],
        small_grads[1],
        small_grads[2],
        small_grads[3],
        grad_out_w,
        small_grads[4],
        small_grads[6:14].T,
        small_grads[5],
        unit_outs[0][0],
        unit_outs[1][0],
        unit_outs[2][0],
        unit_outs[0][1],
        unit_outs[1][1],
        unit_outs[2][1],
    )


def solution(mesh):
    rows, vector, split = P(AXES, None), P(AXES), P("dp", "ep")
    routed = P("dp", "ep", None)
    return jax.shard_map(
        body,
        mesh=mesh,
        in_specs=(
            (rows, vector, P("dp", None), P("dp", None), P(), vector)
            + (rows,) * 3
            + (vector,) * 3
            + (rows, vector, rows, vector)
            + (split,) * 3
            + (routed,) * 3
            + (rows,)
        ),
        out_specs=(
            (rows, rows, vector)
            + (rows,) * 3
            + (vector,) * 3
            + (rows, vector, rows, vector)
            + (split,) * 3
            + (routed,) * 3
        ),
        check_vma=False,
    )
```

```python
import jax
import jax.numpy as jnp
from jax import lax
from jax.experimental import pallas as pl
from jax.experimental.pallas import tpu as pltpu
from jax.sharding import PartitionSpec as P

HD = 128
TOPK = 4
EXP_DEV = 2
RING_SIZE = 8
UNIT_SETS = 1 + EXP_DEV
CORNER_ROWS = 64
UNIT_PAD = 64
TILE_ROWS = 64
ROW_SPLIT = 16
VMEM_BYTES = 60 * 1024 * 1024
SLOT_VMEM_BYTES = 36 * 1024 * 1024
AXES = ("dp", "ep")

RING = (0, 2, 4, 6, 7, 5, 3, 1)
PLACE = tuple(RING.index(j) for j in range(RING_SIZE))

epsilon = 1e-06
rotary_base = 1000000.0
masked_score = -1e30
contract_rows = (((0,), (0,)), ((), ()))
contract_cols = (((1,), (1,)), ((), ()))
single_float = jnp.float32
bf16 = jnp.bfloat16


def dot(left, right, dims=(((1,), (0,)), ((), ()))):
    return lax.dot_general(left, right, dims, preferred_element_type=single_float)


def after(value, *events):
    return lax.optimization_barrier((value, events))[0] if events else value


def move(block, where):
    sets = lax.axis_size("dp") // RING_SIZE
    ranks = lax.axis_size("ep")
    pairs = []
    for j in range(RING_SIZE):
        for e in range(ranks):
            to = where(j, e)
            if to is None:
                continue
            for s in range(sets):
                pairs.append(((j * sets + s) * ranks + e, (to[0] * sets + s) * ranks + to[1]))
    return lax.ppermute(block, AXES, pairs)


def around(j, hops):
    return RING[(PLACE[j] + hops) % RING_SIZE]


def to_core(block):
    return move(block, lambda j, e: (j, e ^ 1))


def to_side(block):
    return move(block, lambda j, e: (j, e ^ 2))


def out_hop(block):
    return move(block, lambda j, e: (around(j, 1 if e % 2 else -1), e))


def back_hop(block):
    return move(block, lambda j, e: (around(j, -1 if e % 2 else 1), e))


def ring_up(block):
    return move(block, lambda j, e: (around(j, 1), e))


def ring_down(block):
    return move(block, lambda j, e: (around(j, -1), e))


def in_set(sets):
    return [[j * sets + s for s in range(sets)] for j in range(RING_SIZE)]


def set_gather(block, axis):
    sets = lax.axis_size("dp") // RING_SIZE
    if sets == 1:
        return block
    return lax.all_gather(block, "dp", axis_index_groups=in_set(sets), axis=axis, tiled=True)


def set_scatter(block, axis):
    sets = lax.axis_size("dp") // RING_SIZE
    if sets == 1:
        return block
    return lax.psum_scatter(
        block, "dp", scatter_dimension=axis, axis_index_groups=in_set(sets), tiled=True
    )


def group_gather(block, ep_index, before_last=()):
    near = to_core(block)
    far = after(to_side(block), *before_last)
    parts = [block, near, far, to_core(far)]
    whole = jnp.zeros((4,) + block.shape, block.dtype)
    for m, part in enumerate(parts):
        whole = lax.dynamic_update_index_in_dim(whole, part, ep_index ^ m, 0)
    return whole


def group_scatter(parts, ep_index, link=bf16, before_last=()):
    part = [lax.dynamic_index_in_dim(parts, ep_index ^ m, 0, False) for m in range(4)]
    got = to_core(jnp.stack([part[1], part[3]]).astype(link)).astype(single_float)
    near = part[0].astype(single_float) + got[0]
    far = part[2].astype(single_float) + got[1]
    far = after(far.astype(link), *before_last)
    return near + to_side(far).astype(single_float)


def group_exchange(blocks, ep_index):
    whole = jnp.zeros_like(blocks)
    for m in range(4):
        block = lax.dynamic_index_in_dim(blocks, ep_index ^ m, 0, False)
        if m:
            block = move(block, lambda j, e, m=m: (j, e ^ m))
        whole = lax.dynamic_update_index_in_dim(whole, block, ep_index ^ m, 0)
    return whole


def ring_position(place):
    return jnp.where(place % 2 == 1, RING_SIZE - 1 - place // 2, place // 2)


def place_at(position):
    position = position % RING_SIZE
    return jnp.where(position < 4, 2 * position, 2 * (RING_SIZE - 1 - position) + 1)


def ring_pieces(blocks, place, arrived):
    position = ring_position(place)
    up = down = blocks
    events = arrived(0, [(place, blocks)])
    for k in range(1, 4):
        up, down = after((up, down), *events)
        up, down = [ring_up(block) for block in up], [ring_down(block) for block in down]
        events = arrived(k, [(place_at(position - k), up), (place_at(position + k), down)])
    up, down = after((up, down), *events)
    last = []
    for first, second in zip(up, down):
        half = first.shape[0] // 32 * 16
        last.append(jnp.concatenate([ring_up(first[:half]), ring_down(second[half:])]))
    arrived(4, [(place_at(position + 4), last)])


def ring_scatter(every, place, events=()):
    position = ring_position(place)
    events = dict(enumerate(events))

    def part(hops):
        where = place_at(position + hops)
        return [wide(lax.dynamic_index_in_dim(parts, where, 0, False)) for parts in every]

    def hop(up, down, k):
        up, down = after(([low(x) for x in up], [low(x) for x in down]), *events.get(k, ()))
        return [wide(ring_up(x)) for x in up], [wide(ring_down(x)) for x in down]

    opposite = part(4)
    cuts = [x.shape[0] // 32 * 16 for x in opposite]
    up, down = hop(
        [x[:cut] for x, cut in zip(opposite, cuts)], [x[cut:] for x, cut in zip(opposite, cuts)], 0
    )
    up = [jnp.pad(x, ((0, y.shape[0] - x.shape[0]), (0, 0))) for x, y in zip(up, opposite)]
    down = [jnp.pad(x, ((y.shape[0] - x.shape[0], 0), (0, 0))) for x, y in zip(down, opposite)]
    for k in (3, 2, 1):
        up = [x + y for x, y in zip(part(k), up)]
        down = [x + y for x, y in zip(part(-k), down)]
        up, down = hop(up, down, 4 - k)
    return [x + y + z for x, y, z in zip(part(0), up, down)]


def ring_exchange(blocks):
    sets = lax.axis_size("dp") // RING_SIZE
    groups = [[j * sets + s for j in range(RING_SIZE)] for s in range(sets)]
    return lax.all_to_all(blocks, "dp", 0, 0, axis_index_groups=groups if sets > 1 else None)


def half_block(block):
    n, tail = CORNER_ROWS, (block.shape[0] - 4 * CORNER_ROWS) // 2
    return jnp.concatenate([block[:n], block[2 * n : 3 * n], block[4 * n : 4 * n + tail]])


def other_half(block):
    n, tail = CORNER_ROWS, (block.shape[0] - 4 * CORNER_ROWS) // 2
    return jnp.concatenate([block[n : 2 * n], block[3 * n : 4 * n], block[4 * n + tail :]])


def spread_half(half):
    n, tail = CORNER_ROWS, half.shape[0] - 2 * CORNER_ROWS
    rows = 4 * n + 2 * tail
    place = lambda first, last, at: jnp.pad(
        half[first:last], ((at, rows - at - (last - first)), (0, 0))
    )
    return place(0, n, 0) + place(n, 2 * n, 2 * n) + place(2 * n, 2 * n + tail, 4 * n)


def gather_start(block):
    head, tail = block[:CORNER_ROWS], block[CORNER_ROWS:]
    far = to_side(head)
    ring = jnp.concatenate([head, to_core(head), far, to_core(far), tail, to_core(tail)])
    return ring, (jnp.concatenate([head, far, tail]), to_side(tail))


def with_side(block, heads):
    return block, to_side(block[heads:])


def scatter_parts(parts):
    count = len(parts) // 2
    out = []
    for block, side in zip(parts[:count], parts[count:]):
        side = jnp.pad(to_side(side), ((block.shape[0] - side.shape[0], 0), (0, 0)))
        out.append(block.astype(single_float) + side.astype(single_float))
    return out


def scatter_end(total, own):
    n = CORNER_ROWS
    got = to_core(other_half(total).astype(bf16)).astype(single_float)
    total = half_block(total) + own + got
    far = to_side(total[n : 2 * n].astype(bf16)).astype(single_float)
    return jnp.concatenate([total[:n] + far, total[2 * n :]])


def low(value):
    return value.astype(bf16)


def wide(value):
    return value.astype(single_float)


def rms_scale(values):
    return lax.rsqrt(jnp.mean(values * values, -1, keepdims=True) + epsilon)


def rotary_table(positions):
    inverse = 1.0 / rotary_base ** (jnp.arange(0, HD, 2, dtype=single_float) / HD)
    angles = positions.astype(single_float)[:, None] * inverse[None, :]
    cosine, sine = jnp.cos(angles), jnp.sin(angles)
    return (
        jnp.concatenate([cosine, cosine], -1)[:, None, :],
        jnp.concatenate([-sine, sine], -1)[:, None, :],
    )


def rotate(values, table, direction):
    heads = values.reshape(values.shape[0], -1, HD)
    swapped = jnp.concatenate([heads[..., HD // 2 :], heads[..., : HD // 2]], -1)
    return heads * table[0] + swapped * (direction * table[1])


def kept_pairs(expert_ids, priority, capacity, ep_index, tokens):
    experts = capacity.shape[0]
    order = priority.reshape(-1, TOPK)
    own_experts = lax.dynamic_slice_in_dim(expert_ids, ep_index * tokens, tokens, 0)
    own_order = lax.dynamic_slice_in_dim(order, ep_index * tokens, tokens, 0)
    all_experts = expert_ids.reshape(1, -1)
    all_order = priority.reshape(1, -1)
    labels = jnp.arange(experts, dtype=jnp.int32)[None, :]
    kept = jnp.zeros((tokens, experts), bool)
    for k in range(TOPK):
        expert = own_experts[:, k : k + 1]
        ahead = (all_experts == expert) & (all_order < own_order[:, k : k + 1])
        slot = jnp.sum(ahead.astype(jnp.int32), 1, keepdims=True)
        kept = kept | ((labels == expert) & (slot < capacity[None, :]))
    return kept


def own_heads(features, core, side):
    lead = features.shape[:-1]
    split = features.reshape(lead + (2, -1, 2, HD))
    axis = len(lead)
    split = lax.dynamic_index_in_dim(split, core, axis, False)
    split = lax.dynamic_index_in_dim(split, side, axis + 1, False)
    return split.reshape(lead + (-1,))


def heads_to_rows(heads, dp_count, n, core, side, ep_index):
    rows = heads.shape[0]
    if 2 * n == HD:
        low, high = heads[..., :n], heads[..., n:]
        keep = jnp.where(core == 0, low, high).reshape(rows, -1)
        got = to_core(jnp.where(core == 0, high, low).reshape(rows, -1))
        return jnp.where(
            core == 0, jnp.concatenate([keep, got], 1), jnp.concatenate([got, keep], 1)
        )
    every = lax.all_gather(heads, "ep", axis=0)
    every = every.reshape((2, 2) + heads.shape).transpose(2, 1, 3, 0, 4)
    every = every.reshape(rows, dp_count, 4, n)
    return lax.dynamic_index_in_dim(every, ep_index, 2, False).reshape(rows, -1)


def rows_to_heads(features, dp_count, n, core, side, ep_index):
    rows = features.shape[0]
    if 2 * n == HD:
        half = features.shape[1] // 2
        low, high = features[:, :half], features[:, half:]
        keep = jnp.where(core == 0, low, high).reshape(rows, -1, n)
        got = to_core(jnp.where(core == 0, high, low)).reshape(rows, -1, n)
        return jnp.where(
            core == 0, jnp.concatenate([keep, got], -1), jnp.concatenate([got, keep], -1)
        )
    every = lax.all_gather(features, "ep", axis=0).reshape(4, rows, dp_count, n)
    every = every.transpose(1, 2, 0, 3).reshape(rows, -1)
    return own_heads(every, core, side).reshape(rows, -1, HD)


def cost(flops, bytes_accessed):
    return pl.CostEstimate(flops=int(flops), bytes_accessed=int(bytes_accessed), transcendentals=0)


def params(grid_rank, vmem=VMEM_BYTES):
    return pltpu.CompilerParams(
        dimension_semantics=("arbitrary",) * grid_rank, vmem_limit_bytes=vmem
    )


def padded(units):
    return -(-units // UNIT_PAD) * UNIT_PAD


def lay_out_units(blocks, offsets, step):
    count, _, rows = blocks[0].shape
    wide_step = padded(step)

    def kernel(*refs):
        whole = refs[-1]
        for owner, part in enumerate(refs[:-1]):
            for j in range(count):
                whole[owner, :step, j * rows : (j + 1) * rows] = part[j]
            if wide_step > step:
                whole[owner, step:, :] = jnp.zeros((wide_step - step, count * rows), bf16)

    half = UNIT_SETS * wide_step
    weights = pl.pallas_call(
        kernel,
        grid=(UNIT_SETS,),
        in_specs=[
            pl.BlockSpec((count, step, rows), lambda i, first=first: (0, first + i, 0))
            for first in offsets
        ],
        out_specs=pl.BlockSpec((len(blocks), wide_step, count * rows), lambda i: (0, i, 0)),
        out_shape=jax.ShapeDtypeStruct((len(blocks), half, count * rows), bf16),
        compiler_params=params(1),
        cost_estimate=cost(0, 4 * len(blocks) * half * count * rows),
        name="lay_out_units",
    )(*blocks)
    return weights.reshape(len(blocks) * half, count * rows)


def routing(logits, kept, experts):
    lane = lax.broadcasted_iota(jnp.int32, logits.shape, 1)
    expert_lane = (lane >= 1) & (lane <= experts)
    top = jnp.max(jnp.where(expert_lane, logits, masked_score), 1, keepdims=True)
    weight = jnp.exp(jnp.where(expert_lane, logits - top, masked_score))
    router = weight / jnp.sum(weight, 1, keepdims=True)
    return lane, jax.nn.sigmoid(logits), router, kept.astype(single_float)


def high_low(value):
    high = value.astype(bf16)
    return high, (value - high.astype(single_float)).astype(bf16)


def unit_factor(lane, share, router, kept, spread_ref, total):
    high, rest = high_low(jnp.where(lane == 0, share, router * kept))
    spread = spread_ref[:, :total]
    return dot(high, spread) + dot(rest, spread)


def by_tiles(rows, total, work):
    def chunk(i, carry):
        here = pl.ds(pl.multiple_of(i * TILE_ROWS, TILE_ROWS), TILE_ROWS)
        for first in range(0, total, HD):
            work(here, first)
        return carry

    lax.fori_loop(0, rows // TILE_ROWS, chunk, 0)


def slot_specs(slot, width, lanes=None):
    if lanes is None:
        return [pl.BlockSpec((part.shape[0], width), lambda *_: (0, 0)) for part in slot]
    return [pl.BlockSpec((part.shape[0], HD), lambda *_: (0, width // HD)) for part in slot]


def slot_shapes(slot, width):
    return [jax.ShapeDtypeStruct((part.shape[0], width), bf16) for part in slot]


def split_rows(refs, value):
    start = 0
    for ref in refs:
        ref[...] = value[start : start + ref.shape[0]]
        start += ref.shape[0]


def slot_call(kernel, slot, index, inputs, in_specs, kept, shapes, specs, scratch, flops, name):
    step = sum(part.shape[0] for part in slot)
    arrays = list(kept) if isinstance(kept[0], jax.Array) else []
    kept_shapes = [jax.ShapeDtypeStruct(k.shape, k.dtype) for k in kept]
    kept_specs = [pl.BlockSpec((step, k.shape[1]), lambda *_: (index, 0)) for k in kept]
    return pl.pallas_call(
        kernel,
        grid=(1,),
        in_specs=in_specs + [pl.BlockSpec(memory_space=pl.ANY)] * len(arrays),
        out_specs=kept_specs + specs,
        out_shape=kept_shapes + shapes,
        scratch_shapes=scratch,
        input_output_aliases={len(inputs) + i: i for i in range(len(arrays))},
        compiler_params=params(1, SLOT_VMEM_BYTES),
        cost_estimate=cost(flops, flops // 100),
        name=name,
    )(*inputs, *arrays)


def ffn_forward(slot, index, gate_up, down, rows, spread, experts, kept):
    total, width = down.shape
    step = sum(part.shape[0] for part in slot)
    known = len(kept) if isinstance(kept[0], jax.Array) else 0

    def kernel(*refs):
        count = len(slot)
        parts, lanes, refs = refs[:count], refs[count : 2 * count], refs[2 * count :]
        (gate_up_w, down_w, rows_ref, spread_ref), refs = refs[:4], refs[4 + known :]
        (x_all, scaled), out = refs[:2], refs[2 : 2 + count]
        low_ref, act, rest, logit, both, factor = refs[2 + count :]
        x = jnp.concatenate([part[...] for part in parts], 0)
        x_all[...] = x
        logits = dot(x, rows_ref[...], contract_cols)
        logit[...] = logits
        kept_lanes = jnp.concatenate([part[...] for part in lanes], 0)
        lane, share, router, kept_now = routing(logits, kept_lanes, experts)
        factor[...] = unit_factor(lane, share, router, kept_now, spread_ref, total)
        both[...] = dot(x, gate_up_w[...], contract_cols)

        def work(here, first):
            tile = here, pl.ds(first, HD)
            gate, up = both[tile], both[here, pl.ds(total + first, HD)]
            logistic = jax.nn.sigmoid(gate)
            active = gate * logistic
            act[tile] = active.astype(bf16)
            rest[tile] = (up * (logistic + active * (1.0 - logistic))).astype(bf16)
            hidden = (active * up).astype(bf16)
            low_ref[tile] = hidden
            scaled[tile] = (factor[tile] * hidden.astype(single_float)).astype(bf16)

        by_tiles(step, total, work)
        split_rows(out, dot(scaled[...], down_w[...]).astype(bf16))

    whole = lambda *_: (0, 0)
    resident = pl.BlockSpec(memory_space=pltpu.VMEM)
    unit_block = pl.BlockSpec((step, total), whole)
    return slot_call(
        kernel,
        slot,
        index,
        [*slot, *slot, gate_up, down, rows, spread],
        slot_specs(slot, width) + slot_specs(slot, width, HD) + [resident] * 4,
        kept,
        slot_shapes(slot, width)
        + [jax.ShapeDtypeStruct((step, total), bf16)] * 3
        + [jax.ShapeDtypeStruct((step, HD), single_float)],
        slot_specs(slot, width) + [unit_block] * 3 + [pl.BlockSpec((step, HD), whole)],
        [pltpu.VMEM((step, 2 * total), single_float), pltpu.VMEM((step, total), single_float)],
        6 * step * width * total,
        "ffn_forward",
    )


def ffn_backward(slot, index, grads, gate_up, down, rows, spread, saved, experts, kept):
    total, width = down.shape
    step = sum(part.shape[0] for part in slot)
    known = len(kept) if isinstance(kept[0], jax.Array) else 0

    def kernel(*refs):
        count = len(slot)
        parts, lanes, refs = refs[:count], refs[count : 2 * count], refs[2 * count :]
        (gate_up_w, down_w, rows_ref, spread_ref), refs = refs[:4], refs[4:]
        (low_ref, act, rest, logit), refs = refs[:4], refs[4 + known :]
        (grad_all, gate_all, up_all, row_all), out = refs[:4], refs[4 : 4 + count]
        d_hidden, factor, products, d_both = refs[4 + count :]
        grad = jnp.concatenate([part[...] for part in parts], 0)
        grad_all[...] = grad
        kept_lanes = jnp.concatenate([part[...] for part in lanes], 0)
        lane, share, router, kept_now = routing(logit[...], kept_lanes, experts)
        factor[...] = unit_factor(lane, share, router, kept_now, spread_ref, total)
        d_hidden[...] = dot(grad, down_w[...], contract_cols)

        def work(here, first):
            tile, other = (here, pl.ds(first, HD)), (here, pl.ds(total + first, HD))
            d_unit = d_hidden[tile]
            high, remains = high_low(d_unit * low_ref[tile].astype(single_float))
            products[tile] = high
            products[other] = remains
            d_unit = d_unit * factor[tile]
            d_gate = (d_unit * rest[tile].astype(single_float)).astype(bf16)
            d_up = (d_unit * act[tile].astype(single_float)).astype(bf16)
            gate_all[tile] = d_gate
            up_all[tile] = d_up
            d_both[tile] = d_gate
            d_both[other] = d_up

        by_tiles(step, total, work)
        sums = dot(products[...], spread_ref[...], contract_cols)
        d_router = sums * kept_now
        d_logits = router * (d_router - jnp.sum(router * d_router, 1, keepdims=True))
        d_rows = jnp.where(lane == 0, sums * share * (1.0 - share), d_logits)
        high = d_rows.astype(bf16).astype(single_float)
        remains = pltpu.roll(d_rows - high, ROW_SPLIT, 1)
        rows_both = jnp.where(lane < ROW_SPLIT, high, remains).astype(bf16)
        row_all[...] = rows_both
        d_ring = dot(d_both[...], gate_up_w[...]) + dot(rows_both, rows_ref[...])
        split_rows(out, d_ring.astype(bf16))

    whole = lambda *_: (0, 0)
    resident = pl.BlockSpec(memory_space=pltpu.VMEM)
    unit_block = pl.BlockSpec((step, total), whole)
    return slot_call(
        kernel,
        grads,
        index,
        [*grads, *slot, gate_up, down, rows, spread, *saved],
        slot_specs(grads, width)
        + slot_specs(slot, width, HD)
        + [resident] * 4
        + [unit_block] * 3
        + [pl.BlockSpec((step, HD), whole)],
        kept,
        slot_shapes(grads, width),
        slot_specs(grads, width),
        [
            pltpu.VMEM((step, total), single_float),
            pltpu.VMEM((step, total), single_float),
            pltpu.VMEM((step, 2 * total), bf16),
            pltpu.VMEM((step, 2 * total), bf16),
        ],
        6 * step * width * total,
        "ffn_backward",
    )


def pack_unit_grads(pairs, units):
    width = pairs[0][0].shape[1]
    rows, wide_step = width // RING_SIZE, padded(units)
    steps = len(pairs) * UNIT_SETS

    def kernel(*refs):
        out = refs[-1]
        for p in range(len(pairs)):
            own, got = refs[2 * p : 2 * p + 2]

            @pl.when(pl.program_id(0) // UNIT_SETS == p)
            def _():
                for j in range(RING_SIZE):
                    part = (slice(0, units), slice(j * rows, (j + 1) * rows))
                    total = own[part].astype(single_float) + got[part].astype(single_float)
                    out[j] = total.astype(bf16)

    def block(p):
        return pl.BlockSpec(
            (wide_step, width), lambda i: (jnp.clip(i - p * UNIT_SETS, 0, UNIT_SETS - 1), 0)
        )

    return pl.pallas_call(
        kernel,
        grid=(steps,),
        in_specs=[block(p) for p in range(len(pairs)) for _ in range(2)],
        out_specs=pl.BlockSpec((RING_SIZE, units, rows), lambda i: (0, i, 0)),
        out_shape=jax.ShapeDtypeStruct((RING_SIZE, steps * units, rows), bf16),
        compiler_params=params(1),
        cost_estimate=cost(0, 6 * steps * units * width),
        name="pack_unit_grads",
    )(*[array for pair in pairs for array in pair])


def unpack_unit_grads(blocks, matrix, units):
    rows = blocks.shape[2]
    half = UNIT_SETS * units
    width = units * RING_SIZE

    def kernel(part, shared, routed, joined):
        for s in range(1 + EXP_DEV):
            for j in range(RING_SIZE):
                joined[j * units : (j + 1) * units, :] = part[j, s * units : (s + 1) * units, :]
            turned = joined[...].astype(single_float).T
            if s == 0:
                shared[...] = turned
            else:
                routed[s - 1] = turned

    return pl.pallas_call(
        kernel,
        grid=(1,),
        in_specs=[pl.BlockSpec((RING_SIZE, half, rows), lambda i: (0, matrix, 0))],
        out_specs=[
            pl.BlockSpec((rows, width), lambda i: (0, 0)),
            pl.BlockSpec((EXP_DEV, rows, width), lambda i: (0, 0, 0)),
        ],
        scratch_shapes=[pltpu.VMEM((width, rows), bf16)],
        out_shape=[
            jax.ShapeDtypeStruct((rows, width), single_float),
            jax.ShapeDtypeStruct((EXP_DEV, rows, width), single_float),
        ],
        compiler_params=params(1),
        cost_estimate=cost(0, 18 * rows * width),
        name="unpack_unit_grads",
    )(blocks)


def body(
    hidden_in,
    segment_ids,
    expert_ids,
    priority,
    capacity,
    norm_attn,
    w_query,
    w_key,
    w_value,
    bias_query,
    bias_key,
    bias_value,
    w_out,
    norm_ffn,
    w_router,
    w_shared_gate,
    shared_gate_proj,
    shared_up_proj,
    shared_down_proj,
    expert_gate_proj,
    expert_up_proj,
    expert_down_proj,
    out_grad,
):
    tokens, model_width = hidden_in.shape
    group_rows = 4 * tokens
    head_scale = HD ** (-0.5)
    dp_count = lax.axis_size("dp")
    sets = dp_count // RING_SIZE
    place = lax.axis_index("dp") // sets
    ep_index = lax.axis_index("ep")
    core, side = ep_index % 2, ep_index // 2
    n = norm_attn.shape[0]
    experts = capacity.shape[0]

    group_x = group_gather(hidden_in, ep_index).reshape(group_rows, model_width)
    segments = group_gather(segment_ids.reshape(1, tokens), ep_index).reshape(group_rows)
    group_index = jnp.arange(group_rows, dtype=jnp.int32)
    first = segments == segments[0]
    first_count = jnp.sum(first.astype(jnp.int32))
    positions = jnp.where(first, group_index, group_index - first_count)
    valid = (segments[:, None] == segments[None, :]) & (
        group_index[None, :] <= group_index[:, None]
    )
    table = rotary_table(positions)

    row_block = model_width // RING_SIZE
    units = expert_gate_proj.shape[2] // RING_SIZE
    half_units = (1 + EXP_DEV) * padded(units)

    def unit_slices(shared, routed):
        every = jnp.concatenate([shared[:, None, :], routed], 1)
        every = every.reshape(every.shape[0], 1 + EXP_DEV, RING_SIZE, -1)
        every = set_gather(every.transpose(2, 1, 3, 0), 3)
        return every.reshape(RING_SIZE, -1, row_block)

    gate_units = ring_exchange(unit_slices(shared_gate_proj, expert_gate_proj))

    def head_columns(weight):
        split = weight.reshape(n, 2, -1, 2, HD).transpose(3, 1, 0, 2, 4)
        return split.reshape(4, n, -1)

    small = jnp.concatenate(
        [
            jnp.stack([norm_attn, bias_query, bias_key, bias_value, norm_ffn, w_shared_gate]),
            w_router.T,
            jnp.zeros((2, n), bf16),
        ]
    )
    qkv = jnp.concatenate([head_columns(w) for w in (w_query, w_key, w_value)], -1)
    head_width = qkv.shape[-1] // 3
    quarter = row_block // 4
    small = jnp.pad(small, ((0, 0), (0, 3 * head_width - n)))
    qkv = jnp.concatenate([qkv, jnp.broadcast_to(small, (4,) + small.shape)], 1)
    qkv = group_exchange(qkv, ep_index)
    small = set_gather(qkv[:, n:, :n].transpose(1, 0, 2).reshape(16, 4 * n), 1)
    small = jnp.pad(small, ((0, 0), (0, 3 * head_width - row_block)))
    qkv = set_gather(qkv[:, :n].reshape(4 * n, -1), 0)
    gathered = [
        jnp.zeros((RING_SIZE, row_block, 3 * head_width), bf16),
        jnp.zeros((RING_SIZE, quarter, model_width), bf16),
        jnp.zeros((RING_SIZE, 16, row_block), bf16),
    ]
    later_units = []

    def arrived(k, pieces):
        for where, (dense, rows) in pieces:
            found = dense[:row_block], rows, dense[row_block:, :row_block]
            for i in range(3):
                gathered[i] = lax.dynamic_update_index_in_dim(gathered[i], found[i], where, 0)
        if k in (0, 4):
            return ()
        if k < 3:
            halves = ((shared_up_proj, expert_up_proj), (shared_down_proj, expert_down_proj))[k - 1]
            later_units.append(unit_slices(*after(halves, pieces[0][1][0])))
        return (gate_units,) if k == 1 else (later_units[k - 2],)

    ring_pieces([jnp.concatenate([qkv, small]), set_gather(w_out, 0)], place, arrived)
    qkv_weight = gathered[0].reshape(model_width, -1)
    out_weight = gathered[1].reshape(-1, model_width)
    small = gathered[2].transpose(1, 0, 2).reshape(16, model_width)
    attention_gain = small[0].astype(single_float)
    feedforward_gain = small[4].astype(single_float)
    gate_rows = small[5:14]
    gate_rows = jnp.pad(gate_rows, ((0, ROW_SPLIT - gate_rows.shape[0]), (0, 0)))
    gate_rows = jnp.pad(
        jnp.concatenate([gate_rows, gate_rows]), ((0, HD - 2 * ROW_SPLIT), (0, 0))
    )
    head_bias = own_heads(small[1:4], core, side).astype(single_float)
    late_units = ring_exchange(after(jnp.concatenate(later_units, 1), gathered[0]))

    gate_other = to_core(after(gate_units, gathered[0]))

    kept_own = kept_pairs(expert_ids, priority, capacity, ep_index, tokens)
    kept_own = jnp.pad(kept_own.astype(bf16), ((0, 0), (1, HD - 1 - experts)))

    x_float = group_x.astype(single_float)
    attn_in = (x_float * rms_scale(x_float) * attention_gain).astype(bf16)
    pre = dot(attn_in, qkv_weight)
    query = rotate(pre[:, :head_width] + head_bias[0], table, 1.0).astype(bf16)
    key = rotate(pre[:, head_width : 2 * head_width] + head_bias[1], table, 1.0).astype(bf16)
    value = (pre[:, 2 * head_width :] + head_bias[2]).astype(bf16).reshape(group_rows, -1, HD)

    def score_table():
        raw = jnp.einsum("thd,khd->htk", query, key, preferred_element_type=single_float)
        return jnp.where(valid[None], raw * head_scale, masked_score)

    scores = score_table()
    top_score = jnp.max(scores, -1, keepdims=True)
    exps = jnp.exp(scores - top_score)
    totals = jnp.sum(exps, -1, keepdims=True)
    log_total = top_score + jnp.log(totals)
    probs_low = (exps / totals).astype(bf16)
    attn = jnp.einsum("htk,khd->thd", probs_low, value, preferred_element_type=single_float)
    attn_rows = heads_to_rows(attn.astype(bf16), dp_count, n, core, side, ep_index)
    mid = hidden_in.astype(single_float) + group_scatter(
        dot(attn_rows, out_weight).reshape(4, tokens, model_width),
        ep_index,
        before_last=(gate_other,),
    )
    scale_two = rms_scale(mid)
    normed_two = mid * scale_two
    ffn_in = (normed_two * feedforward_gain).astype(bf16)

    class Walk:
        def __init__(self, block):
            self.block, self.own = gather_start(block)
            self.sides = []

        def hop(self, k, *events):
            events = (*events, *self.sides[:-1])
            if k:
                self.block = out_hop(after(self.block, *events))
                slot = with_side(self.block, 4 * CORNER_ROWS)
                self.sides = self.sides[-1:] + [slot[1]]
                return slot
            self.block = out_hop(after(half_block(self.block), *events))
            far = with_side(self.block, 2 * CORNER_ROWS)
            return self.own[0], far[0], self.own[1], far[1]

    held = [EXP_DEV * (ep_index ^ flip) + i for flip in (0, 1) for i in range(EXP_DEV)]
    lanes = [0] + [1 + e for e in held[:EXP_DEV]] + [0] + [1 + e for e in held[EXP_DEV:]]
    lanes = jnp.repeat(jnp.stack([jnp.asarray(lane, jnp.int32) for lane in lanes]), padded(units))
    spread = (jnp.arange(HD, dtype=jnp.int32)[:, None] == lanes[None, :]).astype(bf16)
    spread = jnp.concatenate([spread, spread], 1)
    total = 2 * half_units
    all_rows = 4 * group_rows
    shape = lambda lanes: jax.ShapeDtypeStruct((all_rows, lanes), bf16)
    kept = [shape(model_width), shape(total)]
    ring_slots, grad_slots, results = [None] * 4, [None] * 4, [None] * 4

    def forward(k, kept, *events):
        found = ffn_forward(
            after(ring_slots[k], *events), k, gate_up, down, gate_rows, spread, experts, kept
        )
        count = len(ring_slots[k])
        results[k] = found[2 : 2 + count], found[2 + count :]
        return found[:2]

    def backward(k, kept, *events):
        found = ffn_backward(
            ring_slots[k],
            k,
            after(grad_slots[k], *events),
            gate_up,
            down,
            gate_rows,
            spread,
            results[k][1],
            experts,
            kept,
        )
        return found[:4], scatter_parts(found[4:])

    late_other = to_core(late_units)
    walk = Walk(jnp.concatenate([ffn_in, kept_own], 1))
    ring_slots[1] = walk.hop(1)
    gate_up = lay_out_units([gate_units, gate_other, late_units, late_other], [0] * 4, units)
    ring_slots[2] = walk.hop(2, gate_up)
    down = lay_out_units(
        after([late_units, late_other], ring_slots[1][0]), [UNIT_SETS, UNIT_SETS], units
    )
    ring_slots[3] = walk.hop(3, down)
    kept = forward(1, kept, ring_slots[2][0])
    grad_walk = Walk(after(out_grad, ring_slots[2][0]))
    ring_slots[0] = walk.hop(0, *kept)
    kept = forward(2, kept, ring_slots[3][0])
    grad_slots[1] = grad_walk.hop(1, walk.block, ring_slots[3][1], *kept)
    kept = forward(3, kept, walk.block)
    grad_slots[2] = grad_walk.hop(2, *ring_slots[0][2:], *kept)
    kept = forward(0, kept, grad_slots[1][0])
    grad_slots[3] = grad_walk.hop(3, *kept)
    ring_in, scaled_hidden = kept
    out_own, out_far = scatter_parts(after(results[0][0], grad_slots[2][0]))
    (out_slot,) = scatter_parts(after(results[3][0], grad_slots[2][0]))
    grad_slots[0] = grad_walk.hop(0, out_far, out_slot)

    def back(block, *events):
        return wide(back_hop(after(low(block), *events)))

    out = back(out_far, grad_slots[3][0])
    kept = [shape(model_width), shape(total), shape(total), shape(HD)]
    kept, (d_slot_3,) = backward(3, kept, grad_slots[3][0])
    (out_slot_2,) = scatter_parts(after(results[2][0], out))
    out = back(spread_half(out) + out_slot, kept[3])
    kept, (d_own, d_far) = backward(0, kept, kept[3])
    (out_slot_1,) = scatter_parts(after(results[1][0], kept[3]))
    out = back(out + out_slot_2, kept[3])
    kept, (d_slot_2,) = backward(2, kept, kept[3])
    d_ring = back(d_far, kept[3])
    out = back(out + out_slot_1, kept[3])
    kept, (d_slot_1,) = backward(1, kept, kept[3])
    ring_grad, d_gate, d_up, d_rows = kept
    down_grad = dot(
        *after((scaled_hidden, ring_grad), d_ring, d_rows), contract_rows
    ).astype(bf16)
    d_ring = back(spread_half(d_ring) + d_slot_3, d_rows)

    def pair(grad):
        return grad, to_core(grad[half_units:])

    down_pair = pair(down_grad)
    gate_grad = dot(*after((d_gate, ring_in), d_ring, down_grad), contract_rows).astype(bf16)
    d_ring = back(d_ring + d_slot_2, down_grad)
    down_grad = pack_unit_grads([after(down_pair, gate_grad)], units)
    up_grad = dot(*after((d_up, ring_in), d_ring, down_grad), contract_rows).astype(bf16)
    d_ring = back(d_ring + d_slot_1, down_grad, out)
    down_grad = ring_exchange(down_grad)
    d_ffn_in = scatter_end(after(d_ring, up_grad), d_own)
    grad_rows = dot(d_rows, ring_in, contract_rows)
    grad_rows = grad_rows[: 1 + experts] + grad_rows[ROW_SPLIT : ROW_SPLIT + 1 + experts]

    d_normed_two = d_ffn_in * feedforward_gain
    d_mid = out_grad.astype(single_float) + scale_two * (
        d_normed_two - normed_two * jnp.mean(d_normed_two * normed_two, -1, keepdims=True)
    )
    grad_gain_ffn = jnp.sum(d_ffn_in * normed_two, 0)
    late_grads = [pair(after(grad, d_ffn_in)) for grad in (gate_grad, up_grad)]
    late_grads = pack_unit_grads(late_grads, units)
    d_branch = group_gather(d_mid.astype(bf16), ep_index, (late_grads, down_grad))
    d_branch = d_branch.reshape(group_rows, model_width)
    late_grads = ring_exchange(after(late_grads, down_grad))
    d_attn = dot(d_branch, out_weight, contract_cols).astype(bf16)
    d_attn = rows_to_heads(d_attn, dp_count, n, core, side, ep_index)
    output = (mid + scatter_end(after(out, d_attn), out_own)).astype(bf16)
    grad_out_rows = dot(attn_rows, d_branch, contract_rows).astype(bf16)
    probs = jnp.exp(score_table() - log_total)
    d_probs = jnp.einsum("thd,khd->htk", d_attn, value, preferred_element_type=single_float)
    d_value = jnp.einsum("htk,thd->khd", probs_low, d_attn, preferred_element_type=single_float)
    d_scores = (probs * (d_probs - jnp.sum(probs * d_probs, -1, keepdims=True))).astype(bf16)
    d_query = head_scale * jnp.einsum(
        "htk,khd->thd", d_scores, key, preferred_element_type=single_float
    )
    d_key = head_scale * jnp.einsum(
        "htk,thd->khd", d_scores, query, preferred_element_type=single_float
    )
    d_pre = [rotate(d_query, table, -1.0), rotate(d_key, table, -1.0), d_value]
    d_pre = jnp.concatenate([d.reshape(group_rows, -1) for d in d_pre], 1).astype(bf16)
    d_attn_in = group_scatter(
        dot(d_pre, qkv_weight, contract_cols).reshape(4, tokens, model_width),
        ep_index,
    )
    grad_bias = jnp.sum(d_pre.astype(single_float), 0).reshape(3, 1, -1, 1, HD)
    grad_qkv = dot(attn_in, d_pre, contract_rows).astype(bf16)
    grad_qkv = grad_qkv.reshape(RING_SIZE, row_block, 3 * head_width)
    own_x = hidden_in.astype(single_float)
    scale_one = rms_scale(own_x)
    normed_one = own_x * scale_one
    grad_gain_attn = jnp.sum(d_attn_in * normed_one, 0)
    d_normed_one = d_attn_in * attention_gain
    input_grad = d_mid + scale_one * (
        d_normed_one - normed_one * jnp.mean(d_normed_one * normed_one, -1, keepdims=True)
    )

    grad_bias_full = jnp.zeros((3, 2, model_width // (4 * HD), 2, HD), single_float)
    grad_bias_full = lax.dynamic_update_slice(grad_bias_full, grad_bias, (0, core, 0, side, 0))
    small_grads = jnp.concatenate(
        [
            grad_gain_attn[None],
            grad_bias_full.reshape(3, model_width),
            grad_gain_ffn[None],
            grad_rows,
            jnp.zeros((2, model_width), single_float),
        ]
    )
    small_grads = small_grads.reshape(16, RING_SIZE, sets, 4, n).transpose(3, 1, 0, 2, 4)
    small_grads = group_scatter(
        small_grads.reshape(4, RING_SIZE, 16, sets * n), ep_index, single_float
    )
    small_grads = jnp.pad(small_grads, ((0, 0), (0, 0), (0, model_width - sets * n)))
    grad_rows = jnp.concatenate(
        [grad_out_rows.reshape(RING_SIZE, -1, model_width), small_grads.astype(bf16)], 1
    )

    def finished(grad, m):
        if sets == 1:
            shared, routed = unpack_unit_grads(grad, m, units)
            return shared, routed.transpose(1, 0, 2)
        grad = grad[:, m * UNIT_SETS * units : (m + 1) * UNIT_SETS * units]
        grad = set_scatter(grad, 2).reshape(RING_SIZE, UNIT_SETS, units, -1)
        grad = grad.transpose(3, 1, 0, 2).astype(single_float)
        grad = grad.reshape(grad.shape[0], UNIT_SETS, -1)
        return grad[:, 0], grad[:, 1:]

    down_out = finished(after(down_grad, grad_rows), 0)
    gate_out = finished(after(late_grads, grad_rows), 0)
    up_out = finished(after(late_grads, grad_rows), 1)
    grad_qkv, grad_rows = ring_scatter(
        [grad_qkv, grad_rows],
        place,
        [(late_grads,), (down_out,), (gate_out,), (up_out,)],
    )
    grad_out_w = set_scatter(grad_rows[:quarter], 0)
    small_grads = set_scatter(grad_rows[quarter:, : sets * n], 1)
    grad_qkv = set_scatter(grad_qkv, 0).astype(bf16)
    grad_qkv = group_exchange(grad_qkv.reshape(4, n, 3 * head_width), ep_index)
    grad_qkv = grad_qkv.reshape(2, 2, n, 3, -1, HD).transpose(3, 2, 1, 4, 0, 5)
    grad_qkv = grad_qkv.reshape(3, n, model_width).astype(single_float)
    unit_outs = [gate_out, up_out, down_out]
    return (
        output,
        input_grad,
        small_grads[0],
        grad_qkv[0],
        grad_qkv[1],
        grad_qkv[2],
        small_grads[1],
        small_grads[2],
        small_grads[3],
        grad_out_w,
        small_grads[4],
        small_grads[6:14].T,
        small_grads[5],
        unit_outs[0][0],
        unit_outs[1][0],
        unit_outs[2][0],
        unit_outs[0][1],
        unit_outs[1][1],
        unit_outs[2][1],
    )


def solution(mesh):
    rows, vector, split = P(AXES, None), P(AXES), P("dp", "ep")
    routed = P("dp", "ep", None)
    return jax.shard_map(
        body,
        mesh=mesh,
        in_specs=(
            (rows, vector, P("dp", None), P("dp", None), P(), vector)
            + (rows,) * 3
            + (vector,) * 3
            + (rows, vector, rows, vector)
            + (split,) * 3
            + (routed,) * 3
            + (rows,)
        ),
        out_specs=(
            (rows, rows, vector)
            + (rows,) * 3
            + (vector,) * 3
            + (rows, vector, rows, vector)
            + (split,) * 3
            + (routed,) * 3
        ),
        check_vma=False,
    )
```

```python
import jax
import jax.numpy as jnp
from jax import lax
from jax.experimental import pallas as pl
from jax.experimental.pallas import tpu as pltpu
from jax.sharding import PartitionSpec as P

HD = 128
TOPK = 4
EXP_DEV = 2
RING_SIZE = 8
UNIT_SETS = 1 + EXP_DEV
CORNER_ROWS = 64
UNIT_PAD = 64
TILE_ROWS = 64
ROW_SPLIT = 16
VMEM_BYTES = 60 * 1024 * 1024
SLOT_VMEM_BYTES = 36 * 1024 * 1024
AXES = ("dp", "ep")

RING = (0, 2, 4, 6, 7, 5, 3, 1)
PLACE = tuple(RING.index(j) for j in range(RING_SIZE))

epsilon = 1e-06
rotary_base = 1000000.0
masked_score = -1e30
contract_rows = (((0,), (0,)), ((), ()))
contract_cols = (((1,), (1,)), ((), ()))
single_float = jnp.float32
bf16 = jnp.bfloat16


def dot(left, right, dims=(((1,), (0,)), ((), ()))):
    return lax.dot_general(left, right, dims, preferred_element_type=single_float)


def after(value, *events):
    return lax.optimization_barrier((value, events))[0] if events else value


def move(block, where):
    sets = lax.axis_size("dp") // RING_SIZE
    ranks = lax.axis_size("ep")
    pairs = []
    for j in range(RING_SIZE):
        for e in range(ranks):
            to = where(j, e)
            if to is None:
                continue
            for s in range(sets):
                pairs.append(((j * sets + s) * ranks + e, (to[0] * sets + s) * ranks + to[1]))
    return lax.ppermute(block, AXES, pairs)


def around(j, hops):
    return RING[(PLACE[j] + hops) % RING_SIZE]


def to_core(block):
    return move(block, lambda j, e: (j, e ^ 1))


def to_side(block):
    return move(block, lambda j, e: (j, e ^ 2))


def out_hop(block):
    return move(block, lambda j, e: (around(j, 1 if e % 2 else -1), e))


def back_hop(block):
    return move(block, lambda j, e: (around(j, -1 if e % 2 else 1), e))


def ring_up(block):
    return move(block, lambda j, e: (around(j, 1), e))


def ring_down(block):
    return move(block, lambda j, e: (around(j, -1), e))


def in_set(sets):
    return [[j * sets + s for s in range(sets)] for j in range(RING_SIZE)]


def set_gather(block, axis):
    sets = lax.axis_size("dp") // RING_SIZE
    if sets == 1:
        return block
    return lax.all_gather(block, "dp", axis_index_groups=in_set(sets), axis=axis, tiled=True)


def set_scatter(block, axis):
    sets = lax.axis_size("dp") // RING_SIZE
    if sets == 1:
        return block
    return lax.psum_scatter(
        block, "dp", scatter_dimension=axis, axis_index_groups=in_set(sets), tiled=True
    )


def group_gather(block, ep_index, before_last=()):
    near = to_core(block)
    far = after(to_side(block), *before_last)
    parts = [block, near, far, to_core(far)]
    whole = jnp.zeros((4,) + block.shape, block.dtype)
    for m, part in enumerate(parts):
        whole = lax.dynamic_update_index_in_dim(whole, part, ep_index ^ m, 0)
    return whole


def group_scatter(parts, ep_index, link=bf16, before_last=()):
    part = [lax.dynamic_index_in_dim(parts, ep_index ^ m, 0, False) for m in range(4)]
    got = to_core(jnp.stack([part[1], part[3]]).astype(link)).astype(single_float)
    near = part[0].astype(single_float) + got[0]
    far = part[2].astype(single_float) + got[1]
    far = after(far.astype(link), *before_last)
    return near + to_side(far).astype(single_float)


def group_exchange(blocks, ep_index):
    whole = jnp.zeros_like(blocks)
    for m in range(4):
        block = lax.dynamic_index_in_dim(blocks, ep_index ^ m, 0, False)
        if m:
            block = move(block, lambda j, e, m=m: (j, e ^ m))
        whole = lax.dynamic_update_index_in_dim(whole, block, ep_index ^ m, 0)
    return whole


def ring_position(place):
    return jnp.where(place % 2 == 1, RING_SIZE - 1 - place // 2, place // 2)


def place_at(position):
    position = position % RING_SIZE
    return jnp.where(position < 4, 2 * position, 2 * (RING_SIZE - 1 - position) + 1)


def ring_pieces(blocks, place, arrived):
    position = ring_position(place)
    up = down = blocks
    events = arrived(0, [(place, blocks)])
    for k in range(1, 4):
        up, down = after((up, down), *events)
        up, down = [ring_up(block) for block in up], [ring_down(block) for block in down]
        events = arrived(k, [(place_at(position - k), up), (place_at(position + k), down)])
    up, down = after((up, down), *events)
    last = []
    for first, second in zip(up, down):
        half = first.shape[0] // 32 * 16
        last.append(jnp.concatenate([ring_up(first[:half]), ring_down(second[half:])]))
    arrived(4, [(place_at(position + 4), last)])


def ring_scatter(every, place, events=()):
    position = ring_position(place)
    events = dict(enumerate(events))

    def part(hops):
        where = place_at(position + hops)
        return [wide(lax.dynamic_index_in_dim(parts, where, 0, False)) for parts in every]

    def hop(up, down, k):
        up, down = after(([low(x) for x in up], [low(x) for x in down]), *events.get(k, ()))
        return [wide(ring_up(x)) for x in up], [wide(ring_down(x)) for x in down]

    opposite = part(4)
    cuts = [x.shape[0] // 32 * 16 for x in opposite]
    up, down = hop(
        [x[:cut] for x, cut in zip(opposite, cuts)], [x[cut:] for x, cut in zip(opposite, cuts)], 0
    )
    up = [jnp.pad(x, ((0, y.shape[0] - x.shape[0]), (0, 0))) for x, y in zip(up, opposite)]
    down = [jnp.pad(x, ((y.shape[0] - x.shape[0], 0), (0, 0))) for x, y in zip(down, opposite)]
    for k in (3, 2, 1):
        up = [x + y for x, y in zip(part(k), up)]
        down = [x + y for x, y in zip(part(-k), down)]
        up, down = hop(up, down, 4 - k)
    return [x + y + z for x, y, z in zip(part(0), up, down)]


def ring_exchange(blocks):
    sets = lax.axis_size("dp") // RING_SIZE
    groups = [[j * sets + s for j in range(RING_SIZE)] for s in range(sets)]
    return lax.all_to_all(blocks, "dp", 0, 0, axis_index_groups=groups if sets > 1 else None)


def half_block(block):
    n, tail = CORNER_ROWS, (block.shape[0] - 4 * CORNER_ROWS) // 2
    return jnp.concatenate([block[:n], block[2 * n : 3 * n], block[4 * n : 4 * n + tail]])


def other_half(block):
    n, tail = CORNER_ROWS, (block.shape[0] - 4 * CORNER_ROWS) // 2
    return jnp.concatenate([block[n : 2 * n], block[3 * n : 4 * n], block[4 * n + tail :]])


def spread_half(half):
    n, tail = CORNER_ROWS, half.shape[0] - 2 * CORNER_ROWS
    rows = 4 * n + 2 * tail
    place = lambda first, last, at: jnp.pad(
        half[first:last], ((at, rows - at - (last - first)), (0, 0))
    )
    return place(0, n, 0) + place(n, 2 * n, 2 * n) + place(2 * n, 2 * n + tail, 4 * n)


def gather_start(block):
    head, tail = block[:CORNER_ROWS], block[CORNER_ROWS:]
    far = to_side(head)
    ring = jnp.concatenate([head, to_core(head), far, to_core(far), tail, to_core(tail)])
    return ring, (jnp.concatenate([head, far, tail]), to_side(tail))


def with_side(block, heads):
    return block, to_side(block[heads:])


def scatter_parts(parts):
    count = len(parts) // 2
    out = []
    for block, side in zip(parts[:count], parts[count:]):
        side = jnp.pad(to_side(side), ((block.shape[0] - side.shape[0], 0), (0, 0)))
        out.append(block.astype(single_float) + side.astype(single_float))
    return out


def scatter_end(total, own):
    n = CORNER_ROWS
    got = to_core(other_half(total).astype(bf16)).astype(single_float)
    total = half_block(total) + own + got
    far = to_side(total[n : 2 * n].astype(bf16)).astype(single_float)
    return jnp.concatenate([total[:n] + far, total[2 * n :]])


def low(value):
    return value.astype(bf16)


def wide(value):
    return value.astype(single_float)


def rms_scale(values):
    return lax.rsqrt(jnp.mean(values * values, -1, keepdims=True) + epsilon)


def rotary_table(positions):
    inverse = 1.0 / rotary_base ** (jnp.arange(0, HD, 2, dtype=single_float) / HD)
    angles = positions.astype(single_float)[:, None] * inverse[None, :]
    cosine, sine = jnp.cos(angles), jnp.sin(angles)
    return (
        jnp.concatenate([cosine, cosine], -1)[:, None, :],
        jnp.concatenate([-sine, sine], -1)[:, None, :],
    )


def rotate(values, table, direction):
    heads = values.reshape(values.shape[0], -1, HD)
    swapped = jnp.concatenate([heads[..., HD // 2 :], heads[..., : HD // 2]], -1)
    return heads * table[0] + swapped * (direction * table[1])


def kept_pairs(expert_ids, priority, capacity, ep_index, tokens):
    experts = capacity.shape[0]
    order = priority.reshape(-1, TOPK)
    own_experts = lax.dynamic_slice_in_dim(expert_ids, ep_index * tokens, tokens, 0)
    own_order = lax.dynamic_slice_in_dim(order, ep_index * tokens, tokens, 0)
    all_experts = expert_ids.reshape(1, -1)
    all_order = priority.reshape(1, -1)
    labels = jnp.arange(experts, dtype=jnp.int32)[None, :]
    kept = jnp.zeros((tokens, experts), bool)
    for k in range(TOPK):
        expert = own_experts[:, k : k + 1]
        ahead = (all_experts == expert) & (all_order < own_order[:, k : k + 1])
        slot = jnp.sum(ahead.astype(jnp.int32), 1, keepdims=True)
        kept = kept | ((labels == expert) & (slot < capacity[None, :]))
    return kept


def own_heads(features, core, side):
    lead = features.shape[:-1]
    split = features.reshape(lead + (2, -1, 2, HD))
    axis = len(lead)
    split = lax.dynamic_index_in_dim(split, core, axis, False)
    split = lax.dynamic_index_in_dim(split, side, axis + 1, False)
    return split.reshape(lead + (-1,))


def heads_to_rows(heads, dp_count, n, core, side, ep_index):
    rows = heads.shape[0]
    if 2 * n == HD:
        low, high = heads[..., :n], heads[..., n:]
        keep = jnp.where(core == 0, low, high).reshape(rows, -1)
        got = to_core(jnp.where(core == 0, high, low).reshape(rows, -1))
        return jnp.where(
            core == 0, jnp.concatenate([keep, got], 1), jnp.concatenate([got, keep], 1)
        )
    every = lax.all_gather(heads, "ep", axis=0)
    every = every.reshape((2, 2) + heads.shape).transpose(2, 1, 3, 0, 4)
    every = every.reshape(rows, dp_count, 4, n)
    return lax.dynamic_index_in_dim(every, ep_index, 2, False).reshape(rows, -1)


def rows_to_heads(features, dp_count, n, core, side, ep_index):
    rows = features.shape[0]
    if 2 * n == HD:
        half = features.shape[1] // 2
        low, high = features[:, :half], features[:, half:]
        keep = jnp.where(core == 0, low, high).reshape(rows, -1, n)
        got = to_core(jnp.where(core == 0, high, low)).reshape(rows, -1, n)
        return jnp.where(
            core == 0, jnp.concatenate([keep, got], -1), jnp.concatenate([got, keep], -1)
        )
    every = lax.all_gather(features, "ep", axis=0).reshape(4, rows, dp_count, n)
    every = every.transpose(1, 2, 0, 3).reshape(rows, -1)
    return own_heads(every, core, side).reshape(rows, -1, HD)


def cost(flops, bytes_accessed):
    return pl.CostEstimate(flops=int(flops), bytes_accessed=int(bytes_accessed), transcendentals=0)


def params(grid_rank, vmem=VMEM_BYTES):
    return pltpu.CompilerParams(
        dimension_semantics=("arbitrary",) * grid_rank, vmem_limit_bytes=vmem
    )


def padded(units):
    return -(-units // UNIT_PAD) * UNIT_PAD


def lay_out_units(blocks, offsets, step, last=None):
    count, _, rows = blocks[0].shape
    wide_step = padded(step)
    steps = len(blocks) * UNIT_SETS
    extra = [] if last is None else [last]

    def kernel(*refs):
        whole, now = refs[-1], pl.program_id(0)
        for owner in range(len(blocks)):

            @pl.when(now // UNIT_SETS == owner)
            def _(part=refs[owner]):
                for j in range(count):
                    whole[:step, j * rows : (j + 1) * rows] = part[j]
                if wide_step > step:
                    whole[step:, :] = jnp.zeros((wide_step - step, count * rows), bf16)

        if extra:

            @pl.when(now == steps)
            def _():
                whole[: last.shape[0], :] = refs[len(blocks)][...]

    def block(owner, first):
        turn = lambda i: first + jnp.clip(i - owner * UNIT_SETS, 0, UNIT_SETS - 1)
        return pl.BlockSpec((count, step, rows), lambda i: (0, turn(i), 0))

    total = steps * wide_step + sum(array.shape[0] for array in extra)
    return pl.pallas_call(
        kernel,
        grid=(steps + len(extra),),
        in_specs=[block(owner, first) for owner, first in enumerate(offsets)]
        + [pl.BlockSpec(array.shape, lambda i: (0, 0)) for array in extra],
        out_specs=pl.BlockSpec((wide_step, count * rows), lambda i: (i, 0)),
        out_shape=jax.ShapeDtypeStruct((total, count * rows), bf16),
        compiler_params=params(1),
        cost_estimate=cost(0, 4 * total * count * rows),
        name="lay_out_units",
    )(*blocks, *extra)


def routing(logits, kept, experts):
    lane = lax.broadcasted_iota(jnp.int32, logits.shape, 1)
    expert_lane = (lane >= 1) & (lane <= experts)
    top = jnp.max(jnp.where(expert_lane, logits, masked_score), 1, keepdims=True)
    weight = jnp.exp(jnp.where(expert_lane, logits - top, masked_score))
    router = weight / jnp.sum(weight, 1, keepdims=True)
    return lane, jax.nn.sigmoid(logits), router, kept.astype(single_float)


def high_low(value):
    high = value.astype(bf16)
    return high, (value - high.astype(single_float)).astype(bf16)


def unit_factor(lane, share, router, kept, spread_ref):
    high, rest = high_low(jnp.where(lane == 0, share, router * kept))
    return dot(high, spread_ref[...]) + dot(rest, spread_ref[...])


def by_tiles(rows, total, work):
    def chunk(i, carry):
        here = pl.ds(pl.multiple_of(i * TILE_ROWS, TILE_ROWS), TILE_ROWS)
        for first in range(0, total, HD):
            work(here, first)
        return carry

    lax.fori_loop(0, rows // TILE_ROWS, chunk, 0)


def slot_specs(slot, width, lanes=None):
    if lanes is None:
        return [pl.BlockSpec((part.shape[0], width), lambda *_: (0, 0)) for part in slot]
    return [pl.BlockSpec((part.shape[0], HD), lambda *_: (0, width // HD)) for part in slot]


def slot_shapes(slot, width):
    return [jax.ShapeDtypeStruct((part.shape[0], width), bf16) for part in slot]


def split_rows(refs, value):
    start = 0
    for ref in refs:
        ref[...] = value[start : start + ref.shape[0]]
        start += ref.shape[0]


def slot_call(kernel, slot, index, inputs, in_specs, kept, shapes, specs, scratch, flops, name):
    step = sum(part.shape[0] for part in slot)
    arrays = list(kept) if isinstance(kept[0], jax.Array) else []
    kept_shapes = [jax.ShapeDtypeStruct(k.shape, k.dtype) for k in kept]
    kept_specs = [pl.BlockSpec((step, k.shape[1]), lambda *_: (index, 0)) for k in kept]
    return pl.pallas_call(
        kernel,
        grid=(1,),
        in_specs=in_specs + [pl.BlockSpec(memory_space=pl.ANY)] * len(arrays),
        out_specs=kept_specs + specs,
        out_shape=kept_shapes + shapes,
        scratch_shapes=scratch,
        input_output_aliases={len(inputs) + i: i for i in range(len(arrays))},
        compiler_params=params(1, SLOT_VMEM_BYTES),
        cost_estimate=cost(flops, flops // 100),
        name=name,
    )(*inputs, *arrays)


def ffn_forward(slot, index, gate_up, down, spread, experts, kept):
    total, width = down.shape
    step = sum(part.shape[0] for part in slot)
    known = len(kept) if isinstance(kept[0], jax.Array) else 0

    def kernel(*refs):
        count = len(slot)
        parts, lanes, refs = refs[:count], refs[count : 2 * count], refs[2 * count :]
        (gate_up_w, down_w, spread_ref), refs = refs[:3], refs[3 + known :]
        (x_all, scaled), out = refs[:2], refs[2 : 2 + count]
        low_ref, act, rest, logit, both, factor = refs[2 + count :]
        x = jnp.concatenate([part[...] for part in parts], 0)
        x_all[...] = x
        both[...] = dot(x, gate_up_w[...], contract_cols)
        logits = both[:, 2 * total :]
        logit[...] = logits
        kept_lanes = jnp.concatenate([part[...] for part in lanes], 0)
        lane, share, router, kept_now = routing(logits, kept_lanes, experts)
        factor[...] = unit_factor(lane, share, router, kept_now, spread_ref)

        def work(here, first):
            tile = here, pl.ds(first, HD)
            gate, up = both[tile], both[here, pl.ds(total + first, HD)]
            logistic = jax.nn.sigmoid(gate)
            active = gate * logistic
            act[tile] = active.astype(bf16)
            rest[tile] = (up * (logistic + active * (1.0 - logistic))).astype(bf16)
            hidden = (active * up).astype(bf16)
            low_ref[tile] = hidden
            scaled[tile] = (factor[tile] * hidden.astype(single_float)).astype(bf16)

        by_tiles(step, total, work)
        split_rows(out, dot(scaled[...], down_w[...]).astype(bf16))

    whole = lambda *_: (0, 0)
    resident = pl.BlockSpec(memory_space=pltpu.VMEM)
    unit_block = pl.BlockSpec((step, total), whole)
    return slot_call(
        kernel,
        slot,
        index,
        [*slot, *slot, gate_up, down, spread],
        slot_specs(slot, width) + slot_specs(slot, width, HD) + [resident] * 3,
        kept,
        slot_shapes(slot, width)
        + [jax.ShapeDtypeStruct((step, total), bf16)] * 3
        + [jax.ShapeDtypeStruct((step, HD), single_float)],
        slot_specs(slot, width) + [unit_block] * 3 + [pl.BlockSpec((step, HD), whole)],
        [pltpu.VMEM((step, 2 * total + HD), single_float), pltpu.VMEM((step, total), single_float)],
        6 * step * width * total,
        "ffn_forward",
    )


def ffn_backward(slot, index, grads, gate_up, down, spread, saved, experts, kept):
    total, width = down.shape
    step = sum(part.shape[0] for part in slot)
    known = len(kept) if isinstance(kept[0], jax.Array) else 0

    def kernel(*refs):
        count = len(slot)
        parts, lanes, refs = refs[:count], refs[count : 2 * count], refs[2 * count :]
        (gate_up_w, down_w, spread_ref), refs = refs[:3], refs[3:]
        (low_ref, act, rest, logit), refs = refs[:4], refs[4 + known :]
        (grad_all, gate_all, up_all, row_all), out = refs[:4], refs[4 : 4 + count]
        d_hidden, factor, products, d_both = refs[4 + count :]
        grad = jnp.concatenate([part[...] for part in parts], 0)
        grad_all[...] = grad
        kept_lanes = jnp.concatenate([part[...] for part in lanes], 0)
        lane, share, router, kept_now = routing(logit[...], kept_lanes, experts)
        factor[...] = unit_factor(lane, share, router, kept_now, spread_ref)
        d_hidden[...] = dot(grad, down_w[...], contract_cols)

        def work(here, first):
            tile, other = (here, pl.ds(first, HD)), (here, pl.ds(total + first, HD))
            d_unit = d_hidden[tile]
            products[tile] = (d_unit * low_ref[tile].astype(single_float)).astype(bf16)
            d_unit = d_unit * factor[tile]
            d_gate = (d_unit * rest[tile].astype(single_float)).astype(bf16)
            d_up = (d_unit * act[tile].astype(single_float)).astype(bf16)
            gate_all[tile] = d_gate
            up_all[tile] = d_up
            d_both[tile] = d_gate
            d_both[other] = d_up

        by_tiles(step, total, work)
        sums = dot(products[...], spread_ref[...], contract_cols)
        d_router = sums * kept_now
        d_logits = router * (d_router - jnp.sum(router * d_router, 1, keepdims=True))
        d_rows = jnp.where(lane == 0, sums * share * (1.0 - share), d_logits)
        high = d_rows.astype(bf16).astype(single_float)
        remains = pltpu.roll(d_rows - high, ROW_SPLIT, 1)
        rows_both = jnp.where(lane < ROW_SPLIT, high, remains).astype(bf16)
        row_all[...] = rows_both
        d_both[:, 2 * total :] = rows_both
        split_rows(out, dot(d_both[...], gate_up_w[...]).astype(bf16))

    whole = lambda *_: (0, 0)
    resident = pl.BlockSpec(memory_space=pltpu.VMEM)
    unit_block = pl.BlockSpec((step, total), whole)
    return slot_call(
        kernel,
        grads,
        index,
        [*grads, *slot, gate_up, down, spread, *saved],
        slot_specs(grads, width)
        + slot_specs(slot, width, HD)
        + [resident] * 3
        + [unit_block] * 3
        + [pl.BlockSpec((step, HD), whole)],
        kept,
        slot_shapes(grads, width),
        slot_specs(grads, width),
        [
            pltpu.VMEM((step, total), single_float),
            pltpu.VMEM((step, total), single_float),
            pltpu.VMEM((step, total), bf16),
            pltpu.VMEM((step, 2 * total + HD), bf16),
        ],
        6 * step * width * total,
        "ffn_backward",
    )


def pack_unit_grads(pairs, units):
    width = pairs[0][0].shape[1]
    rows, wide_step = width // RING_SIZE, padded(units)
    steps = len(pairs) * UNIT_SETS

    def kernel(*refs):
        out = refs[-1]
        for p in range(len(pairs)):
            own, got = refs[2 * p : 2 * p + 2]

            @pl.when(pl.program_id(0) // UNIT_SETS == p)
            def _():
                for j in range(RING_SIZE):
                    part = (slice(0, units), slice(j * rows, (j + 1) * rows))
                    total = own[part].astype(single_float) + got[part].astype(single_float)
                    out[j] = total.astype(bf16)

    def block(p):
        return pl.BlockSpec(
            (wide_step, width), lambda i: (jnp.clip(i - p * UNIT_SETS, 0, UNIT_SETS - 1), 0)
        )

    return pl.pallas_call(
        kernel,
        grid=(steps,),
        in_specs=[block(p) for p in range(len(pairs)) for _ in range(2)],
        out_specs=pl.BlockSpec((RING_SIZE, units, rows), lambda i: (0, i, 0)),
        out_shape=jax.ShapeDtypeStruct((RING_SIZE, steps * units, rows), bf16),
        compiler_params=params(1),
        cost_estimate=cost(0, 6 * steps * units * width),
        name="pack_unit_grads",
    )(*[array for pair in pairs for array in pair])


def unpack_unit_grads(blocks, matrix, units):
    rows = blocks.shape[2]
    half = UNIT_SETS * units
    width = units * RING_SIZE

    def kernel(part, shared, routed, joined):
        for s in range(1 + EXP_DEV):
            for j in range(RING_SIZE):
                joined[j * units : (j + 1) * units, :] = part[j, s * units : (s + 1) * units, :]
            turned = joined[...].astype(single_float).T
            if s == 0:
                shared[...] = turned
            else:
                routed[s - 1] = turned

    return pl.pallas_call(
        kernel,
        grid=(1,),
        in_specs=[pl.BlockSpec((RING_SIZE, half, rows), lambda i: (0, matrix, 0))],
        out_specs=[
            pl.BlockSpec((rows, width), lambda i: (0, 0)),
            pl.BlockSpec((EXP_DEV, rows, width), lambda i: (0, 0, 0)),
        ],
        scratch_shapes=[pltpu.VMEM((width, rows), bf16)],
        out_shape=[
            jax.ShapeDtypeStruct((rows, width), single_float),
            jax.ShapeDtypeStruct((EXP_DEV, rows, width), single_float),
        ],
        compiler_params=params(1),
        cost_estimate=cost(0, 18 * rows * width),
        name="unpack_unit_grads",
    )(blocks)


def body(
    hidden_in,
    segment_ids,
    expert_ids,
    priority,
    capacity,
    norm_attn,
    w_query,
    w_key,
    w_value,
    bias_query,
    bias_key,
    bias_value,
    w_out,
    norm_ffn,
    w_router,
    w_shared_gate,
    shared_gate_proj,
    shared_up_proj,
    shared_down_proj,
    expert_gate_proj,
    expert_up_proj,
    expert_down_proj,
    out_grad,
):
    tokens, model_width = hidden_in.shape
    group_rows = 4 * tokens
    head_scale = HD ** (-0.5)
    dp_count = lax.axis_size("dp")
    sets = dp_count // RING_SIZE
    place = lax.axis_index("dp") // sets
    ep_index = lax.axis_index("ep")
    core, side = ep_index % 2, ep_index // 2
    n = norm_attn.shape[0]
    experts = capacity.shape[0]

    group_x = group_gather(hidden_in, ep_index).reshape(group_rows, model_width)
    segments = group_gather(segment_ids.reshape(1, tokens), ep_index).reshape(group_rows)
    group_index = jnp.arange(group_rows, dtype=jnp.int32)
    first = segments == segments[0]
    first_count = jnp.sum(first.astype(jnp.int32))
    positions = jnp.where(first, group_index, group_index - first_count)
    valid = (segments[:, None] == segments[None, :]) & (
        group_index[None, :] <= group_index[:, None]
    )
    table = rotary_table(positions)

    row_block = model_width // RING_SIZE
    units = expert_gate_proj.shape[2] // RING_SIZE
    half_units = (1 + EXP_DEV) * padded(units)

    def unit_slices(shared, routed):
        every = jnp.concatenate([shared[:, None, :], routed], 1)
        every = every.reshape(every.shape[0], 1 + EXP_DEV, RING_SIZE, -1)
        every = set_gather(every.transpose(2, 1, 3, 0), 3)
        return every.reshape(RING_SIZE, -1, row_block)

    gate_units = ring_exchange(unit_slices(shared_gate_proj, expert_gate_proj))

    def head_columns(weight):
        split = weight.reshape(n, 2, -1, 2, HD).transpose(3, 1, 0, 2, 4)
        return split.reshape(4, n, -1)

    small = jnp.concatenate(
        [
            jnp.stack([norm_attn, bias_query, bias_key, bias_value, norm_ffn, w_shared_gate]),
            w_router.T,
            jnp.zeros((2, n), bf16),
        ]
    )
    qkv = jnp.concatenate([head_columns(w) for w in (w_query, w_key, w_value)], -1)
    head_width = qkv.shape[-1] // 3
    quarter = row_block // 4
    small = jnp.pad(small, ((0, 0), (0, 3 * head_width - n)))
    qkv = jnp.concatenate([qkv, jnp.broadcast_to(small, (4,) + small.shape)], 1)
    qkv = group_exchange(qkv, ep_index)
    small = set_gather(qkv[:, n:, :n].transpose(1, 0, 2).reshape(16, 4 * n), 1)
    small = jnp.pad(small, ((0, 0), (0, 3 * head_width - row_block)))
    qkv = set_gather(qkv[:, :n].reshape(4 * n, -1), 0)
    gathered = [
        jnp.zeros((RING_SIZE, row_block, 3 * head_width), bf16),
        jnp.zeros((RING_SIZE, quarter, model_width), bf16),
        jnp.zeros((RING_SIZE, 16, row_block), bf16),
    ]
    later_units = []

    def arrived(k, pieces):
        for where, (dense, rows) in pieces:
            found = dense[:row_block], rows, dense[row_block:, :row_block]
            for i in range(3):
                gathered[i] = lax.dynamic_update_index_in_dim(gathered[i], found[i], where, 0)
        if k in (0, 4):
            return ()
        if k < 3:
            halves = ((shared_up_proj, expert_up_proj), (shared_down_proj, expert_down_proj))[k - 1]
            later_units.append(unit_slices(*after(halves, pieces[0][1][0])))
        return (gate_units,) if k == 1 else (later_units[k - 2],)

    ring_pieces([jnp.concatenate([qkv, small]), set_gather(w_out, 0)], place, arrived)
    qkv_weight = gathered[0].reshape(model_width, -1)
    out_weight = gathered[1].reshape(-1, model_width)
    small = gathered[2].transpose(1, 0, 2).reshape(16, model_width)
    attention_gain = small[0].astype(single_float)
    feedforward_gain = small[4].astype(single_float)
    gate_rows = small[5:14]
    gate_rows = jnp.pad(gate_rows, ((0, ROW_SPLIT - gate_rows.shape[0]), (0, 0)))
    gate_rows = jnp.pad(
        jnp.concatenate([gate_rows, gate_rows]), ((0, HD - 2 * ROW_SPLIT), (0, 0))
    )
    head_bias = own_heads(small[1:4], core, side).astype(single_float)
    late_units = ring_exchange(after(jnp.concatenate(later_units, 1), gathered[0]))

    gate_other = to_core(after(gate_units, gathered[0]))

    kept_own = kept_pairs(expert_ids, priority, capacity, ep_index, tokens)
    kept_own = jnp.pad(kept_own.astype(bf16), ((0, 0), (1, HD - 1 - experts)))

    x_float = group_x.astype(single_float)
    attn_in = (x_float * rms_scale(x_float) * attention_gain).astype(bf16)
    pre = dot(attn_in, qkv_weight)
    query = rotate(pre[:, :head_width] + head_bias[0], table, 1.0).astype(bf16)
    key = rotate(pre[:, head_width : 2 * head_width] + head_bias[1], table, 1.0).astype(bf16)
    value = (pre[:, 2 * head_width :] + head_bias[2]).astype(bf16).reshape(group_rows, -1, HD)

    def score_table():
        raw = jnp.einsum("thd,khd->htk", query, key, preferred_element_type=single_float)
        return jnp.where(valid[None], raw * head_scale, masked_score)

    scores = score_table()
    top_score = jnp.max(scores, -1, keepdims=True)
    exps = jnp.exp(scores - top_score)
    totals = jnp.sum(exps, -1, keepdims=True)
    log_total = top_score + jnp.log(totals)
    probs_low = (exps / totals).astype(bf16)
    attn = jnp.einsum("htk,khd->thd", probs_low, value, preferred_element_type=single_float)
    attn_rows = heads_to_rows(attn.astype(bf16), dp_count, n, core, side, ep_index)
    mid = hidden_in.astype(single_float) + group_scatter(
        dot(attn_rows, out_weight).reshape(4, tokens, model_width),
        ep_index,
        before_last=(gate_other,),
    )
    scale_two = rms_scale(mid)
    normed_two = mid * scale_two
    ffn_in = (normed_two * feedforward_gain).astype(bf16)

    class Walk:
        def __init__(self, block):
            self.block, self.own = gather_start(block)
            self.sides = []

        def hop(self, k, *events):
            events = (*events, *self.sides[:-1])
            if k:
                self.block = out_hop(after(self.block, *events))
                slot = with_side(self.block, 4 * CORNER_ROWS)
                self.sides = self.sides[-1:] + [slot[1]]
                return slot
            self.block = out_hop(after(half_block(self.block), *events))
            far = with_side(self.block, 2 * CORNER_ROWS)
            return self.own[0], far[0], self.own[1], far[1]

    held = [EXP_DEV * (ep_index ^ flip) + i for flip in (0, 1) for i in range(EXP_DEV)]
    lanes = [0] + [1 + e for e in held[:EXP_DEV]] + [0] + [1 + e for e in held[EXP_DEV:]]
    lanes = jnp.repeat(jnp.stack([jnp.asarray(lane, jnp.int32) for lane in lanes]), padded(units))
    spread = (jnp.arange(HD, dtype=jnp.int32)[:, None] == lanes[None, :]).astype(bf16)
    total = 2 * half_units
    all_rows = 4 * group_rows
    shape = lambda lanes: jax.ShapeDtypeStruct((all_rows, lanes), bf16)
    kept = [shape(model_width), shape(total)]
    ring_slots, grad_slots, results = [None] * 4, [None] * 4, [None] * 4

    def forward(k, kept, *events):
        found = ffn_forward(
            after(ring_slots[k], *events), k, gate_up, down, spread, experts, kept
        )
        count = len(ring_slots[k])
        results[k] = found[2 : 2 + count], found[2 + count :]
        return found[:2]

    def backward(k, kept, *events):
        found = ffn_backward(
            ring_slots[k],
            k,
            after(grad_slots[k], *events),
            gate_up,
            down,
            spread,
            results[k][1],
            experts,
            kept,
        )
        return found[:4], scatter_parts(found[4:])

    late_other = to_core(late_units)
    walk = Walk(jnp.concatenate([ffn_in, kept_own], 1))
    ring_slots[1] = walk.hop(1)
    gate_up = lay_out_units(
        [gate_units, gate_other, late_units, late_other], [0] * 4, units, gate_rows
    )
    ring_slots[2] = walk.hop(2, gate_up)
    down = lay_out_units(
        after([late_units, late_other], ring_slots[1][0]), [UNIT_SETS, UNIT_SETS], units
    )
    ring_slots[3] = walk.hop(3, down)
    kept = forward(1, kept, ring_slots[2][0])
    grad_walk = Walk(after(out_grad, ring_slots[2][0]))
    ring_slots[0] = walk.hop(0, *kept)
    kept = forward(2, kept, ring_slots[3][0])
    grad_slots[1] = grad_walk.hop(1, walk.block, ring_slots[3][1], *kept)
    kept = forward(3, kept, walk.block)
    grad_slots[2] = grad_walk.hop(2, *ring_slots[0][2:], *kept)
    kept = forward(0, kept, grad_slots[1][0])
    grad_slots[3] = grad_walk.hop(3, *kept)
    ring_in, scaled_hidden = kept
    out_own, out_far = scatter_parts(after(results[0][0], grad_slots[2][0]))
    (out_slot,) = scatter_parts(after(results[3][0], grad_slots[2][0]))
    grad_slots[0] = grad_walk.hop(0, out_far, out_slot)

    def back(block, *events):
        return wide(back_hop(after(low(block), *events)))

    out = back(out_far, grad_slots[3][0])
    kept = [shape(model_width), shape(total), shape(total), shape(HD)]
    kept, (d_slot_3,) = backward(3, kept, grad_slots[3][0])
    (out_slot_2,) = scatter_parts(after(results[2][0], out))
    out = back(spread_half(out) + out_slot, kept[3])
    kept, (d_own, d_far) = backward(0, kept, kept[3])
    (out_slot_1,) = scatter_parts(after(results[1][0], kept[3]))
    out = back(out + out_slot_2, kept[3])
    kept, (d_slot_2,) = backward(2, kept, kept[3])
    d_ring = back(d_far, kept[3])
    out = back(out + out_slot_1, kept[3])
    kept, (d_slot_1,) = backward(1, kept, kept[3])
    ring_grad, d_gate, d_up, d_rows = kept
    down_grad = dot(
        *after((scaled_hidden, ring_grad), d_ring, d_rows), contract_rows
    ).astype(bf16)
    d_ring = back(spread_half(d_ring) + d_slot_3, d_rows)

    def pair(grad):
        return grad, to_core(grad[half_units:])

    down_pair = pair(down_grad)
    gate_grad = dot(*after((d_gate, ring_in), d_ring, down_grad), contract_rows).astype(bf16)
    d_ring = back(d_ring + d_slot_2, down_grad)
    down_grad = pack_unit_grads([after(down_pair, gate_grad)], units)
    up_grad = dot(*after((d_up, ring_in), d_ring, down_grad), contract_rows).astype(bf16)
    d_ring = back(d_ring + d_slot_1, down_grad, out)
    down_grad = ring_exchange(down_grad)
    d_ffn_in = scatter_end(after(d_ring, up_grad), d_own)
    grad_rows = dot(d_rows, ring_in, contract_rows)
    grad_rows = grad_rows[: 1 + experts] + grad_rows[ROW_SPLIT : ROW_SPLIT + 1 + experts]

    d_normed_two = d_ffn_in * feedforward_gain
    d_mid = out_grad.astype(single_float) + scale_two * (
        d_normed_two - normed_two * jnp.mean(d_normed_two * normed_two, -1, keepdims=True)
    )
    grad_gain_ffn = jnp.sum(d_ffn_in * normed_two, 0)
    late_grads = [pair(after(grad, d_ffn_in)) for grad in (gate_grad, up_grad)]
    late_grads = pack_unit_grads(late_grads, units)
    d_branch = group_gather(d_mid.astype(bf16), ep_index, (late_grads, down_grad))
    d_branch = d_branch.reshape(group_rows, model_width)
    late_grads = ring_exchange(after(late_grads, down_grad))
    d_attn = dot(d_branch, out_weight, contract_cols).astype(bf16)
    d_attn = rows_to_heads(d_attn, dp_count, n, core, side, ep_index)
    output = (mid + scatter_end(after(out, d_attn), out_own)).astype(bf16)
    grad_out_rows = dot(attn_rows, d_branch, contract_rows).astype(bf16)
    probs = jnp.exp(score_table() - log_total)
    d_probs = jnp.einsum("thd,khd->htk", d_attn, value, preferred_element_type=single_float)
    d_value = jnp.einsum("htk,thd->khd", probs_low, d_attn, preferred_element_type=single_float)
    d_scores = (probs * (d_probs - jnp.sum(probs * d_probs, -1, keepdims=True))).astype(bf16)
    d_query = head_scale * jnp.einsum(
        "htk,khd->thd", d_scores, key, preferred_element_type=single_float
    )
    d_key = head_scale * jnp.einsum(
        "htk,thd->khd", d_scores, query, preferred_element_type=single_float
    )
    d_pre = [rotate(d_query, table, -1.0), rotate(d_key, table, -1.0), d_value]
    d_pre = jnp.concatenate([d.reshape(group_rows, -1) for d in d_pre], 1).astype(bf16)
    d_attn_in = group_scatter(
        dot(d_pre, qkv_weight, contract_cols).reshape(4, tokens, model_width),
        ep_index,
    )
    grad_bias = jnp.sum(d_pre.astype(single_float), 0).reshape(3, 1, -1, 1, HD)
    grad_qkv = dot(attn_in, d_pre, contract_rows).astype(bf16)
    grad_qkv = grad_qkv.reshape(RING_SIZE, row_block, 3 * head_width)
    own_x = hidden_in.astype(single_float)
    scale_one = rms_scale(own_x)
    normed_one = own_x * scale_one
    grad_gain_attn = jnp.sum(d_attn_in * normed_one, 0)
    d_normed_one = d_attn_in * attention_gain
    input_grad = d_mid + scale_one * (
        d_normed_one - normed_one * jnp.mean(d_normed_one * normed_one, -1, keepdims=True)
    )

    grad_bias_full = jnp.zeros((3, 2, model_width // (4 * HD), 2, HD), single_float)
    grad_bias_full = lax.dynamic_update_slice(grad_bias_full, grad_bias, (0, core, 0, side, 0))
    small_grads = jnp.concatenate(
        [
            grad_gain_attn[None],
            grad_bias_full.reshape(3, model_width),
            grad_gain_ffn[None],
            grad_rows,
            jnp.zeros((2, model_width), single_float),
        ]
    )
    small_grads = small_grads.reshape(16, RING_SIZE, sets, 4, n).transpose(3, 1, 0, 2, 4)
    small_grads = group_scatter(
        small_grads.reshape(4, RING_SIZE, 16, sets * n), ep_index, single_float
    )
    small_grads = jnp.pad(small_grads, ((0, 0), (0, 0), (0, model_width - sets * n)))
    grad_rows = jnp.concatenate(
        [grad_out_rows.reshape(RING_SIZE, -1, model_width), small_grads.astype(bf16)], 1
    )

    def finished(grad, m):
        if sets == 1:
            shared, routed = unpack_unit_grads(grad, m, units)
            return shared, routed.transpose(1, 0, 2)
        grad = grad[:, m * UNIT_SETS * units : (m + 1) * UNIT_SETS * units]
        grad = set_scatter(grad, 2).reshape(RING_SIZE, UNIT_SETS, units, -1)
        grad = grad.transpose(3, 1, 0, 2).astype(single_float)
        grad = grad.reshape(grad.shape[0], UNIT_SETS, -1)
        return grad[:, 0], grad[:, 1:]

    down_out = finished(after(down_grad, grad_rows), 0)
    gate_out = finished(after(late_grads, grad_rows), 0)
    up_out = finished(after(late_grads, grad_rows), 1)
    grad_qkv, grad_rows = ring_scatter(
        [grad_qkv, grad_rows],
        place,
        [(late_grads,), (down_out,), (gate_out,), (up_out,)],
    )
    grad_out_w = set_scatter(grad_rows[:quarter], 0)
    small_grads = set_scatter(grad_rows[quarter:, : sets * n], 1)
    grad_qkv = set_scatter(grad_qkv, 0).astype(bf16)
    grad_qkv = group_exchange(grad_qkv.reshape(4, n, 3 * head_width), ep_index)
    grad_qkv = grad_qkv.reshape(2, 2, n, 3, -1, HD).transpose(3, 2, 1, 4, 0, 5)
    grad_qkv = grad_qkv.reshape(3, n, model_width).astype(single_float)
    unit_outs = [gate_out, up_out, down_out]
    return (
        output,
        input_grad,
        small_grads[0],
        grad_qkv[0],
        grad_qkv[1],
        grad_qkv[2],
        small_grads[1],
        small_grads[2],
        small_grads[3],
        grad_out_w,
        small_grads[4],
        small_grads[6:14].T,
        small_grads[5],
        unit_outs[0][0],
        unit_outs[1][0],
        unit_outs[2][0],
        unit_outs[0][1],
        unit_outs[1][1],
        unit_outs[2][1],
    )


def solution(mesh):
    rows, vector, split = P(AXES, None), P(AXES), P("dp", "ep")
    routed = P("dp", "ep", None)
    return jax.shard_map(
        body,
        mesh=mesh,
        in_specs=(
            (rows, vector, P("dp", None), P("dp", None), P(), vector)
            + (rows,) * 3
            + (vector,) * 3
            + (rows, vector, rows, vector)
            + (split,) * 3
            + (routed,) * 3
            + (rows,)
        ),
        out_specs=(
            (rows, rows, vector)
            + (rows,) * 3
            + (vector,) * 3
            + (rows, vector, rows, vector)
            + (split,) * 3
            + (routed,) * 3
        ),
        check_vma=False,
    )
```
